32 devices in a mesh: row: 4 (over y, x), col: 8 (over z, core).
Axes of the slice: x: 2, y: 2, z: 4, core: 2. Of those that a mesh axis runs over, the one named last changes fastest.
Arguments:
- slip: float32 [65536, 256], P(('row', 'col')), may hold values from -2 to 2
- state: float32 [65536, 256], P(('row', 'col')), may hold values from 0.4 to 0.9
- tau_load: float32 [65536], P(('row', 'col')), may hold values from 1 to 2
- normal_stress: float32 [65536], P(('row', 'col')), may hold values from 6 to 8
- direct_effect: float32 [65536], P(('row', 'col')), may hold values from 0.8 to 1.6
- evolution_effect: float32 [65536], P(('row', 'col')), may hold values from 0.5 to 1
- slip_distance: float32 [65536], P(('row', 'col')), may hold values from 0.5 to 2
- self_stiffness: float32 [65536], P(('row', 'col')), may hold values from 0.5 to 2
- near_blocks: bfloat16 [3, 65536, 256], P(None, ('row', 'col')), may hold values from -0.21875 to 0.21875
- basis_in: bfloat16 [32, 65536], P(None, ('row', 'col')), may hold values from -0.375 to 0.375
- basis_out: bfloat16 [32, 65536], P(None, ('row', 'col')), may hold values from -1 to 1
- coupling: bfloat16 [8192, 4, 2048], P('row', None, 'col'), may hold values from -0.09375 to 0.09375
- block_rank: int32 [256, 4, 64], P('row', None, 'col'), may hold values from 8 to 32
- adj_bricks: int32 [8, 65536], P(None, ('row', 'col')), may hold values from 0 to 1023
- adj_count: int32 [65536], P(('row', 'col')), may hold values from 1 to 8
- adj_weight: float32 [8, 65536], P(None, ('row', 'col')), may hold values from 0.05 to 1
- pressure_now: bfloat16 [1024, 256], P('col'), may hold values from 0.099609375 to 1
- pressure_rate: bfloat16 [1024, 256], P('col'), may hold values from 0.5 to 5
Outputs:
- slip_out: float32 [65536, 256], P(('row', 'col'))
- state_out: float32 [65536, 256], P(('row', 'col'))
The draws below stay inside these ranges and needn't reach their ends.
Inputs may be any that keep to these rules, and one draw needn't show every extreme that they name: Only the first adj_count entries of a patch's brick list are read. `adj_bricks`: brick numbers index the whole reservoir. `block_rank`: ranks of pairs with |i - j| <= 1 are not read.
All inputs are finite; a program needn't handle non-finite values.
Results may differ from the reference program's by a relative error of at most 0.0007.
Values may be sent and summed in bfloat16 or wider, within the bound.
No kernel may reach another device: no remote copies, remote signals or barrier semaphores. Data moves between devices by JAX's collectives and lax.ppermute only.
A program may use at most 192 MiB of HBM per device.

```python
import math
import jax
import jax.numpy as jnp
from jax import lax

BS = 256
R = 32
ADJ = 8
BPD = 8
ENS = 256
NBLK = 256
PATCHES = 65536
BRICKS = 1024
N_ROW = 4
N_COL = 8


def set_ends(array, stream_key, low, top_value):
    longest = array.shape.index(max(array.shape))
    spots = []
    for shift in (0, 1):
        where = [jax.random.randint(jax.random.fold_in(stream_key, axis), (), 0, length) for axis, length in enumerate(array.shape)]
        where[longest] = (where[longest] + shift) % array.shape[longest]
        spots.append(tuple(where))
    return array.at[spots[0]].set(low).at[spots[1]].set(top_value)


def strengthened(drawn, own_key, source, target, parts, factor):
    def block_of(dim):
        return (jnp.arange(drawn.shape[dim]) // (drawn.shape[dim] // parts)).reshape((-1,) + (1,) * (drawn.ndim - 1 - dim))

    first = jax.random.permutation(own_key, parts)[block_of(target)]
    second = (block_of(target) + parts // 2) % parts
    return jnp.where((block_of(source) == first) | (block_of(source) == second), factor * drawn, drawn)


def block_levels(key, shape, pieces, low, largest):
    loudness, own = 1.0, jax.random.fold_in(key, 6)
    for dim, blocks in pieces:
        draws = jnp.exp(jax.random.uniform(jax.random.fold_in(own, dim), (blocks,), jnp.float32, low / len(pieces), largest / len(pieces)))
        loudness = loudness * jnp.repeat(draws, shape[dim] // blocks).reshape([-1 if axis == dim else 1 for axis in range(len(shape))])
    return loudness


def gaussian(own_key, extent, spread, bound, cuts=(), kind=jnp.bfloat16):
    factor_of = block_levels(own_key, extent, cuts, -0.22, 0.18) if cuts else 1.0
    values = jax.random.normal(own_key, extent, jnp.float32) * spread * factor_of
    return jnp.minimum(jnp.maximum(values, -bound), bound).astype(kind)


def noise_with(rng, shape, width, most, pieces, heavy, kind=jnp.bfloat16):
    result = width * jax.random.normal(rng, shape, jnp.float32)
    if pieces:
        result = result * block_levels(rng, shape, pieces, -0.22, 0.18)
    return jnp.clip(strengthened(result, jax.random.fold_in(rng, 3), *heavy), -most, most).astype(kind)


def setup_inputs(seed: int = 0) -> dict:
    seeds = jax.random.split(jax.random.key(seed), 19)
    return {
        "slip": gaussian(seeds[0], (PATCHES, ENS), 0.5, 2.0, ((0, 32),), jnp.float32),
        "state": jnp.clip(0.4 + 0.49999997 * jax.random.uniform(seeds[1], (PATCHES, ENS), jnp.float32) ** block_levels(seeds[1], (PATCHES, ENS), ((0, 32),), -0.2, 0.2), 0.4, 0.9),
        "tau_load": jnp.clip(1.0 + 1.0 * jax.random.uniform(seeds[2], (PATCHES,), jnp.float32) ** block_levels(seeds[2], (PATCHES,), ((0, 32),), -0.2, 0.2), 1.0, 2.0),
        "normal_stress": jnp.clip(6.0 + 2.0 * jax.random.uniform(seeds[3], (PATCHES,), jnp.float32) ** block_levels(seeds[3], (PATCHES,), ((0, 32),), -0.2, 0.2), 6.0, 8.0),
        "direct_effect": jnp.clip(jnp.exp(math.log(1.6) - 0.6931472 * jax.random.uniform(seeds[4], (PATCHES,), jnp.float32) ** block_levels(seeds[4], (PATCHES,), ((0, 32),), -0.2, 0.2)), 0.8, 1.6),
        "evolution_effect": jnp.clip(jnp.exp(math.log(1.0) - 0.6931472 * jax.random.uniform(seeds[5], (PATCHES,), jnp.float32) ** block_levels(seeds[5], (PATCHES,), ((0, 32),), -0.2, 0.2)), 0.5, 1.0),
        "slip_distance": jnp.clip(jnp.exp(math.log(2.0) - 1.3862944 * jax.random.uniform(seeds[6], (PATCHES,), jnp.float32) ** block_levels(seeds[6], (PATCHES,), ((0, 32),), -0.2, 0.2)), 0.5, 2.0),
        "self_stiffness": jnp.clip(jnp.exp(math.log(2.0) - 1.3862944 * jax.random.uniform(seeds[7], (PATCHES,), jnp.float32) ** block_levels(seeds[7], (PATCHES,), ((0, 32),), -0.2, 0.2)), 0.5, 2.0),
        "near_blocks": gaussian(seeds[8], (3, PATCHES, BS), (3 * BS) ** -0.5, 0.21875, ((1, 32),)),
        "basis_in": gaussian(seeds[9], (R, PATCHES), BS ** -0.5, 0.375, ((1, 32),)),
        "basis_out": gaussian(seeds[10], (R, PATCHES), R ** -0.5, 1.0, ((1, 32),)),
        "coupling": noise_with(seeds[11], (NBLK * R, N_ROW, N_COL * BPD * R), (NBLK * R) ** -0.5, 0.09375, ((0, 4), (2, 8)), (2, 0, 8, 2.0)),
        "block_rank": set_ends(jax.random.randint(seeds[12], (NBLK, N_ROW, N_COL * BPD), R // 4, R + 1), jax.random.fold_in(seeds[12], 1), R // 4, R).astype(jnp.int32),
        "adj_bricks": set_ends(jax.random.randint(seeds[13], (ADJ, PATCHES), 0, BRICKS), jax.random.fold_in(seeds[13], 1), 0, BRICKS - 1).astype(jnp.int32),
        "adj_count": set_ends(jax.random.randint(seeds[14], (PATCHES,), 1, ADJ + 1), jax.random.fold_in(seeds[14], 1), 1, ADJ).astype(jnp.int32),
        "adj_weight": jnp.clip(jnp.exp(math.log(1.0) - 2.9957323 * jax.random.uniform(seeds[15], (ADJ, PATCHES), jnp.float32) ** block_levels(seeds[15], (ADJ, PATCHES), ((1, 32),), -0.2, 0.2)), 0.05, 1.0),
        "pressure_now": jnp.clip(jnp.exp(math.log(1.0) - 2.306499 * jax.random.uniform(seeds[16], (BRICKS, ENS), jnp.float32) ** block_levels(seeds[16], (BRICKS, ENS), ((0, 8),), -0.2, 0.2)), 0.099609375, 1.0).astype(jnp.bfloat16),
        "pressure_rate": jnp.clip(jnp.exp(math.log(5.0) - 2.3025851 * jax.random.uniform(seeds[17], (BRICKS, ENS), jnp.float32) ** block_levels(seeds[17], (BRICKS, ENS), ((0, 8),), -0.2, 0.2)), 0.5, 5.0).astype(jnp.bfloat16),
    }


STEP_SIZE = 0.5
REF_FRICTION = 0.6


def fault_pressure(field, adj_bricks, adj_count, adj_weight):
    weight_sum = jnp.zeros(adj_count.shape, jnp.float32)
    total = jnp.zeros((adj_count.shape[0], field.shape[1]), jnp.float32)
    for slot_index in range(adj_bricks.shape[0]):
        live = (adj_count > slot_index).astype(jnp.float32)
        weighting = adj_weight[slot_index] * live
        weight_sum = weight_sum + weighting
        total = total + weighting[:, None] * field[adj_bricks[slot_index]].astype(jnp.float32)
    return total / weight_sum[:, None]


def far_mask(row_blocks, col_blocks, ranks):
    apart = jnp.abs(row_blocks[:, None] - col_blocks[None, :]) > 1
    levels = jnp.arange(R, dtype=jnp.int32)
    out_keep = levels[None, :, None, None] < ranks[:, None, :, None]
    in_keep = levels[None, None, None, :] < ranks[:, None, :, None]
    keep = apart[:, None, :, None] & out_keep & in_keep
    return keep.reshape(row_blocks.shape[0] * R, col_blocks.shape[0] * R).astype(jnp.bfloat16)


def rates(slip_now, state_now, outer, pressure, tau_load, normal_stress, direct_effect, evolution_effect, slip_distance, self_stiffness):
    tau = tau_load[:, None] - self_stiffness[:, None] * slip_now - outer
    sigma = normal_stress[:, None] - pressure
    speed = jnp.exp((tau / sigma - state_now) / direct_effect[:, None])
    drift = (evolution_effect / slip_distance)[:, None] * (jnp.exp((REF_FRICTION - state_now) / evolution_effect[:, None]) - speed)
    return speed, drift


def reference(slip, state, tau_load, normal_stress, direct_effect, evolution_effect, slip_distance, self_stiffness, near_blocks, basis_in, basis_out, coupling, block_rank, adj_bricks, adj_count, adj_weight, pressure_now, pressure_rate):
    base_press = fault_pressure(pressure_now, adj_bricks, adj_count, adj_weight)
    rate_press = fault_pressure(pressure_rate, adj_bricks, adj_count, adj_weight)
    matrix = coupling.reshape(NBLK * R, NBLK * R)
    ranks = block_rank.reshape(NBLK, NBLK)
    all_blocks = jnp.arange(NBLK, dtype=jnp.int32)
    group = 16
    near_whole = near_blocks.reshape(3, NBLK, BS, BS)

    def stress(slip_now):
        rounded = slip_now.astype(jnp.bfloat16)
        coeff = jnp.einsum("rnb,nbe->nre", basis_in.reshape(R, NBLK, BS).astype(jnp.float32), rounded.reshape(NBLK, BS, ENS).astype(jnp.float32))
        coeff = coeff.astype(jnp.bfloat16).reshape(NBLK * R, ENS)

        def row_group(group_index):
            first = group_index * group
            rows = lax.dynamic_slice_in_dim(matrix, first * R, group * R, 0)
            rank_rows = lax.dynamic_slice_in_dim(ranks, first, group, 0)
            row_blocks = first + jnp.arange(group, dtype=jnp.int32)
            masked = rows * far_mask(row_blocks, all_blocks, rank_rows)
            return jnp.dot(masked, coeff, preferred_element_type=jnp.float32)

        summed = lax.map(row_group, jnp.arange(NBLK // group, dtype=jnp.int32))
        far_coeff = summed.reshape(NBLK, R, ENS).astype(jnp.bfloat16)
        far = jnp.einsum("rnb,nre->nbe", basis_out.reshape(R, NBLK, BS).astype(jnp.float32), far_coeff.astype(jnp.float32)).reshape(PATCHES, ENS)
        blocks = rounded.reshape(NBLK, BS, ENS).astype(jnp.float32)
        zero_block = jnp.zeros((1, BS, ENS), jnp.float32)
        padded = jnp.concatenate([zero_block, blocks, zero_block], 0)
        terms = []
        for neighbour in range(3):
            terms.append(jnp.einsum("npm,nme->npe", near_whole[neighbour].astype(jnp.float32), padded[neighbour:neighbour + NBLK]))
        near = (terms[0] + terms[1] + terms[2]).reshape(PATCHES, ENS)
        return near + far

    params = (tau_load, normal_stress, direct_effect, evolution_effect, slip_distance, self_stiffness)
    speed0, drift0 = rates(slip, state, stress(slip), base_press, *params)
    slip_mid = slip + STEP_SIZE * speed0
    state_mid = state + STEP_SIZE * drift0
    speed1, drift1 = rates(slip_mid, state_mid, stress(slip_mid), base_press + STEP_SIZE * rate_press, *params)
    slip_out = slip + (0.5 * STEP_SIZE) * (speed0 + speed1)
    state_out = state + (0.5 * STEP_SIZE) * (drift0 + drift1)
    return slip_out, state_out
```

```python
import functools

import jax
import jax.numpy as jnp
from jax import lax
from jax.experimental import pallas as pl
from jax.experimental.pallas import tpu as pltpu
from jax.sharding import PartitionSpec as P

BS = 256
R = 32

STEP_SIZE = 0.5
REF_FRICTION = 0.6
LIMIT = 48 * 1024 * 1024
F32 = jnp.float32
BF16 = jnp.bfloat16


def dot(a, b):
    return jnp.dot(a, b, preferred_element_type=F32)


def dot_t(a, b):
    return lax.dot_general(a, b, (((0,), (0,)), ((), ())), preferred_element_type=F32)


def params():
    return pltpu.CompilerParams(vmem_limit_bytes=LIMIT)


def project_kernel(slip_ref, basis_ref, coeff_ref, rounded_ref):
    rounded = slip_ref[...].astype(BF16)
    rounded_ref[...] = rounded
    coeff_ref[...] = dot(basis_ref[...], rounded).astype(BF16)


def project(slip, basis_in):
    patches, ens = slip.shape
    count = patches // BS
    return pl.pallas_call(
        project_kernel,
        grid=(count,),
        in_specs=[
            pl.BlockSpec((BS, ens), lambda n: (n, 0)),
            pl.BlockSpec((R, BS), lambda n: (0, n)),
        ],
        out_specs=[
            pl.BlockSpec((R, ens), lambda n: (n, 0)),
            pl.BlockSpec((BS, ens), lambda n: (n, 0)),
        ],
        out_shape=[
            jax.ShapeDtypeStruct((count * R, ens), BF16),
            jax.ShapeDtypeStruct((patches, ens), BF16),
        ],
        compiler_params=params(),
    )(slip, basis_in)


def couple_kernel(sources, where_ref, matrix_ref, *refs):
    coeffs, out_ref = refs[:sources], refs[sources]
    total = None
    for d in range(sources):
        term = dot(matrix_ref[where_ref[1 + d]], coeffs[d][...])
        total = term if total is None else total + term
    out_ref[...] = total.astype(out_ref.dtype)


def couple(where, matrix, coeffs, heights, kind):
    sources, rows, width = matrix.shape
    share, ens = coeffs[0].shape
    grid_spec = pltpu.PrefetchScalarGridSpec(
        num_scalar_prefetch=1,
        grid=(heights,),
        in_specs=[
            pl.BlockSpec(
                (sources, share, width),
                lambda d, w: (0, 2 * lax.rem(lax.div(w[0], 2) + d, heights) + lax.rem(w[0], 2), 0),
            )
        ]
        + [pl.BlockSpec((share, ens), lambda d, w: (0, 0))] * sources,
        out_specs=pl.BlockSpec((share, ens), lambda d, w: (d, 0)),
    )
    return pl.pallas_call(
        functools.partial(couple_kernel, sources),
        grid_spec=grid_spec,
        out_shape=jax.ShapeDtypeStruct((heights * share, ens), kind),
        compiler_params=params(),
    )(where, matrix, *coeffs)


def pressure_kernel(pieces, bricks_ref, weight_ref, *refs):
    fields, (base_ref, mid_ref), (matrix,) = refs[:pieces], refs[pieces : pieces + 2], refs[pieces + 2 :]
    size = fields[0].shape[0]
    ens = base_ref.shape[1]
    slots = bricks_ref.shape[0]
    ids = bricks_ref[...].T
    weights = weight_ref[...].T
    rows = 64
    for top in range(0, BS, rows):
        id_of = [jnp.broadcast_to(ids[top : top + rows, k : k + 1], (rows, 128)) for k in range(slots)]
        weight_of = [
            jnp.broadcast_to(weights[top : top + rows, k : k + 1], (rows, 128)) for k in range(slots)
        ]
        lane = lax.broadcasted_iota(jnp.int32, (rows, 128), 1).astype(F32)
        for left in range(0, pieces * size, 128):
            here = lane + float(left)
            tile = jnp.zeros((rows, 128), F32)
            for k in range(slots):
                tile = jnp.where(id_of[k] == here, weight_of[k], tile)
            matrix[top : top + rows, left : left + 128] = tile.astype(BF16)
    total = None
    for first in range(0, pieces, 2):
        group = range(first, min(first + 2, pieces))
        field = jnp.concatenate([fields[j][...] for j in group], axis=0)
        term = dot(matrix[:, first * size : first * size + field.shape[0]], field)
        total = term if total is None else total + term
    base = total[:, :ens]
    base_ref[...] = base
    mid_ref[...] = base + STEP_SIZE * total[:, ens:]


def pressure(bricks, weights, fields):
    slots, patches = bricks.shape
    size, both = fields[0].shape
    ens = both // 2
    pieces = len(fields)
    return pl.pallas_call(
        functools.partial(pressure_kernel, pieces),
        grid=(patches // BS,),
        in_specs=[
            pl.BlockSpec((slots, BS), lambda n: (0, n)),
            pl.BlockSpec((slots, BS), lambda n: (0, n)),
        ]
        + [pl.BlockSpec((size, both), lambda n: (0, 0))] * pieces,
        out_specs=[pl.BlockSpec((BS, ens), lambda n: (n, 0))] * 2,
        out_shape=[jax.ShapeDtypeStruct((patches, ens), F32)] * 2,
        scratch_shapes=[pltpu.VMEM((BS, pieces * size), BF16)],
        compiler_params=params(),
    )(bricks, weights, *fields)


def field_and_rates(
    heights, slip_ref, state_ref, press_ref, numbers_ref, near_ref, before_ref, own_ref, after_ref,
    first_ref, last_ref, basis_ref, parts,
):
    n = pl.program_id(0)
    count = pl.num_programs(0)
    far = parts[0][...].astype(F32)
    for part in parts[1:]:
        far = far + part[...].astype(F32)
    far = far.astype(BF16)
    before = jnp.where(n == 0, first_ref[...], before_ref[...])
    after = jnp.where(n == count - 1, last_ref[...], after_ref[...])
    outer = dot(near_ref[0], before) + dot(near_ref[1], own_ref[...]) + dot(near_ref[2], after)
    outer = outer + dot_t(basis_ref[...], far)
    numbers = numbers_ref[...].T
    load, normal, inv_direct, inv_evolution, ratio, stiffness = (numbers[:, k : k + 1] for k in range(6))
    state = state_ref[...]
    tau = load - stiffness * slip_ref[...] - outer
    sigma = normal - press_ref[...]
    speed = jnp.exp((tau / sigma - state) * inv_direct)
    drift = ratio * (jnp.exp((REF_FRICTION - state) * inv_evolution) - speed)
    return speed, drift


def first_kernel(heights, *refs):
    inputs, parts = refs[:11], refs[11 : 11 + heights]
    basis_in_ref, slip_mid_ref, state_mid_ref, rounded_ref, coeff_ref = refs[11 + heights :]
    speed, drift = field_and_rates(heights, *inputs, parts)
    slip_mid = inputs[0][...] + STEP_SIZE * speed
    slip_mid_ref[...] = slip_mid
    state_mid_ref[...] = inputs[1][...] + STEP_SIZE * drift
    rounded = slip_mid.astype(BF16)
    rounded_ref[...] = rounded
    coeff_ref[...] = dot(basis_in_ref[...], rounded).astype(BF16)


def second_kernel(heights, *refs):
    inputs, parts = refs[:11], refs[11 : 11 + heights]
    slip_ref, state_ref, slip_out_ref, state_out_ref = refs[11 + heights :]
    speed, drift = field_and_rates(heights, *inputs, parts)
    slip_out_ref[...] = 0.5 * (slip_ref[...] + inputs[0][...]) + (0.5 * STEP_SIZE) * speed
    state_out_ref[...] = 0.5 * (state_ref[...] + inputs[1][...]) + (0.5 * STEP_SIZE) * drift


def section(slip, state, press, numbers, near_blocks, rounded, first, last, basis_out, parts, basis_in=None, start=None):
    patches, ens = slip.shape
    count = patches // BS
    heights = len(parts)
    block = pl.BlockSpec((BS, ens), lambda n: (n, 0))
    whole = pl.BlockSpec((BS, ens), lambda n: (0, 0))
    basis = pl.BlockSpec((R, BS), lambda n: (0, n))
    levels = pl.BlockSpec((R, ens), lambda n: (n, 0))
    in_specs = [
        block,
        block,
        block,
        pl.BlockSpec((numbers.shape[0], BS), lambda n: (0, n)),
        pl.BlockSpec((3, BS, BS), lambda n: (0, n, 0)),
        pl.BlockSpec((BS, ens), lambda n: (jnp.maximum(n - 1, 0), 0)),
        block,
        pl.BlockSpec((BS, ens), lambda n: (jnp.minimum(n + 1, count - 1), 0)),
        whole,
        whole,
        basis,
    ] + [levels] * heights
    operands = [slip, state, press, numbers, near_blocks, rounded, rounded, rounded, first, last, basis_out, *parts]
    full = jax.ShapeDtypeStruct((patches, ens), F32)
    if start is None:
        return pl.pallas_call(
            functools.partial(first_kernel, heights),
            grid=(count,),
            in_specs=in_specs + [basis],
            out_specs=[block, block, block, levels],
            out_shape=[
                full,
                full,
                jax.ShapeDtypeStruct((patches, ens), BF16),
                jax.ShapeDtypeStruct((count * R, ens), BF16),
            ],
            compiler_params=params(),
        )(*operands, basis_in)
    return pl.pallas_call(
        functools.partial(second_kernel, heights),
        grid=(count,),
        in_specs=in_specs + [block, block],
        out_specs=[block, block],
        out_shape=[full, full],
        compiler_params=params(),
    )(*operands, *start)


def brick_weights(adj_bricks, adj_count, adj_weight):
    slots = adj_bricks.shape[0]
    live = adj_count[None, :] > jnp.arange(slots, dtype=jnp.int32)[:, None]
    weights = jnp.where(live, adj_weight, 0.0)
    total = jnp.sum(weights, axis=0)
    merged = []
    for k in range(slots):
        same = adj_bricks == adj_bricks[k][None, :]
        merged.append(jnp.sum(jnp.where(same, weights, 0.0), axis=0))
    return live, jnp.stack(merged) / total[None, :]


def masked_coupling(coupling, block_rank, row_index, col_index, row_count, col_count):
    rows, sources, width = coupling.shape
    share = width // R
    blocks = rows // R
    receiver = row_index * blocks + jnp.arange(blocks, dtype=jnp.int32)
    source = (
        (jnp.arange(sources, dtype=jnp.int32)[:, None] * col_count + col_index) * share
        + jnp.arange(share, dtype=jnp.int32)[None, :]
    )
    apart = jnp.abs(receiver[:, None, None] - source[None]) > 1
    rank = jnp.where(apart, block_rank, 0)
    rank = jnp.transpose(rank, (1, 0, 2))
    rank_full = jnp.repeat(rank, R, axis=2).reshape(sources, blocks, 1, width)
    level = jnp.maximum(
        jnp.arange(R, dtype=jnp.int32)[:, None], jnp.arange(width, dtype=jnp.int32)[None, :] % R
    )
    keep = level[None, None] < rank_full
    matrix = jnp.transpose(coupling, (1, 0, 2)).reshape(sources, blocks, R, width)
    return jnp.where(keep, matrix, jnp.zeros((), BF16)).reshape(sources, rows, width)


def per_device(
    slip,
    state,
    tau_load,
    normal_stress,
    direct_effect,
    evolution_effect,
    slip_distance,
    self_stiffness,
    near_blocks,
    basis_in,
    basis_out,
    coupling,
    block_rank,
    adj_bricks,
    adj_count,
    adj_weight,
    pressure_now,
    pressure_rate,
):
    row_count = lax.axis_size("row")
    col_count = lax.axis_size("col")
    row_index = lax.axis_index("row")
    col_index = lax.axis_index("col")
    heights = col_count // 2
    height, core = col_index // 2, col_index % 2
    both = ("row", "col")
    devices = row_count * col_count

    def to_row(array, d):
        return lax.ppermute(array, "row", [(i, (i + d) % row_count) for i in range(row_count)])

    def to_height(array, d):
        pairs = [(2 * z + k, 2 * ((z + d) % heights) + k) for z in range(heights) for k in range(2)]
        return lax.ppermute(array, "col", pairs)

    def to_core(array):
        return lax.ppermute(array, "col", [(2 * z + k, 2 * z + 1 - k) for z in range(heights) for k in range(2)])

    def halo(rounded):
        up = [(i, i + 1) for i in range(devices - 1)]
        down = [(j, i) for i, j in up]
        before = lax.ppermute(rounded[-BS:], both, up)
        after = lax.ppermute(rounded[:BS], both, down)
        return before, after

    joined = jnp.concatenate([pressure_now, pressure_rate], axis=1)
    size = joined.shape[0]
    fields = [joined] + [to_height(joined, d) for d in range(1, heights)]
    fields = fields + [to_core(field) for field in fields]
    live, weights = brick_weights(adj_bricks, adj_count, adj_weight)
    owner, within = adj_bricks // size, adj_bricks % size
    distance = (height - owner // 2) % heights
    other = (owner % 2 != core).astype(jnp.int32)
    bricks = jnp.where(live, (other * heights + distance) * size + within, -1).astype(F32)

    numbers = jnp.stack(
        [
            tau_load,
            normal_stress,
            1.0 / direct_effect,
            1.0 / evolution_effect,
            evolution_effect / slip_distance,
            self_stiffness,
            tau_load,
            tau_load,
        ]
    )
    masked = masked_coupling(coupling, block_rank, row_index, col_index, row_count, col_count)
    source_rows = [(row_index - d) % row_count for d in range(row_count)]
    own_where = jnp.stack([col_index] + source_rows).astype(jnp.int32)
    pair_where = jnp.stack([2 * height + 1 - core] + source_rows).astype(jnp.int32)
    share = coupling.shape[2]

    def far_parts(coeff):
        coeffs = [coeff] + [to_row(coeff, d) for d in range(1, row_count)]
        sent = to_core(couple(pair_where, masked, coeffs, heights, BF16))
        kept = couple(own_where, masked, coeffs, heights, F32)
        chip = (kept + sent.astype(F32)).astype(BF16)
        pieces = [chip[d * share : (d + 1) * share] for d in range(heights)]
        return pieces[:1] + [to_height(pieces[d], d) for d in range(1, heights)]

    coeff, rounded = project(slip, basis_in)
    first, last = halo(rounded)
    parts = far_parts(coeff)
    base_press, mid_press = pressure(bricks, weights, fields)
    slip_mid, state_mid, rounded, coeff = section(
        slip, state, base_press, numbers, near_blocks, rounded, first, last, basis_out, parts, basis_in=basis_in
    )
    first, last = halo(rounded)
    parts = far_parts(coeff)
    slip_out, state_out = section(
        slip_mid, state_mid, mid_press, numbers, near_blocks, rounded, first, last, basis_out, parts,
        start=(slip, state),
    )
    return (slip_out, state_out)


def solution(mesh):
    in_specs = (
        P(("row", "col"), None),
        P(("row", "col"), None),
        P(("row", "col")),
        P(("row", "col")),
        P(("row", "col")),
        P(("row", "col")),
        P(("row", "col")),
        P(("row", "col")),
        P(None, ("row", "col"), None),
        P(None, ("row", "col")),
        P(None, ("row", "col")),
        P("row", None, "col"),
        P("row", None, "col"),
        P(None, ("row", "col")),
        P(("row", "col")),
        P(None, ("row", "col")),
        P("col", None),
        P("col", None),
    )
    out_specs = (P(("row", "col"), None), P(("row", "col"), None))
    return jax.shard_map(
        per_device, mesh=mesh, in_specs=in_specs, out_specs=out_specs, check_vma=False
    )
```

```python
import functools

import jax
import jax.numpy as jnp
from jax import lax
from jax.experimental import pallas as pl
from jax.experimental.pallas import tpu as pltpu
from jax.sharding import PartitionSpec as P

BS = 256
R = 32

STEP_SIZE = 0.5
REF_FRICTION = 0.6
LIMIT = 16 * 1024 * 1024
F32 = jnp.float32
BF16 = jnp.bfloat16


def dot(a, b):
    return jnp.dot(a, b, preferred_element_type=F32)


def dot_t(a, b):
    return lax.dot_general(a, b, (((0,), (0,)), ((), ())), preferred_element_type=F32)


def params():
    return pltpu.CompilerParams(vmem_limit_bytes=LIMIT)


def project_kernel(slip_ref, basis_ref, coeff_ref, rounded_ref):
    rounded = slip_ref[...].astype(BF16)
    rounded_ref[...] = rounded
    coeff_ref[...] = dot(basis_ref[...], rounded).astype(BF16)


def project(slip, basis_in):
    patches, ens = slip.shape
    count = patches // BS
    return pl.pallas_call(
        project_kernel,
        grid=(count,),
        in_specs=[
            pl.BlockSpec((BS, ens), lambda n: (n, 0)),
            pl.BlockSpec((R, BS), lambda n: (0, n)),
        ],
        out_specs=[
            pl.BlockSpec((R, ens), lambda n: (n, 0)),
            pl.BlockSpec((BS, ens), lambda n: (n, 0)),
        ],
        out_shape=[
            jax.ShapeDtypeStruct((count * R, ens), BF16),
            jax.ShapeDtypeStruct((patches, ens), BF16),
        ],
        compiler_params=params(),
    )(slip, basis_in)


def couple_kernel(sources, where_ref, matrix_ref, *refs):
    coeffs, out_ref = refs[:sources], refs[sources]
    total = None
    for d in range(sources):
        term = dot(matrix_ref[where_ref[1 + d]], coeffs[d][...])
        total = term if total is None else total + term
    out_ref[...] = total.astype(out_ref.dtype)


def couple(where, matrix, coeffs, heights, kind):
    sources, rows, width = matrix.shape
    share, ens = coeffs[0].shape
    grid_spec = pltpu.PrefetchScalarGridSpec(
        num_scalar_prefetch=1,
        grid=(heights,),
        in_specs=[
            pl.BlockSpec(
                (sources, share, width),
                lambda d, w: (0, 2 * lax.rem(lax.div(w[0], 2) + d, heights) + lax.rem(w[0], 2), 0),
            )
        ]
        + [pl.BlockSpec((share, ens), lambda d, w: (0, 0))] * sources,
        out_specs=pl.BlockSpec((share, ens), lambda d, w: (d, 0)),
    )
    return pl.pallas_call(
        functools.partial(couple_kernel, sources),
        grid_spec=grid_spec,
        out_shape=jax.ShapeDtypeStruct((heights * share, ens), kind),
        compiler_params=params(),
    )(where, matrix, *coeffs)


def chip_sum_kernel(kept_ref, sent_ref, *outs):
    share = outs[0].shape[0]
    for d, out_ref in enumerate(outs):
        rows = slice(d * share, (d + 1) * share)
        out_ref[...] = (kept_ref[rows] + sent_ref[rows].astype(F32)).astype(BF16)


def chip_sum(kept, sent, heights):
    rows, ens = kept.shape
    return pl.pallas_call(
        chip_sum_kernel,
        out_shape=[jax.ShapeDtypeStruct((rows // heights, ens), BF16)] * heights,
        compiler_params=params(),
    )(kept, sent)


def fill_weights(bricks_ref, weight_ref, matrix):
    slots = bricks_ref.shape[0]
    ids = bricks_ref[...].T
    weights = weight_ref[...].T
    rows = 16
    lane = lax.broadcasted_iota(jnp.int32, (rows, 128), 1).astype(F32)
    for top in range(0, BS, rows):
        id_of = [jnp.broadcast_to(ids[top : top + rows, k : k + 1], (rows, 128)) for k in range(slots)]
        weight_of = [
            jnp.broadcast_to(weights[top : top + rows, k : k + 1], (rows, 128)) for k in range(slots)
        ]
        for left in range(0, matrix.shape[1], 128):
            here = lane + float(left)
            tile = jnp.zeros((rows, 128), F32)
            for k in range(slots):
                tile = jnp.where(id_of[k] == here, weight_of[k], tile)
            matrix[top : top + rows, left : left + 128] = tile.astype(BF16)


def near_tau(slip, numbers, near_ref, rounded_ref, first_ref, last_ref):
    n = pl.program_id(0)
    count = pl.num_programs(0)
    before_at = pl.multiple_of(jnp.maximum(n - 1, 0) * BS, BS)
    own_at = pl.multiple_of(n * BS, BS)
    after_at = pl.multiple_of(jnp.minimum(n + 1, count - 1) * BS, BS)
    before = jnp.where(n == 0, first_ref[...], rounded_ref[pl.ds(before_at, BS), :])
    after = jnp.where(n == count - 1, last_ref[...], rounded_ref[pl.ds(after_at, BS), :])
    near = dot(near_ref[0], before) + dot(near_ref[1], rounded_ref[pl.ds(own_at, BS), :]) + dot(near_ref[2], after)
    return numbers[:, 0:1] - numbers[:, 5:6] * slip - near


def prepare_first_kernel(
    bricks_ref, weight_ref, own_ref, other_ref, slip_ref, state_ref, numbers_ref, near_ref, rounded_ref, first_ref,
    last_ref, shift_ref, scale_ref, rest_ref, scale_mid_ref, matrix,
):
    fill_weights(bricks_ref, weight_ref, matrix)
    half = own_ref.shape[0]
    ens = slip_ref.shape[1]
    total = dot(matrix[:, :half], own_ref[...]) + dot(matrix[:, half:], other_ref[...])
    numbers = numbers_ref[...].T
    normal, inv_direct, inv_evolution, ratio = (numbers[:, k : k + 1] for k in range(1, 5))
    base = total[:, :ens]
    scale = inv_direct / (normal - base)
    scale_ref[...] = scale
    scale_mid_ref[...] = inv_direct / (normal - (base + STEP_SIZE * total[:, ens:]))
    state = state_ref[...]
    tau = near_tau(slip_ref[...], numbers, near_ref, rounded_ref, first_ref, last_ref)
    shift_ref[...] = tau * scale - state * inv_direct
    rest_ref[...] = state + (STEP_SIZE * ratio) * jnp.exp((REF_FRICTION - state) * inv_evolution)


def finish_first_kernel(
    heights, shift_ref, scale_ref, rest_ref, slip_ref, numbers_ref, basis_out_ref, basis_in_ref, *refs
):
    parts, (slip_mid_ref, state_mid_ref, rounded_ref, coeff_ref) = refs[:heights], refs[heights:]
    speed = jnp.exp(shift_ref[...] - scale_ref[...] * far_field(basis_out_ref, parts))
    slip_mid = slip_ref[...] + STEP_SIZE * speed
    slip_mid_ref[...] = slip_mid
    state_mid_ref[...] = rest_ref[...] - (STEP_SIZE * numbers_ref[4:5, :].T) * speed
    rounded = slip_mid.astype(BF16)
    rounded_ref[...] = rounded
    coeff_ref[...] = dot(basis_in_ref[...], rounded).astype(BF16)


def prepare_second_kernel(
    slip_ref, state_ref, slip_mid_ref, state_mid_ref, scale_ref, numbers_ref, near_ref, rounded_ref, first_ref,
    last_ref, shift_ref, slip_rest_ref, rest_ref,
):
    numbers = numbers_ref[...].T
    inv_direct, inv_evolution, ratio = (numbers[:, k : k + 1] for k in range(2, 5))
    slip = slip_mid_ref[...]
    state = state_mid_ref[...]
    tau = near_tau(slip, numbers, near_ref, rounded_ref, first_ref, last_ref)
    shift_ref[...] = tau * scale_ref[...] - state * inv_direct
    slip_rest_ref[...] = 0.5 * (slip_ref[...] + slip)
    friction = jnp.exp((REF_FRICTION - state) * inv_evolution)
    rest_ref[...] = 0.5 * (state_ref[...] + state) + (0.5 * STEP_SIZE * ratio) * friction


def finish_second_kernel(heights, shift_ref, scale_ref, rest_ref, slip_rest_ref, numbers_ref, basis_out_ref, *refs):
    parts, (slip_out_ref, state_out_ref) = refs[:heights], refs[heights:]
    speed = jnp.exp(shift_ref[...] - scale_ref[...] * far_field(basis_out_ref, parts))
    slip_out_ref[...] = slip_rest_ref[...] + (0.5 * STEP_SIZE) * speed
    state_out_ref[...] = rest_ref[...] - (0.5 * STEP_SIZE * numbers_ref[4:5, :].T) * speed


def far_field(basis_ref, parts):
    far = parts[0][...].astype(F32)
    for part in parts[1:]:
        far = far + part[...].astype(F32)
    return dot_t(basis_ref[...], far.astype(BF16))


class Specs:
    def __init__(self, slip, numbers):
        patches, ens = slip.shape
        self.count = patches // BS
        self.block = pl.BlockSpec((BS, ens), lambda n: (n, 0))
        self.edge = pl.BlockSpec((BS, ens), lambda n: (0, 0))
        self.all = pl.BlockSpec((patches, ens), lambda n: (0, 0))
        self.basis = pl.BlockSpec((R, BS), lambda n: (0, n))
        self.levels = pl.BlockSpec((R, ens), lambda n: (n, 0))
        self.numbers = pl.BlockSpec((numbers.shape[0], BS), lambda n: (0, n))
        self.near = pl.BlockSpec((3, BS, BS), lambda n: (0, n, 0))
        self.full = jax.ShapeDtypeStruct((patches, ens), F32)
        self.half = jax.ShapeDtypeStruct((patches, ens), BF16)


def prepare_first(bricks, weights, own, other, slip, state, numbers, near_blocks, rounded, first, last):
    s = Specs(slip, numbers)
    slots = pl.BlockSpec((bricks.shape[0], BS), lambda n: (0, n))
    field = pl.BlockSpec(own.shape, lambda n: (0, 0))
    return pl.pallas_call(
        prepare_first_kernel,
        grid=(s.count,),
        in_specs=[slots, slots, field, field, s.block, s.block, s.numbers, s.near, s.all, s.edge, s.edge],
        out_specs=[s.block] * 4,
        out_shape=[s.full] * 4,
        scratch_shapes=[pltpu.VMEM((BS, 2 * own.shape[0]), BF16)],
        compiler_params=params(),
    )(bricks, weights, own, other, slip, state, numbers, near_blocks, rounded, first, last)


def prepare_second(slip, state, slip_mid, state_mid, scale, numbers, near_blocks, rounded, first, last):
    s = Specs(slip, numbers)
    return pl.pallas_call(
        prepare_second_kernel,
        grid=(s.count,),
        in_specs=[s.block] * 5 + [s.numbers, s.near, s.all, s.edge, s.edge],
        out_specs=[s.block] * 3,
        out_shape=[s.full] * 3,
        compiler_params=params(),
    )(slip, state, slip_mid, state_mid, scale, numbers, near_blocks, rounded, first, last)


def finish_first(shift, scale, rest, slip, numbers, basis_out, basis_in, parts):
    s = Specs(slip, numbers)
    return pl.pallas_call(
        functools.partial(finish_first_kernel, len(parts)),
        grid=(s.count,),
        in_specs=[s.block] * 4 + [s.numbers, s.basis, s.basis] + [s.levels] * len(parts),
        out_specs=[s.block, s.block, s.block, s.levels],
        out_shape=[s.full, s.full, s.half, jax.ShapeDtypeStruct((s.count * R, slip.shape[1]), BF16)],
        compiler_params=params(),
    )(shift, scale, rest, slip, numbers, basis_out, basis_in, *parts)


def finish_second(shift, scale, rest, slip_rest, numbers, basis_out, parts):
    s = Specs(shift, numbers)
    return pl.pallas_call(
        functools.partial(finish_second_kernel, len(parts)),
        grid=(s.count,),
        in_specs=[s.block] * 4 + [s.numbers, s.basis] + [s.levels] * len(parts),
        out_specs=[s.block] * 2,
        out_shape=[s.full] * 2,
        compiler_params=params(),
    )(shift, scale, rest, slip_rest, numbers, basis_out, *parts)


def brick_weights(adj_bricks, adj_count, adj_weight):
    slots = adj_bricks.shape[0]
    live = adj_count[None, :] > jnp.arange(slots, dtype=jnp.int32)[:, None]
    weights = jnp.where(live, adj_weight, 0.0)
    total = jnp.sum(weights, axis=0)
    merged = []
    for k in range(slots):
        same = adj_bricks == adj_bricks[k][None, :]
        merged.append(jnp.sum(jnp.where(same, weights, 0.0), axis=0))
    return live, jnp.stack(merged) / total[None, :]


def masked_coupling(coupling, block_rank, row_index, col_index, row_count, col_count):
    rows, sources, width = coupling.shape
    share = width // R
    blocks = rows // R
    receiver = row_index * blocks + jnp.arange(blocks, dtype=jnp.int32)
    source = (
        (jnp.arange(sources, dtype=jnp.int32)[:, None] * col_count + col_index) * share
        + jnp.arange(share, dtype=jnp.int32)[None, :]
    )
    apart = jnp.abs(receiver[:, None, None] - source[None]) > 1
    rank = jnp.where(apart, block_rank, 0)
    rank = jnp.transpose(rank, (1, 0, 2))
    rank_full = jnp.repeat(rank, R, axis=2).reshape(sources, blocks, 1, width)
    level = jnp.maximum(
        jnp.arange(R, dtype=jnp.int32)[:, None], jnp.arange(width, dtype=jnp.int32)[None, :] % R
    )
    keep = level[None, None] < rank_full
    matrix = jnp.transpose(coupling, (1, 0, 2)).reshape(sources, blocks, R, width)
    return jnp.where(keep, matrix, jnp.zeros((), BF16)).reshape(sources, rows, width)


def per_device(
    slip,
    state,
    tau_load,
    normal_stress,
    direct_effect,
    evolution_effect,
    slip_distance,
    self_stiffness,
    near_blocks,
    basis_in,
    basis_out,
    coupling,
    block_rank,
    adj_bricks,
    adj_count,
    adj_weight,
    pressure_now,
    pressure_rate,
):
    row_count = lax.axis_size("row")
    col_count = lax.axis_size("col")
    row_index = lax.axis_index("row")
    col_index = lax.axis_index("col")
    heights = col_count // 2
    height, core = col_index // 2, col_index % 2
    both = ("row", "col")
    devices = row_count * col_count

    def to_row(array, d):
        return lax.ppermute(array, "row", [(i, (i + d) % row_count) for i in range(row_count)])

    def to_height(array, d):
        pairs = [(2 * z + k, 2 * ((z + d) % heights) + k) for z in range(heights) for k in range(2)]
        return lax.ppermute(array, "col", pairs)

    def to_core(array):
        return lax.ppermute(array, "col", [(2 * z + k, 2 * z + 1 - k) for z in range(heights) for k in range(2)])

    def halo(rounded):
        up = [(i, i + 1) for i in range(devices - 1)]
        down = [(j, i) for i, j in up]
        before = lax.ppermute(rounded[-BS:], both, up)
        after = lax.ppermute(rounded[:BS], both, down)
        return before, after

    size = pressure_now.shape[0]
    live, weights = brick_weights(adj_bricks, adj_count, adj_weight)
    owner, within = adj_bricks // size, adj_bricks % size
    distance = (height - owner // 2) % heights
    other = (owner % 2 != core).astype(jnp.int32)
    bricks = jnp.where(live, (other * heights + distance) * size + within, -1).astype(F32)

    numbers = jnp.stack(
        [
            tau_load,
            normal_stress,
            1.0 / direct_effect,
            1.0 / evolution_effect,
            evolution_effect / slip_distance,
            self_stiffness,
            tau_load,
            tau_load,
        ]
    )
    masked = masked_coupling(coupling, block_rank, row_index, col_index, row_count, col_count)
    source_rows = [(row_index - d) % row_count for d in range(row_count)]
    own_where = jnp.stack([col_index] + source_rows).astype(jnp.int32)
    pair_where = jnp.stack([2 * height + 1 - core] + source_rows).astype(jnp.int32)
    share = coupling.shape[2]

    def far_parts(coeffs):
        sent = to_core(couple(pair_where, masked, coeffs, heights, BF16))
        kept = couple(own_where, masked, coeffs, heights, F32)
        pieces = list(chip_sum(kept, sent, heights))
        return pieces[:1] + [to_height(pieces[d], d) for d in range(1, heights)]

    def row_coeffs(coeff):
        return [coeff] + [to_row(coeff, d) for d in range(1, row_count)]

    coeff, rounded = project(slip, basis_in)
    coeffs = row_coeffs(coeff)
    now, rate, _ = lax.optimization_barrier((pressure_now, pressure_rate, coeff))
    joined = jnp.concatenate([now, rate], axis=1)
    own = jnp.concatenate([joined] + [to_height(joined, d) for d in range(1, heights)], axis=0)
    first, last = halo(rounded)
    coeffs, first, last, own = lax.optimization_barrier((coeffs, first, last, own))
    other = to_core(own)
    parts = far_parts(coeffs)
    shift, scale, rest, scale_mid = prepare_first(
        bricks, weights, own, other, slip, state, numbers, near_blocks, rounded, first, last
    )
    slip_mid, state_mid, rounded, coeff = finish_first(
        shift, scale, rest, slip, numbers, basis_out, basis_in, parts
    )
    coeffs = row_coeffs(coeff)
    first, last = halo(rounded)
    coeffs, first, last = lax.optimization_barrier((coeffs, first, last))
    parts = far_parts(coeffs)
    shift, slip_rest, rest = prepare_second(
        slip, state, slip_mid, state_mid, scale_mid, numbers, near_blocks, rounded, first, last
    )
    slip_out, state_out = finish_second(shift, scale_mid, rest, slip_rest, numbers, basis_out, parts)
    return (slip_out, state_out)


def solution(mesh):
    in_specs = (
        P(("row", "col"), None),
        P(("row", "col"), None),
        P(("row", "col")),
        P(("row", "col")),
        P(("row", "col")),
        P(("row", "col")),
        P(("row", "col")),
        P(("row", "col")),
        P(None, ("row", "col"), None),
        P(None, ("row", "col")),
        P(None, ("row", "col")),
        P("row", None, "col"),
        P("row", None, "col"),
        P(None, ("row", "col")),
        P(("row", "col")),
        P(None, ("row", "col")),
        P("col", None),
        P("col", None),
    )
    out_specs = (P(("row", "col"), None), P(("row", "col"), None))
    return jax.shard_map(
        per_device, mesh=mesh, in_specs=in_specs, out_specs=out_specs, check_vma=False
    )
```

```python
import functools

import jax
import jax.numpy as jnp
from jax import lax
from jax.experimental import pallas as pl
from jax.experimental.pallas import tpu as pltpu
from jax.sharding import PartitionSpec as P

BS = 256
R = 32

STEP_SIZE = 0.5
REF_FRICTION = 0.6
LIMIT = 16 * 1024 * 1024
F32 = jnp.float32
BF16 = jnp.bfloat16


def dot(a, b):
    return jnp.dot(a, b, preferred_element_type=F32)


def dot_t(a, b):
    return lax.dot_general(a, b, (((0,), (0,)), ((), ())), preferred_element_type=F32)


VMEM = pl.BlockSpec(memory_space=pltpu.VMEM)
SMEM = pl.BlockSpec(memory_space=pltpu.SMEM)


def call(kernel, outs, *operands, specs=None, **grid):
    return pl.pallas_call(
        kernel,
        in_specs=specs or [VMEM] * len(operands),
        out_shape=outs,
        compiler_params=pltpu.CompilerParams(vmem_limit_bytes=LIMIT),
        **grid,
    )(*operands)


def rows_at(n, size):
    return pl.ds(pl.multiple_of(n * size, size), size)


def project_kernel(slip_ref, basis_ref, coeff_ref, rounded_ref, first_ref, last_ref):
    count = slip_ref.shape[0] // BS

    @pl.loop(0, count)
    def _(n):
        at = rows_at(n, BS)
        rounded = slip_ref[at, :].astype(BF16)
        rounded_ref[at, :] = rounded
        coeff_ref[rows_at(n, R), :] = dot(basis_ref[:, at], rounded).astype(BF16)

    first_ref[...] = rounded_ref[:BS]
    last_ref[...] = rounded_ref[-BS:]


def project(slip, basis_in):
    patches, ens = slip.shape
    edge = jax.ShapeDtypeStruct((BS, ens), BF16)
    return call(
        project_kernel,
        [
            jax.ShapeDtypeStruct((patches // BS * R, ens), BF16),
            jax.ShapeDtypeStruct((patches, ens), BF16),
            edge,
            edge,
        ],
        slip,
        basis_in,
    )


def setup_kernel(
    load_ref, normal_ref, direct_ref, evolution_ref, distance_ref, stiffness_ref, bricks_ref, count_ref, weight_ref,
    now_ref, rate_ref, coeff_ref, numbers_ref, ids_ref, shares_ref, joined_ref,
):
    slots, patches = bricks_ref.shape
    ens = now_ref.shape[1]
    joined_ref[:, :ens] = now_ref[...]
    joined_ref[:, ens:] = rate_ref[...]

    @pl.loop(0, patches // BS)
    def _(n):
        at = rows_at(n, BS)
        evolution = evolution_ref[:, at]
        rows = [
            load_ref[:, at],
            normal_ref[:, at],
            1.0 / direct_ref[:, at],
            1.0 / evolution,
            evolution / distance_ref[:, at],
            stiffness_ref[:, at],
        ]
        rows = rows + rows[:2]
        numbers_ref[at, :] = jnp.concatenate(rows, axis=0).T
        bricks = bricks_ref[:, at]
        slot = lax.broadcasted_iota(jnp.int32, (slots, BS), 0)
        weights = jnp.where(slot < count_ref[:, at], weight_ref[:, at], 0.0)
        merged = jnp.zeros((slots, BS), F32)
        for k in range(slots):
            merged = merged + jnp.where(bricks == bricks[k : k + 1], weights[k : k + 1], 0.0)
        shares = merged / jnp.sum(weights, axis=0, keepdims=True)
        ids_ref[at, :] = bricks.T.astype(jnp.int32).astype(jnp.int16)
        shares_ref[at, :] = shares.T.astype(BF16)


def weights_kernel(ids_ref, shares_ref, matrix_ref):
    patches, slots = ids_ref.shape
    rows = 32

    @pl.loop(0, patches // rows)
    def _(n):
        at = rows_at(n, rows)
        ids, shares = ids_ref[at, :], shares_ref[at, :]
        id_of = [jnp.broadcast_to(ids[:, k : k + 1], (rows, 128)) for k in range(slots)]
        share_of = [jnp.broadcast_to(shares[:, k : k + 1], (rows, 128)) for k in range(slots)]
        lane = lax.broadcasted_iota(jnp.int32, (rows, 128), 1).astype(jnp.int16)
        for left in range(0, matrix_ref.shape[1], 128):
            here = lane + jnp.int16(left)
            tile = jnp.zeros((rows, 128), BF16)
            for k in range(slots):
                tile = jnp.where(id_of[k] == here, share_of[k], tile)
            matrix_ref[at, left : left + 128] = tile


def couple_kernel(sources, heights, where_ref, matrix_ref, *refs):
    coeffs, out_ref = refs[:sources], refs[sources]
    share = coeffs[0].shape[0]

    @pl.loop(0, heights)
    def _(d):
        height = lax.rem(where_ref[0] + d, heights)
        at = rows_at(2 * height + where_ref[1], share)
        total = None
        for step in range(sources):
            term = dot(matrix_ref[where_ref[2 + step], at, :], coeffs[step][...])
            total = term if total is None else total + term
        out_ref[rows_at(d, share), :] = total.astype(out_ref.dtype)


def couple(where, matrix, coeffs, heights, kind):
    share, ens = coeffs[0].shape
    return call(
        functools.partial(couple_kernel, len(coeffs), heights),
        jax.ShapeDtypeStruct((heights * share, ens), kind),
        where,
        matrix,
        *coeffs,
        specs=[SMEM] + [VMEM] * (1 + len(coeffs)),
    )


def chip_sum_kernel(kept_ref, sent_ref, *outs):
    share = outs[0].shape[0]
    for d, out_ref in enumerate(outs):

        @pl.loop(0, share // 32)
        def _(n):
            at = pl.ds(pl.multiple_of(d * share + n * 32, 32), 32)
            out_ref[rows_at(n, 32), :] = (kept_ref[at, :] + sent_ref[at, :].astype(F32)).astype(BF16)


def chip_sum(kept, sent, heights):
    rows, ens = kept.shape
    return list(call(chip_sum_kernel, [jax.ShapeDtypeStruct((rows // heights, ens), BF16)] * heights, kept, sent))


def near_tau(n, slip, numbers, near_ref, rounded_ref, first_ref, last_ref):
    count = rounded_ref.shape[0] // BS
    at = rows_at(n, BS)
    before = jnp.where(n == 0, first_ref[...], rounded_ref[rows_at(jnp.maximum(n - 1, 0), BS), :])
    after = jnp.where(n == count - 1, last_ref[...], rounded_ref[rows_at(jnp.minimum(n + 1, count - 1), BS), :])
    near = dot(near_ref[0, at, :], before) + dot(near_ref[1, at, :], rounded_ref[at, :]) + dot(near_ref[2, at, :], after)
    return numbers[:, 0:1] - numbers[:, 5:6] * slip - near


def prepare_first_kernel(
    matrix_ref, own_ref, other_ref, slip_ref, state_ref, numbers_ref, near_ref, rounded_ref, first_ref,
    last_ref, shift_ref, scale_ref, rest_ref, scale_mid_ref,
):
    half = own_ref.shape[0]
    patches, ens = slip_ref.shape

    @pl.loop(0, patches // BS)
    def _(n):
        at = rows_at(n, BS)
        total = dot(matrix_ref[at, :half], own_ref[...]) + dot(matrix_ref[at, half:], other_ref[...])
        numbers = numbers_ref[at, :]
        normal, inv_direct, inv_evolution, ratio = (numbers[:, k : k + 1] for k in range(1, 5))
        base = total[:, :ens]
        scale = inv_direct / (normal - base)
        scale_ref[at, :] = scale
        scale_mid_ref[at, :] = inv_direct / (normal - (base + STEP_SIZE * total[:, ens:]))
        state = state_ref[at, :]
        tau = near_tau(n, slip_ref[at, :], numbers, near_ref, rounded_ref, first_ref, last_ref)
        shift_ref[at, :] = tau * scale - state * inv_direct
        rest_ref[at, :] = state + (STEP_SIZE * ratio) * jnp.exp((REF_FRICTION - state) * inv_evolution)


def far_speed(n, shift_ref, scale_ref, basis_ref, parts):
    at = rows_at(n, BS)
    levels = rows_at(n, R)
    far = parts[0][levels, :].astype(F32)
    for part in parts[1:]:
        far = far + part[levels, :].astype(F32)
    return jnp.exp(shift_ref[at, :] - scale_ref[at, :] * dot_t(basis_ref[:, at], far.astype(BF16)))


def finish_first_kernel(
    heights, shift_ref, scale_ref, rest_ref, slip_ref, numbers_ref, basis_out_ref, basis_in_ref, *refs
):
    parts = refs[:heights]
    slip_mid_ref, state_mid_ref, rounded_ref, coeff_ref, first_ref, last_ref = refs[heights:]

    @pl.loop(0, slip_ref.shape[0] // BS)
    def _(n):
        at = rows_at(n, BS)
        speed = far_speed(n, shift_ref, scale_ref, basis_out_ref, parts)
        slip_mid = slip_ref[at, :] + STEP_SIZE * speed
        slip_mid_ref[at, :] = slip_mid
        state_mid_ref[at, :] = rest_ref[at, :] - (STEP_SIZE * numbers_ref[at, 4:5]) * speed
        rounded = slip_mid.astype(BF16)
        rounded_ref[at, :] = rounded
        coeff_ref[rows_at(n, R), :] = dot(basis_in_ref[:, at], rounded).astype(BF16)

    first_ref[...] = rounded_ref[:BS]
    last_ref[...] = rounded_ref[-BS:]


def prepare_second_kernel(
    slip_ref, state_ref, slip_mid_ref, state_mid_ref, scale_ref, numbers_ref, near_ref, rounded_ref, first_ref,
    last_ref, shift_ref, slip_rest_ref, rest_ref,
):
    @pl.loop(0, slip_ref.shape[0] // BS)
    def _(n):
        at = rows_at(n, BS)
        numbers = numbers_ref[at, :]
        inv_direct, inv_evolution, ratio = (numbers[:, k : k + 1] for k in range(2, 5))
        slip = slip_mid_ref[at, :]
        state = state_mid_ref[at, :]
        tau = near_tau(n, slip, numbers, near_ref, rounded_ref, first_ref, last_ref)
        shift_ref[at, :] = tau * scale_ref[at, :] - state * inv_direct
        slip_rest_ref[at, :] = 0.5 * (slip_ref[at, :] + slip)
        friction = jnp.exp((REF_FRICTION - state) * inv_evolution)
        rest_ref[at, :] = 0.5 * (state_ref[at, :] + state) + (0.5 * STEP_SIZE * ratio) * friction


def finish_second_kernel(heights, shift_ref, scale_ref, rest_ref, slip_rest_ref, numbers_ref, basis_out_ref, *refs):
    parts, (slip_out_ref, state_out_ref) = refs[:heights], refs[heights:]
    n = pl.program_id(0)
    at = rows_at(n, BS)
    speed = far_speed(n, shift_ref, scale_ref, basis_out_ref, parts)
    slip_out_ref[...] = slip_rest_ref[at, :] + (0.5 * STEP_SIZE) * speed
    state_out_ref[...] = rest_ref[at, :] - (0.5 * STEP_SIZE * numbers_ref[at, 4:5]) * speed


def masked_coupling(coupling, block_rank, row_index, col_index, row_count, col_count):
    rows, sources, width = coupling.shape
    share = width // R
    blocks = rows // R
    receiver = row_index * blocks + jnp.arange(blocks, dtype=jnp.int32)
    source = (
        (jnp.arange(sources, dtype=jnp.int32)[:, None] * col_count + col_index) * share
        + jnp.arange(share, dtype=jnp.int32)[None, :]
    )
    apart = jnp.abs(receiver[:, None, None] - source[None]) > 1
    rank = jnp.where(apart, block_rank, 0)
    rank = jnp.transpose(rank, (1, 0, 2))
    rank_full = jnp.repeat(rank, R, axis=2).reshape(sources, blocks, 1, width)
    level = jnp.maximum(
        jnp.arange(R, dtype=jnp.int32)[:, None], jnp.arange(width, dtype=jnp.int32)[None, :] % R
    )
    keep = level[None, None] < rank_full
    matrix = jnp.transpose(coupling, (1, 0, 2)).reshape(sources, blocks, R, width)
    return jnp.where(keep, matrix, jnp.zeros((), BF16)).reshape(sources, rows, width)


def per_device(
    slip,
    state,
    tau_load,
    normal_stress,
    direct_effect,
    evolution_effect,
    slip_distance,
    self_stiffness,
    near_blocks,
    basis_in,
    basis_out,
    coupling,
    block_rank,
    adj_bricks,
    adj_count,
    adj_weight,
    pressure_now,
    pressure_rate,
):
    row_count = lax.axis_size("row")
    col_count = lax.axis_size("col")
    row_index = lax.axis_index("row")
    col_index = lax.axis_index("col")
    heights = col_count // 2
    height, core = col_index // 2, col_index % 2
    both = ("row", "col")
    devices = row_count * col_count

    def to_row(array, d):
        return lax.ppermute(array, "row", [(i, (i + d) % row_count) for i in range(row_count)])

    def to_height(array, d):
        pairs = [(2 * z + k, 2 * ((z + d) % heights) + k) for z in range(heights) for k in range(2)]
        return lax.ppermute(array, "col", pairs)

    def to_core(array):
        return lax.ppermute(array, "col", [(2 * z + k, 2 * z + 1 - k) for z in range(heights) for k in range(2)])

    def halo(first, last):
        up = [(i, i + 1) for i in range(devices - 1)]
        down = [(j, i) for i, j in up]
        return lax.ppermute(last, both, up), lax.ppermute(first, both, down)

    patches, ens = slip.shape
    slots = adj_bricks.shape[0]
    size = pressure_now.shape[0]
    share = coupling.shape[2]
    owner, within = adj_bricks // size, adj_bricks % size
    away = (height - owner // 2) % heights
    other_core = (owner % 2 != core).astype(jnp.int32)
    live = adj_count[None, :] > jnp.arange(slots, dtype=jnp.int32)[:, None]
    bricks = jnp.where(live, (other_core * heights + away) * size + within, -1).astype(F32)
    masked = masked_coupling(coupling, block_rank, row_index, col_index, row_count, col_count)
    source_rows = [(row_index - d) % row_count for d in range(row_count)]
    own_where = jnp.stack([height, core] + source_rows).astype(jnp.int32)
    pair_where = jnp.stack([height, 1 - core] + source_rows).astype(jnp.int32)

    def far_parts(coeffs):
        sent = to_core(couple(pair_where, masked, coeffs, heights, BF16))
        kept = couple(own_where, masked, coeffs, heights, F32)
        pieces = chip_sum(kept, sent, heights)
        return pieces[:1] + [to_height(pieces[d], d) for d in range(1, heights)]

    def row_coeffs(coeff):
        return [coeff] + [to_row(coeff, d) for d in range(1, row_count)]

    full = jax.ShapeDtypeStruct((patches, ens), F32)
    half = jax.ShapeDtypeStruct((patches, ens), BF16)
    edge = jax.ShapeDtypeStruct((BS, ens), BF16)
    per_patch = [tau_load, normal_stress, direct_effect, evolution_effect, slip_distance, self_stiffness]

    coeff, rounded, first, last = project(slip, basis_in)
    coeffs = row_coeffs(coeff)
    numbers, ids, shares, joined = call(
        setup_kernel,
        [
            jax.ShapeDtypeStruct((patches, 8), F32),
            jax.ShapeDtypeStruct((patches, slots), jnp.int16),
            jax.ShapeDtypeStruct((patches, slots), BF16),
            jax.ShapeDtypeStruct((size, 2 * ens), BF16),
        ],
        *[array[None] for array in per_patch],
        bricks,
        adj_count[None],
        adj_weight,
        pressure_now,
        pressure_rate,
        coeff,
    )
    own = jnp.concatenate([joined] + [to_height(joined, d) for d in range(1, heights)], axis=0)
    other = to_core(own)
    first, last = halo(first, last)
    coeffs, first, last = lax.optimization_barrier((coeffs, first, last))
    parts = far_parts(coeffs)
    matrix = call(
        weights_kernel, jax.ShapeDtypeStruct((patches, 2 * heights * size), BF16), ids, shares
    )
    shift, scale, rest, scale_mid = call(
        prepare_first_kernel, [full] * 4, matrix, own, other, slip, state, numbers, near_blocks, rounded, first, last
    )
    slip_mid, state_mid, rounded, coeff, first, last = call(
        functools.partial(finish_first_kernel, heights),
        [full, full, half, jax.ShapeDtypeStruct((patches // BS * R, ens), BF16), edge, edge],
        shift, scale, rest, slip, numbers, basis_out, basis_in, *parts,
    )
    coeffs = row_coeffs(coeff)
    first, last = halo(first, last)
    coeffs, first, last = lax.optimization_barrier((coeffs, first, last))
    parts = far_parts(coeffs)
    shift, slip_rest, rest = call(
        prepare_second_kernel, [full] * 3,
        slip, state, slip_mid, state_mid, scale_mid, numbers, near_blocks, rounded, first, last,
    )
    slip_out, state_out = call(
        functools.partial(finish_second_kernel, heights),
        [full] * 2,
        shift, scale_mid, rest, slip_rest, numbers, basis_out, *parts,
        grid=(patches // BS,),
        out_specs=[pl.BlockSpec((BS, ens), lambda n: (n, 0))] * 2,
    )
    return (slip_out, state_out)


def solution(mesh):
    in_specs = (
        P(("row", "col"), None),
        P(("row", "col"), None),
        P(("row", "col")),
        P(("row", "col")),
        P(("row", "col")),
        P(("row", "col")),
        P(("row", "col")),
        P(("row", "col")),
        P(None, ("row", "col"), None),
        P(None, ("row", "col")),
        P(None, ("row", "col")),
        P("row", None, "col"),
        P("row", None, "col"),
        P(None, ("row", "col")),
        P(("row", "col")),
        P(None, ("row", "col")),
        P("col", None),
        P("col", None),
    )
    out_specs = (P(("row", "col"), None), P(("row", "col"), None))
    return jax.shard_map(
        per_device, mesh=mesh, in_specs=in_specs, out_specs=out_specs, check_vma=False
    )
```

```python
import functools

import jax
import jax.numpy as jnp
from jax import lax
from jax.experimental import pallas as pl
from jax.experimental.pallas import tpu as pltpu
from jax.sharding import PartitionSpec as P

BS = 256
R = 32

STEP_SIZE = 0.5
REF_FRICTION = 0.6
LIMIT = 16 * 1024 * 1024
F32 = jnp.float32
BF16 = jnp.bfloat16


def dot(a, b):
    return jnp.dot(a, b, preferred_element_type=F32)


def dot_t(a, b):
    return lax.dot_general(a, b, (((0,), (0,)), ((), ())), preferred_element_type=F32)


VMEM = pl.BlockSpec(memory_space=pltpu.VMEM)
SMEM = pl.BlockSpec(memory_space=pltpu.SMEM)


def call(kernel, outs, *operands, specs=None, **grid):
    return pl.pallas_call(
        kernel,
        in_specs=specs or [VMEM] * len(operands),
        out_shape=outs,
        compiler_params=pltpu.CompilerParams(vmem_limit_bytes=LIMIT),
        **grid,
    )(*operands)


def rows_at(n, size):
    return pl.ds(pl.multiple_of(n * size, size), size)


HBM = pl.BlockSpec(memory_space=pl.ANY)


def in_hbm(*arrays):
    return [pltpu.with_memory_space_constraint(array, pltpu.HBM) for array in arrays]


def start_copies(pairs, sems, first=0):
    copies = [pltpu.make_async_copy(a, b, sems.at[first + k]) for k, (a, b) in enumerate(pairs)]
    for copy in copies:
        copy.start()
    return copies


def project_kernel(slip_hbm, basis_hbm, coeff_ref, rounded_ref, first_ref, last_ref, slip_ref, basis_ref, sems):
    count = slip_ref.shape[0] // BS
    blocks = [pl.ds(n * BS, BS) for n in range(count)]
    copies = start_copies(
        [(basis_hbm, basis_ref)] + [(slip_hbm.at[at, :], slip_ref.at[at, :]) for at in blocks], sems
    )
    copies[0].wait()
    for n, at in enumerate(blocks):
        copies[1 + n].wait()
        rounded = slip_ref[at, :].astype(BF16)
        rounded_ref[at, :] = rounded
        if n == 0:
            first_ref[...] = rounded
        if n == count - 1:
            last_ref[...] = rounded
        coeff_ref[n * R : (n + 1) * R, :] = dot(basis_ref[:, at], rounded).astype(BF16)


def project(slip, basis_in):
    patches, ens = slip.shape
    count = patches // BS
    edge = jax.ShapeDtypeStruct((BS, ens), BF16)
    return call(
        project_kernel,
        [
            jax.ShapeDtypeStruct((count * R, ens), BF16),
            jax.ShapeDtypeStruct((patches, ens), BF16),
            edge,
            edge,
            jax.ShapeDtypeStruct((patches, ens), F32),
        ],
        *in_hbm(slip, basis_in),
        specs=[HBM] * 2,
        scratch_shapes=[pltpu.VMEM(basis_in.shape, BF16), pltpu.SemaphoreType.DMA((1 + count,))],
    )


def ranks_kernel(
    col_count, where_ref, rank_hbm, now_hbm, rate_hbm, coeff_ref, wide_ref, joined_ref, rank_ref, sems
):
    sources, share, blocks = rank_ref.shape
    ens = now_hbm.shape[1]
    copies = start_copies(
        [
            (rank_hbm, rank_ref),
            (now_hbm, joined_ref.at[:, pl.ds(0, ens)]),
            (rate_hbm, joined_ref.at[:, pl.ds(ens, ens)]),
        ],
        sems,
    )
    width = share * R
    column = lax.broadcasted_iota(jnp.int32, (share, width), 1)
    spread = (lax.div(column, R) == lax.broadcasted_iota(jnp.int32, (share, width), 0)).astype(F32).astype(BF16)
    level = lax.rem(lax.broadcasted_iota(jnp.int32, (blocks, width), 1), R).astype(F32)
    receiver = where_ref[0] * blocks + lax.broadcasted_iota(jnp.int32, (share, blocks), 1)
    copies[0].wait()
    for source in range(sources):
        own = (source * col_count + where_ref[1]) * share + lax.broadcasted_iota(jnp.int32, (share, blocks), 0)
        rank = jnp.where(jnp.abs(receiver - own) > 1, rank_ref[source], 0).astype(F32)
        wide = dot_t(rank.astype(BF16), spread)
        wide_ref[source] = jnp.where(level < wide, wide, 0.0)
    copies[1].wait()
    copies[2].wait()


def side_by_side_kernel(*refs):
    pieces, out_ref = refs[:-1], refs[-1]
    size = pieces[0].shape[0]
    for k, piece in enumerate(pieces):
        out_ref[k * size : (k + 1) * size, :] = piece[...]


def weights_kernel(
    heights, size, where_ref, load_hbm, normal_hbm, direct_hbm, evolution_hbm, distance_hbm, stiffness_hbm,
    count_hbm, bricks_hbm, weight_hbm, near_hbm, state_hbm, after_ref, numbers_ref, matrix_ref, near_ref, state_ref,
    vectors, count_ref, bricks_ref, weight_ref, id_wide, share_wide, sems,
):
    slots, patches = bricks_ref.shape
    sources = [load_hbm, normal_hbm, direct_hbm, evolution_hbm, distance_hbm, stiffness_hbm]
    small = [(source, vectors.at[k]) for k, source in enumerate(sources)]
    small = small + [(count_hbm, count_ref), (bricks_hbm, bricks_ref), (weight_hbm, weight_ref)]
    copies = start_copies(small, sems)
    large = start_copies([(near_hbm, near_ref), (state_hbm, state_ref)], sems, len(small))
    height, core = where_ref[0].astype(F32), where_ref[1].astype(F32)
    lanes = 128
    column = lax.div(lax.broadcasted_iota(jnp.int32, (slots, slots * lanes), 1), lanes)
    spread = (column == lax.broadcasted_iota(jnp.int32, (slots, slots * lanes), 0)).astype(F32).astype(BF16)
    spread_both = jnp.concatenate([spread, spread], axis=0)
    for copy in copies:
        copy.wait()

    @pl.loop(0, patches // BS)
    def _(n):
        at = rows_at(n, BS)
        load, normal, direct, evolution, distance, stiffness = (vectors[k, :, at] for k in range(6))
        rows = [load, normal, 1.0 / direct, 1.0 / evolution, evolution / distance, stiffness, load, normal]
        numbers_ref[at, :] = jnp.concatenate(rows, axis=0).T
        bricks = bricks_ref[:, at].astype(F32)
        live = lax.broadcasted_iota(jnp.int32, (slots, BS), 0) < count_ref[:, at]
        weights = jnp.where(live, weight_ref[:, at], 0.0)
        merged = jnp.zeros((slots, BS), F32)
        for k in range(slots):
            merged = merged + jnp.where(bricks == bricks[k : k + 1], weights[k : k + 1], 0.0)
        shares = merged / jnp.sum(weights, axis=0, keepdims=True)
        owner = jnp.floor((bricks + 0.5) * (1.0 / size))
        chip = jnp.floor(owner * 0.5 + 0.25)
        away = height - chip
        away = jnp.where(away < 0, away + heights, away)
        other = jnp.where(owner - 2.0 * chip == core, 0.0, float(heights))
        place = jnp.where(live, (other + away - owner) * size + bricks, -1.0)
        high = jnp.floor((place + 0.5) * (1.0 / lanes)) * lanes
        place_both = jnp.concatenate([high, place - high], axis=0).astype(BF16)
        id_wide[...] = dot_t(place_both, spread_both)
        share_wide[...] = dot_t(shares.astype(BF16), spread)
        group = 16

        @pl.loop(0, BS // group, unroll=2)
        def _(m):
            part = rows_at(m, group)
            to = pl.ds(pl.multiple_of(n * BS + m * group, group), group)
            ids = [id_wide[part, k * lanes : (k + 1) * lanes] for k in range(slots)]
            values = [share_wide[part, k * lanes : (k + 1) * lanes] for k in range(slots)]
            lane = lax.broadcasted_iota(jnp.int32, (group, lanes), 1).astype(F32)
            for left in range(0, matrix_ref.shape[1], lanes):
                here = lane + float(left)
                tile = jnp.zeros((group, lanes), F32)
                for k in range(slots):
                    tile = jnp.where(ids[k] == here, values[k], tile)
                matrix_ref[to, left : left + lanes] = tile.astype(BF16)

    for copy in large:
        copy.wait()


def couple_kernel(sources, heights, where_ref, matrix_ref, *refs):
    coeffs, out_ref = refs[:sources], refs[sources]
    share = coeffs[0].shape[0]

    @pl.loop(0, heights)
    def _(d):
        height = lax.rem(where_ref[0] + d, heights)
        at = rows_at(2 * height + where_ref[1], share)
        total = None
        for step in range(sources):
            term = dot(matrix_ref[where_ref[2 + step], at, :], coeffs[step][...])
            total = term if total is None else total + term
        out_ref[rows_at(d, share), :] = total.astype(out_ref.dtype)


def couple(where, matrix, coeffs, heights, kind):
    share, ens = coeffs[0].shape
    return call(
        functools.partial(couple_kernel, len(coeffs), heights),
        jax.ShapeDtypeStruct((heights * share, ens), kind),
        where,
        matrix,
        *coeffs,
        specs=[SMEM] + [VMEM] * (1 + len(coeffs)),
    )


def chip_sum_kernel(kept_ref, sent_ref, *outs):
    share = outs[0].shape[0]
    for d, out_ref in enumerate(outs):

        @pl.loop(0, share // 32)
        def _(n):
            at = pl.ds(pl.multiple_of(d * share + n * 32, 32), 32)
            out_ref[rows_at(n, 32), :] = (kept_ref[at, :] + sent_ref[at, :].astype(F32)).astype(BF16)


def chip_sum(kept, sent, heights):
    rows, ens = kept.shape
    return list(call(chip_sum_kernel, [jax.ShapeDtypeStruct((rows // heights, ens), BF16)] * heights, kept, sent))


def near_tau(n, slip, numbers, near_ref, rounded_ref, first_ref, last_ref):
    count = rounded_ref.shape[0] // BS
    at = rows_at(n, BS)
    before = jnp.where(n == 0, first_ref[...], rounded_ref[rows_at(jnp.maximum(n - 1, 0), BS), :])
    after = jnp.where(n == count - 1, last_ref[...], rounded_ref[rows_at(jnp.minimum(n + 1, count - 1), BS), :])
    near = dot(near_ref[0, at, :], before) + dot(near_ref[1, at, :], rounded_ref[at, :]) + dot(near_ref[2, at, :], after)
    return numbers[:, 0:1] - numbers[:, 5:6] * slip - near


def prepare_first_kernel(
    matrix_ref, own_ref, other_ref, slip_ref, state_ref, numbers_ref, near_ref, rounded_ref, first_ref,
    last_ref, shift_ref, scale_ref, rest_ref, scale_mid_ref,
):
    half = own_ref.shape[0]
    patches, ens = slip_ref.shape

    @pl.loop(0, patches // BS)
    def _(n):
        at = rows_at(n, BS)
        total = dot(matrix_ref[at, :half], own_ref[...]) + dot(matrix_ref[at, half:], other_ref[...])
        numbers = numbers_ref[at, :]
        normal, inv_direct, inv_evolution, ratio = (numbers[:, k : k + 1] for k in range(1, 5))
        base = total[:, :ens]
        scale = inv_direct / (normal - base)
        scale_ref[at, :] = scale
        scale_mid_ref[at, :] = inv_direct / (normal - (base + STEP_SIZE * total[:, ens:]))
        state = state_ref[at, :]
        tau = near_tau(n, slip_ref[at, :], numbers, near_ref, rounded_ref, first_ref, last_ref)
        shift_ref[at, :] = tau * scale - state * inv_direct
        rest_ref[at, :] = state + (STEP_SIZE * ratio) * jnp.exp((REF_FRICTION - state) * inv_evolution)


def far_speed(n, shift_ref, scale_ref, basis_ref, parts):
    at = rows_at(n, BS)
    levels = rows_at(n, R)
    far = parts[0][levels, :].astype(F32)
    for part in parts[1:]:
        far = far + part[levels, :].astype(F32)
    return jnp.exp(shift_ref[at, :] - scale_ref[at, :] * dot_t(basis_ref[:, at], far.astype(BF16)))


def finish_first_kernel(
    heights, shift_ref, scale_ref, rest_ref, slip_ref, numbers_ref, basis_out_ref, basis_in_ref, *refs
):
    parts = refs[:heights]
    slip_mid_ref, state_mid_ref, rounded_ref, coeff_ref, first_ref, last_ref = refs[heights:]

    @pl.loop(0, slip_ref.shape[0] // BS)
    def _(n):
        at = rows_at(n, BS)
        speed = far_speed(n, shift_ref, scale_ref, basis_out_ref, parts)
        slip_mid = slip_ref[at, :] + STEP_SIZE * speed
        slip_mid_ref[at, :] = slip_mid
        state_mid_ref[at, :] = rest_ref[at, :] - (STEP_SIZE * numbers_ref[at, 4:5]) * speed
        rounded = slip_mid.astype(BF16)
        rounded_ref[at, :] = rounded
        coeff_ref[rows_at(n, R), :] = dot(basis_in_ref[:, at], rounded).astype(BF16)

    first_ref[...] = rounded_ref[:BS]
    last_ref[...] = rounded_ref[-BS:]


def prepare_second_kernel(
    slip_ref, state_ref, slip_mid_ref, state_mid_ref, scale_ref, numbers_ref, near_ref, rounded_ref, first_ref,
    last_ref, shift_ref, slip_rest_ref, rest_ref,
):
    @pl.loop(0, slip_ref.shape[0] // BS)
    def _(n):
        at = rows_at(n, BS)
        numbers = numbers_ref[at, :]
        inv_direct, inv_evolution, ratio = (numbers[:, k : k + 1] for k in range(2, 5))
        slip = slip_mid_ref[at, :]
        state = state_mid_ref[at, :]
        tau = near_tau(n, slip, numbers, near_ref, rounded_ref, first_ref, last_ref)
        shift_ref[at, :] = tau * scale_ref[at, :] - state * inv_direct
        slip_rest_ref[at, :] = 0.5 * (slip_ref[at, :] + slip)
        friction = jnp.exp((REF_FRICTION - state) * inv_evolution)
        rest_ref[at, :] = 0.5 * (state_ref[at, :] + state) + (0.5 * STEP_SIZE * ratio) * friction


def finish_second_kernel(heights, shift_ref, scale_ref, rest_ref, slip_rest_ref, numbers_ref, basis_out_ref, *refs):
    parts, (slip_out_ref, state_out_ref) = refs[:heights], refs[heights:]
    n = pl.program_id(0)
    at = rows_at(n, BS)
    speed = far_speed(n, shift_ref, scale_ref, basis_out_ref, parts)
    slip_out_ref[...] = slip_rest_ref[at, :] + (0.5 * STEP_SIZE) * speed
    state_out_ref[...] = rest_ref[at, :] - (0.5 * STEP_SIZE * numbers_ref[at, 4:5]) * speed


def masked_coupling(coupling, wide):
    rows, sources, width = coupling.shape
    blocks = rows // R
    keep = jnp.arange(R, dtype=jnp.int32).astype(F32)[None, None, :, None] < wide[:, :, None, :]
    matrix = jnp.transpose(coupling, (1, 0, 2)).reshape(sources, blocks, R, width)
    masked = jnp.where(keep, matrix, jnp.zeros((), BF16)).reshape(sources, rows, width)
    return pltpu.with_memory_space_constraint(masked, pltpu.VMEM)


def per_device(
    slip,
    state,
    tau_load,
    normal_stress,
    direct_effect,
    evolution_effect,
    slip_distance,
    self_stiffness,
    near_blocks,
    basis_in,
    basis_out,
    coupling,
    block_rank,
    adj_bricks,
    adj_count,
    adj_weight,
    pressure_now,
    pressure_rate,
):
    row_count = lax.axis_size("row")
    col_count = lax.axis_size("col")
    row_index = lax.axis_index("row")
    col_index = lax.axis_index("col")
    heights = col_count // 2
    height, core = col_index // 2, col_index % 2
    both = ("row", "col")
    devices = row_count * col_count

    def to_row(array, d):
        return lax.ppermute(array, "row", [(i, (i + d) % row_count) for i in range(row_count)])

    def to_height(array, d):
        pairs = [(2 * z + k, 2 * ((z + d) % heights) + k) for z in range(heights) for k in range(2)]
        return lax.ppermute(array, "col", pairs)

    def to_core(array):
        return lax.ppermute(array, "col", [(2 * z + k, 2 * z + 1 - k) for z in range(heights) for k in range(2)])

    def halo(first, last):
        up = [(i, i + 1) for i in range(devices - 1)]
        down = [(j, i) for i, j in up]
        return lax.ppermute(last, both, up), lax.ppermute(first, both, down)

    patches, ens = slip.shape
    slots = adj_bricks.shape[0]
    size = pressure_now.shape[0]
    share = coupling.shape[2]
    source_rows = [(row_index - d) % row_count for d in range(row_count)]
    own_where = jnp.stack([height, core] + source_rows).astype(jnp.int32)
    pair_where = jnp.stack([height, 1 - core] + source_rows).astype(jnp.int32)

    def far_parts(coeffs, first, last):
        sent = to_core(couple(pair_where, masked, coeffs, heights, BF16))
        kept = couple(own_where, masked, coeffs, heights, F32)
        pieces = chip_sum(kept, sent, heights)
        pieces, first, last = lax.optimization_barrier((pieces, first, last))
        parts = pieces[:1] + [to_height(pieces[d], d) for d in range(1, heights)]
        return parts, *halo(first, last)

    def row_coeffs(coeff):
        return [coeff] + [to_row(coeff, d) for d in range(1, row_count)]

    full = jax.ShapeDtypeStruct((patches, ens), F32)
    half = jax.ShapeDtypeStruct((patches, ens), BF16)
    edge = jax.ShapeDtypeStruct((BS, ens), BF16)
    per_patch = [tau_load, normal_stress, direct_effect, evolution_effect, slip_distance, self_stiffness]

    coeff, rounded, first, last, slip = project(slip, basis_in)
    coeffs = row_coeffs(coeff)
    ranks = jnp.transpose(block_rank, (1, 2, 0))
    place = jnp.stack([row_index, col_index]).astype(jnp.int32)
    wide, joined = call(
        functools.partial(ranks_kernel, col_count),
        [
            jax.ShapeDtypeStruct((ranks.shape[0], ranks.shape[2], share), F32),
            jax.ShapeDtypeStruct((size, 2 * ens), BF16),
        ],
        place,
        *in_hbm(ranks, pressure_now, pressure_rate),
        coeff,
        specs=[SMEM] + [HBM] * 3 + [VMEM],
        scratch_shapes=[pltpu.VMEM(ranks.shape, jnp.int32), pltpu.SemaphoreType.DMA((3,))],
    )
    own = call(
        side_by_side_kernel,
        jax.ShapeDtypeStruct((heights * size, 2 * ens), BF16),
        joined,
        *[to_height(joined, d) for d in range(1, heights)],
    )
    other = to_core(own)
    masked = masked_coupling(coupling, wide)
    parts, before, after = far_parts(coeffs, first, last)
    numbers, matrix, near, state = call(
        functools.partial(weights_kernel, heights, size),
        [
            jax.ShapeDtypeStruct((patches, 8), F32),
            jax.ShapeDtypeStruct((patches, 2 * heights * size), BF16),
            jax.ShapeDtypeStruct(near_blocks.shape, BF16),
            full,
        ],
        jnp.stack([height, core]).astype(jnp.int32),
        *in_hbm(*[array[None] for array in per_patch], adj_count[None], adj_bricks, adj_weight, near_blocks, state),
        parts[0],
        specs=[SMEM] + [HBM] * 11 + [VMEM],
        scratch_shapes=[
            pltpu.VMEM((6, 1, patches), F32),
            pltpu.VMEM((1, patches), jnp.int32),
            pltpu.VMEM(adj_bricks.shape, jnp.int32),
            pltpu.VMEM(adj_weight.shape, F32),
            pltpu.VMEM((BS, slots * 128), F32),
            pltpu.VMEM((BS, slots * 128), F32),
            pltpu.SemaphoreType.DMA((11,)),
        ],
    )
    shift, scale, rest, scale_mid = call(
        prepare_first_kernel, [full] * 4, matrix, own, other, slip, state, numbers, near, rounded, before, after
    )
    slip_mid, state_mid, rounded, coeff, first, last = call(
        functools.partial(finish_first_kernel, heights),
        [full, full, half, jax.ShapeDtypeStruct((patches // BS * R, ens), BF16), edge, edge],
        shift, scale, rest, slip, numbers, basis_out, basis_in, *parts,
    )
    coeffs = row_coeffs(coeff)
    parts, before, after = far_parts(coeffs, first, last)
    shift, slip_rest, rest = call(
        prepare_second_kernel, [full] * 3,
        slip, state, slip_mid, state_mid, scale_mid, numbers, near, rounded, before, after,
    )
    slip_out, state_out = call(
        functools.partial(finish_second_kernel, heights),
        [full] * 2,
        shift, scale_mid, rest, slip_rest, numbers, basis_out, *parts,
        grid=(patches // BS,),
        out_specs=[pl.BlockSpec((BS, ens), lambda n: (n, 0))] * 2,
    )
    return (slip_out, state_out)


def solution(mesh):
    in_specs = (
        P(("row", "col"), None),
        P(("row", "col"), None),
        P(("row", "col")),
        P(("row", "col")),
        P(("row", "col")),
        P(("row", "col")),
        P(("row", "col")),
        P(("row", "col")),
        P(None, ("row", "col"), None),
        P(None, ("row", "col")),
        P(None, ("row", "col")),
        P("row", None, "col"),
        P("row", None, "col"),
        P(None, ("row", "col")),
        P(("row", "col")),
        P(None, ("row", "col")),
        P("col", None),
        P("col", None),
    )
    out_specs = (P(("row", "col"), None), P(("row", "col"), None))
    return jax.shard_map(
        per_device, mesh=mesh, in_specs=in_specs, out_specs=out_specs, check_vma=False
    )
```

```python
import functools

import jax
import jax.numpy as jnp
from jax import lax
from jax.experimental import pallas as pl
from jax.experimental.pallas import tpu as pltpu
from jax.sharding import PartitionSpec as P

BS = 256
R = 32

STEP_SIZE = 0.5
REF_FRICTION = 0.6
LIMIT = 16 * 1024 * 1024
F32 = jnp.float32
BF16 = jnp.bfloat16


def dot(a, b):
    return jnp.dot(a, b, preferred_element_type=F32)


def dot_t(a, b):
    return lax.dot_general(a, b, (((0,), (0,)), ((), ())), preferred_element_type=F32)


VMEM = pl.BlockSpec(memory_space=pltpu.VMEM)
SMEM = pl.BlockSpec(memory_space=pltpu.SMEM)


def call(kernel, outs, *operands, specs=None, **grid):
    return pl.pallas_call(
        kernel,
        in_specs=specs or [VMEM] * len(operands),
        out_shape=outs,
        compiler_params=pltpu.CompilerParams(vmem_limit_bytes=LIMIT),
        **grid,
    )(*operands)


def rows_at(n, size):
    return pl.ds(pl.multiple_of(n * size, size), size)


HBM = pl.BlockSpec(memory_space=pl.ANY)


def in_hbm(*arrays):
    return [pltpu.with_memory_space_constraint(array, pltpu.HBM) for array in arrays]


def start_copies(pairs, sems, first=0):
    copies = [pltpu.make_async_copy(a, b, sems.at[first + k]) for k, (a, b) in enumerate(pairs)]
    for copy in copies:
        copy.start()
    return copies


def project_kernel(slip_hbm, basis_hbm, coeff_ref, rounded_ref, first_ref, last_ref, slip_ref, basis_ref, sems):
    count = slip_ref.shape[0] // BS
    blocks = [pl.ds(n * BS, BS) for n in range(count)]
    copies = start_copies(
        [(basis_hbm, basis_ref)] + [(slip_hbm.at[at, :], slip_ref.at[at, :]) for at in blocks], sems
    )
    copies[0].wait()
    for n, at in enumerate(blocks):
        copies[1 + n].wait()
        rounded = slip_ref[at, :].astype(BF16)
        rounded_ref[at, :] = rounded
        if n == 0:
            first_ref[...] = rounded
        if n == count - 1:
            last_ref[...] = rounded
        coeff_ref[n * R : (n + 1) * R, :] = dot(basis_ref[:, at], rounded).astype(BF16)


def project(slip, basis_in):
    patches, ens = slip.shape
    count = patches // BS
    edge = jax.ShapeDtypeStruct((BS, ens), BF16)
    return call(
        project_kernel,
        [
            jax.ShapeDtypeStruct((count * R, ens), BF16),
            jax.ShapeDtypeStruct((patches, ens), BF16),
            edge,
            edge,
            jax.ShapeDtypeStruct((patches, ens), F32),
        ],
        *in_hbm(slip, basis_in),
        specs=[HBM] * 2,
        scratch_shapes=[pltpu.VMEM(basis_in.shape, BF16), pltpu.SemaphoreType.DMA((1 + count,))],
    )


def ranks_kernel(
    col_count, where_ref, rank_hbm, now_hbm, rate_hbm, wide_ref, joined_ref, rank_ref, sems
):
    sources, share, blocks = rank_ref.shape
    ens = now_hbm.shape[1]
    copies = start_copies(
        [
            (rank_hbm, rank_ref),
            (now_hbm, joined_ref.at[:, pl.ds(0, ens)]),
            (rate_hbm, joined_ref.at[:, pl.ds(ens, ens)]),
        ],
        sems,
    )
    width = share * R
    column = lax.broadcasted_iota(jnp.int32, (share, width), 1)
    spread = (lax.div(column, R) == lax.broadcasted_iota(jnp.int32, (share, width), 0)).astype(F32).astype(BF16)
    level = lax.rem(lax.broadcasted_iota(jnp.int32, (blocks, width), 1), R).astype(F32)
    receiver = where_ref[0] * blocks + lax.broadcasted_iota(jnp.int32, (share, blocks), 1)
    copies[0].wait()
    for source in range(sources):
        own = (source * col_count + where_ref[1]) * share + lax.broadcasted_iota(jnp.int32, (share, blocks), 0)
        rank = jnp.where(jnp.abs(receiver - own) > 1, rank_ref[source], 0).astype(F32)
        wide = dot_t(rank.astype(BF16), spread)
        wide_ref[source] = jnp.where(level < wide, wide, 0.0)
    copies[1].wait()
    copies[2].wait()


def side_by_side_kernel(*refs):
    pieces, out_ref = refs[:-1], refs[-1]
    size = pieces[0].shape[0]
    for k, piece in enumerate(pieces):
        out_ref[k * size : (k + 1) * size, :] = piece[...]


def fill_numbers(vectors, numbers_ref):
    @pl.loop(0, numbers_ref.shape[0] // BS)
    def _(n):
        at = rows_at(n, BS)
        load, normal, direct, evolution, distance, stiffness = (vectors[k, :, at] for k in range(6))
        rows = [load, normal, 1.0 / direct, 1.0 / evolution, evolution / distance, stiffness, load, normal]
        numbers_ref[at, :] = jnp.concatenate(rows, axis=0).T


def weights_first_kernel(
    heights, size, where_ref, load_hbm, normal_hbm, direct_hbm, evolution_hbm, distance_hbm, stiffness_hbm,
    count_hbm, bricks_hbm, weight_hbm, after_ref, numbers_ref, matrix_ref,
    vectors, count_ref, bricks_ref, weight_ref, id_wide, share_wide, sems,
):
    sources = [load_hbm, normal_hbm, direct_hbm, evolution_hbm, distance_hbm, stiffness_hbm]
    small = [(source, vectors.at[k]) for k, source in enumerate(sources)]
    small = small + [(count_hbm, count_ref), (bricks_hbm, bricks_ref), (weight_hbm, weight_ref)]
    for copy in start_copies(small, sems):
        copy.wait()
    fill_numbers(vectors, numbers_ref)
    fill_weights(heights, size, 0, where_ref, count_ref, bricks_ref, weight_ref, matrix_ref, id_wide, share_wide)


def weights_second_kernel(
    heights, size, where_ref, count_hbm, bricks_hbm, weight_hbm, near_hbm, state_hbm, after_ref,
    matrix_ref, near_ref, state_ref, count_ref, bricks_ref, weight_ref, id_wide, share_wide, sems,
):
    small = [(count_hbm, count_ref), (bricks_hbm, bricks_ref), (weight_hbm, weight_ref)]
    copies = start_copies(small, sems)
    large = start_copies([(near_hbm, near_ref), (state_hbm, state_ref)], sems, len(small))
    for copy in copies:
        copy.wait()
    half = bricks_ref.shape[1] // 2
    fill_weights(heights, size, half, where_ref, count_ref, bricks_ref, weight_ref, matrix_ref, id_wide, share_wide)
    for copy in large:
        copy.wait()


def fill_weights(
    heights, size, start, where_ref, count_ref, bricks_ref, weight_ref, matrix_ref, id_wide, share_wide
):
    slots = bricks_ref.shape[0]
    height, core = where_ref[0].astype(F32), where_ref[1].astype(F32)
    lanes = 128
    column = lax.div(lax.broadcasted_iota(jnp.int32, (slots, slots * lanes), 1), lanes)
    spread = (column == lax.broadcasted_iota(jnp.int32, (slots, slots * lanes), 0)).astype(F32).astype(BF16)
    spread_both = jnp.concatenate([spread, spread], axis=0)

    @pl.loop(0, matrix_ref.shape[0] // BS)
    def _(n):
        at = pl.ds(pl.multiple_of(start + n * BS, BS), BS)
        bricks = bricks_ref[:, at].astype(F32)
        live = lax.broadcasted_iota(jnp.int32, (slots, BS), 0) < count_ref[:, at]
        weights = jnp.where(live, weight_ref[:, at], 0.0)
        merged = jnp.zeros((slots, BS), F32)
        for k in range(slots):
            merged = merged + jnp.where(bricks == bricks[k : k + 1], weights[k : k + 1], 0.0)
        shares = merged / jnp.sum(weights, axis=0, keepdims=True)
        owner = jnp.floor((bricks + 0.5) * (1.0 / size))
        chip = jnp.floor(owner * 0.5 + 0.25)
        away = height - chip
        away = jnp.where(away < 0, away + heights, away)
        other = jnp.where(owner - 2.0 * chip == core, 0.0, float(heights))
        place = jnp.where(live, (other + away - owner) * size + bricks, -1.0)
        high = jnp.floor((place + 0.5) * (1.0 / lanes)) * lanes
        place_both = jnp.concatenate([high, place - high], axis=0).astype(BF16)
        id_wide[...] = dot_t(place_both, spread_both)
        share_wide[...] = dot_t(shares.astype(BF16), spread)
        group = 16

        @pl.loop(0, BS // group, unroll=2)
        def _(m):
            part = rows_at(m, group)
            to = pl.ds(pl.multiple_of(n * BS + m * group, group), group)
            ids = [id_wide[part, k * lanes : (k + 1) * lanes] for k in range(slots)]
            values = [share_wide[part, k * lanes : (k + 1) * lanes] for k in range(slots)]
            lane = lax.broadcasted_iota(jnp.int32, (group, lanes), 1).astype(F32)
            for left in range(0, matrix_ref.shape[1], lanes):
                here = lane + float(left)
                tile = jnp.zeros((group, lanes), F32)
                for k in range(slots):
                    tile = jnp.where(ids[k] == here, values[k], tile)
                matrix_ref[to, left : left + lanes] = tile.astype(BF16)


def couple_kernel(sources, where_ref, matrix_ref, *refs):
    coeffs, out_ref = refs[:sources], refs[sources]
    total = None
    for step in range(sources):
        term = dot(matrix_ref[where_ref[2 + step]], coeffs[step][...])
        total = term if total is None else total + term
    out_ref[...] = total.astype(out_ref.dtype)


def couple(where, matrix, coeffs, heights, kind):
    sources, rows, width = matrix.shape
    share, ens = coeffs[0].shape
    return pl.pallas_call(
        functools.partial(couple_kernel, sources),
        grid_spec=pltpu.PrefetchScalarGridSpec(
            num_scalar_prefetch=1,
            grid=(heights,),
            in_specs=[
                pl.BlockSpec(
                    (sources, share, width), lambda d, w: (0, 2 * lax.rem(w[0] + d, heights) + w[1], 0)
                )
            ]
            + [VMEM] * sources,
            out_specs=pl.BlockSpec((share, ens), lambda d, w: (d, 0)),
        ),
        out_shape=jax.ShapeDtypeStruct((heights * share, ens), kind),
        compiler_params=pltpu.CompilerParams(vmem_limit_bytes=LIMIT),
    )(where, *in_hbm(matrix), *coeffs)


def edges_kernel(first_ref, last_ref, after_ref, first_out, last_out):
    first_out[...] = first_ref[...]
    last_out[...] = last_ref[...]


def chip_sum_kernel(kept_ref, sent_ref, *outs):
    share = outs[0].shape[0]
    for d, out_ref in enumerate(outs):

        @pl.loop(0, share // 32)
        def _(n):
            at = pl.ds(pl.multiple_of(d * share + n * 32, 32), 32)
            out_ref[rows_at(n, 32), :] = (kept_ref[at, :] + sent_ref[at, :].astype(F32)).astype(BF16)


def chip_sum(kept, sent, heights):
    rows, ens = kept.shape
    return list(call(chip_sum_kernel, [jax.ShapeDtypeStruct((rows // heights, ens), BF16)] * heights, kept, sent))


def near_tau(n, slip, numbers, near_ref, rounded_ref, first_ref, last_ref):
    count = rounded_ref.shape[0] // BS
    at = rows_at(n, BS)
    before = jnp.where(n == 0, first_ref[...], rounded_ref[rows_at(jnp.maximum(n - 1, 0), BS), :])
    after = jnp.where(n == count - 1, last_ref[...], rounded_ref[rows_at(jnp.minimum(n + 1, count - 1), BS), :])
    near = dot(near_ref[0, at, :], before) + dot(near_ref[1, at, :], rounded_ref[at, :]) + dot(near_ref[2, at, :], after)
    return numbers[:, 0:1] - numbers[:, 5:6] * slip - near


def prepare_first_kernel(
    low_ref, high_ref, own_ref, other_ref, slip_ref, state_ref, numbers_ref, near_ref, rounded_ref, first_ref,
    last_ref, shift_ref, scale_ref, rest_ref, scale_mid_ref,
):
    half = own_ref.shape[0]
    ens = slip_ref.shape[1]
    blocks = low_ref.shape[0] // BS

    def block(matrix_ref, m, n):
        at, own_at = rows_at(n, BS), rows_at(m, BS)
        total = dot(matrix_ref[own_at, :half], own_ref[...]) + dot(matrix_ref[own_at, half:], other_ref[...])
        numbers = numbers_ref[at, :]
        normal, inv_direct, inv_evolution, ratio = (numbers[:, k : k + 1] for k in range(1, 5))
        base = total[:, :ens]
        scale = inv_direct / (normal - base)
        scale_ref[at, :] = scale
        scale_mid_ref[at, :] = inv_direct / (normal - (base + STEP_SIZE * total[:, ens:]))
        state = state_ref[at, :]
        tau = near_tau(n, slip_ref[at, :], numbers, near_ref, rounded_ref, first_ref, last_ref)
        shift_ref[at, :] = tau * scale - state * inv_direct
        rest_ref[at, :] = state + (STEP_SIZE * ratio) * jnp.exp((REF_FRICTION - state) * inv_evolution)

    @pl.loop(0, blocks)
    def _(m):
        block(low_ref, m, m)

    @pl.loop(0, blocks)
    def _(m):
        block(high_ref, m, blocks + m)


def far_speed(n, shift_ref, scale_ref, basis_ref, parts):
    at = rows_at(n, BS)
    levels = rows_at(n, R)
    far = parts[0][levels, :].astype(F32)
    for part in parts[1:]:
        far = far + part[levels, :].astype(F32)
    return jnp.exp(shift_ref[at, :] - scale_ref[at, :] * dot_t(basis_ref[:, at], far.astype(BF16)))


def finish_first_kernel(
    heights, shift_ref, scale_ref, rest_ref, slip_ref, numbers_ref, basis_out_ref, basis_in_ref, *refs
):
    parts = refs[:heights]
    slip_mid_ref, state_mid_ref, rounded_ref, coeff_ref, first_ref, last_ref = refs[heights:]

    @pl.loop(0, slip_ref.shape[0] // BS)
    def _(n):
        at = rows_at(n, BS)
        speed = far_speed(n, shift_ref, scale_ref, basis_out_ref, parts)
        slip_mid = slip_ref[at, :] + STEP_SIZE * speed
        slip_mid_ref[at, :] = slip_mid
        state_mid_ref[at, :] = rest_ref[at, :] - (STEP_SIZE * numbers_ref[at, 4:5]) * speed
        rounded = slip_mid.astype(BF16)
        rounded_ref[at, :] = rounded
        coeff_ref[rows_at(n, R), :] = dot(basis_in_ref[:, at], rounded).astype(BF16)

    first_ref[...] = rounded_ref[:BS]
    last_ref[...] = rounded_ref[-BS:]


def prepare_second_kernel(
    slip_ref, state_ref, slip_mid_ref, state_mid_ref, scale_ref, numbers_ref, near_ref, rounded_ref, first_ref,
    last_ref, shift_ref, slip_rest_ref, rest_ref,
):
    @pl.loop(0, slip_ref.shape[0] // BS)
    def _(n):
        at = rows_at(n, BS)
        numbers = numbers_ref[at, :]
        inv_direct, inv_evolution, ratio = (numbers[:, k : k + 1] for k in range(2, 5))
        slip = slip_mid_ref[at, :]
        state = state_mid_ref[at, :]
        tau = near_tau(n, slip, numbers, near_ref, rounded_ref, first_ref, last_ref)
        shift_ref[at, :] = tau * scale_ref[at, :] - state * inv_direct
        slip_rest_ref[at, :] = 0.5 * (slip_ref[at, :] + slip)
        friction = jnp.exp((REF_FRICTION - state) * inv_evolution)
        rest_ref[at, :] = 0.5 * (state_ref[at, :] + state) + (0.5 * STEP_SIZE * ratio) * friction


def finish_second_kernel(heights, shift_ref, scale_ref, rest_ref, slip_rest_ref, numbers_ref, basis_out_ref, *refs):
    parts, (slip_out_ref, state_out_ref) = refs[:heights], refs[heights:]
    n = pl.program_id(0)
    at = rows_at(n, BS)
    speed = far_speed(n, shift_ref, scale_ref, basis_out_ref, parts)
    slip_out_ref[...] = slip_rest_ref[at, :] + (0.5 * STEP_SIZE) * speed
    state_out_ref[...] = rest_ref[at, :] - (0.5 * STEP_SIZE * numbers_ref[at, 4:5]) * speed


def masked_coupling(coupling, wide):
    rows, sources, width = coupling.shape
    blocks = rows // R
    keep = jnp.arange(R, dtype=jnp.int32).astype(F32)[None, None, :, None] < wide[:, :, None, :]
    matrix = jnp.transpose(coupling, (1, 0, 2)).reshape(sources, blocks, R, width)
    return jnp.where(keep, matrix, jnp.zeros((), BF16)).reshape(sources, rows, width)


def per_device(
    slip,
    state,
    tau_load,
    normal_stress,
    direct_effect,
    evolution_effect,
    slip_distance,
    self_stiffness,
    near_blocks,
    basis_in,
    basis_out,
    coupling,
    block_rank,
    adj_bricks,
    adj_count,
    adj_weight,
    pressure_now,
    pressure_rate,
):
    row_count = lax.axis_size("row")
    col_count = lax.axis_size("col")
    row_index = lax.axis_index("row")
    col_index = lax.axis_index("col")
    heights = col_count // 2
    height, core = col_index // 2, col_index % 2
    both = ("row", "col")
    devices = row_count * col_count

    def to_row(array, d):
        return lax.ppermute(array, "row", [(i, (i + d) % row_count) for i in range(row_count)])

    def to_height(array, d):
        pairs = [(2 * z + k, 2 * ((z + d) % heights) + k) for z in range(heights) for k in range(2)]
        return lax.ppermute(array, "col", pairs)

    def to_core(array):
        return lax.ppermute(array, "col", [(2 * z + k, 2 * z + 1 - k) for z in range(heights) for k in range(2)])

    def halo(first, last):
        up = [(i, i + 1) for i in range(devices - 1)]
        down = [(j, i) for i, j in up]
        return lax.ppermute(last, both, up), lax.ppermute(first, both, down)

    patches, ens = slip.shape
    slots = adj_bricks.shape[0]
    size = pressure_now.shape[0]
    share = coupling.shape[2]
    source_rows = [(row_index - d) % row_count for d in range(row_count)]
    own_where = jnp.stack([height, core] + source_rows).astype(jnp.int32)
    pair_where = jnp.stack([height, 1 - core] + source_rows).astype(jnp.int32)

    def far_parts(coeffs, first, last):
        sent = to_core(couple(pair_where, masked, coeffs, heights, BF16))
        kept = couple(own_where, masked, coeffs, heights, F32)
        pieces = chip_sum(kept, sent, heights)
        first, last = call(edges_kernel, [edge, edge], first, last, pieces[0])
        parts = pieces[:1] + [to_height(pieces[d], d) for d in range(1, heights)]
        return parts, *halo(first, last)

    def row_coeffs(coeff):
        return [coeff] + [to_row(coeff, d) for d in range(1, row_count)]

    full = jax.ShapeDtypeStruct((patches, ens), F32)
    half = jax.ShapeDtypeStruct((patches, ens), BF16)
    edge = jax.ShapeDtypeStruct((BS, ens), BF16)
    per_patch = [tau_load, normal_stress, direct_effect, evolution_effect, slip_distance, self_stiffness]

    ranks = jnp.transpose(block_rank, (1, 2, 0))
    place = jnp.stack([row_index, col_index]).astype(jnp.int32)
    wide, joined = call(
        functools.partial(ranks_kernel, col_count),
        [
            jax.ShapeDtypeStruct((ranks.shape[0], ranks.shape[2], share), F32),
            jax.ShapeDtypeStruct((size, 2 * ens), BF16),
        ],
        place,
        *in_hbm(ranks, pressure_now, pressure_rate),
        specs=[SMEM] + [HBM] * 3,
        scratch_shapes=[pltpu.VMEM(ranks.shape, jnp.int32), pltpu.SemaphoreType.DMA((3,))],
    )
    own = call(
        side_by_side_kernel,
        jax.ShapeDtypeStruct((heights * size, 2 * ens), BF16),
        joined,
        *[to_height(joined, d) for d in range(1, heights)],
    )
    other = to_core(own)
    masked = masked_coupling(coupling, wide)
    masked, slip = lax.optimization_barrier((masked, slip))
    coeff, rounded, first, last, slip = project(slip, basis_in)
    coeffs = row_coeffs(coeff)
    place = jnp.stack([height, core]).astype(jnp.int32)
    brick_lists = [adj_count[None], adj_bricks, adj_weight]
    part = jax.ShapeDtypeStruct((patches // 2, 2 * heights * size), BF16)
    list_scratch = [
        pltpu.VMEM((1, patches), jnp.int32),
        pltpu.VMEM(adj_bricks.shape, jnp.int32),
        pltpu.VMEM(adj_weight.shape, F32),
        pltpu.VMEM((BS, slots * 128), F32),
        pltpu.VMEM((BS, slots * 128), F32),
    ]
    numbers, low = call(
        functools.partial(weights_first_kernel, heights, size),
        [jax.ShapeDtypeStruct((patches, 8), F32), part],
        place,
        *in_hbm(*[array[None] for array in per_patch], *brick_lists),
        coeff,
        specs=[SMEM] + [HBM] * 9 + [VMEM],
        scratch_shapes=[pltpu.VMEM((6, 1, patches), F32)] + list_scratch + [pltpu.SemaphoreType.DMA((9,))],
    )
    coeffs, low = lax.optimization_barrier((coeffs, low))
    parts, before, after = far_parts(coeffs, first, last)
    high, near, state = call(
        functools.partial(weights_second_kernel, heights, size),
        [part, jax.ShapeDtypeStruct(near_blocks.shape, BF16), full],
        place,
        *in_hbm(*brick_lists, near_blocks, state),
        parts[0],
        specs=[SMEM] + [HBM] * 5 + [VMEM],
        scratch_shapes=list_scratch + [pltpu.SemaphoreType.DMA((5,))],
    )
    shift, scale, rest, scale_mid = call(
        prepare_first_kernel, [full] * 4, low, high, own, other, slip, state, numbers, near, rounded, before, after
    )
    slip_mid, state_mid, rounded, coeff, first, last = call(
        functools.partial(finish_first_kernel, heights),
        [full, full, half, jax.ShapeDtypeStruct((patches // BS * R, ens), BF16), edge, edge],
        shift, scale, rest, slip, numbers, basis_out, basis_in, *parts,
    )
    coeffs = row_coeffs(coeff)
    parts, before, after = far_parts(coeffs, first, last)
    shift, slip_rest, rest = call(
        prepare_second_kernel, [full] * 3,
        slip, state, slip_mid, state_mid, scale_mid, numbers, near, rounded, before, after,
    )
    slip_out, state_out = call(
        functools.partial(finish_second_kernel, heights),
        [full] * 2,
        shift, scale_mid, rest, slip_rest, numbers, basis_out, *parts,
        grid=(patches // BS,),
        out_specs=[pl.BlockSpec((BS, ens), lambda n: (n, 0))] * 2,
    )
    return (slip_out, state_out)


def solution(mesh):
    in_specs = (
        P(("row", "col"), None),
        P(("row", "col"), None),
        P(("row", "col")),
        P(("row", "col")),
        P(("row", "col")),
        P(("row", "col")),
        P(("row", "col")),
        P(("row", "col")),
        P(None, ("row", "col"), None),
        P(None, ("row", "col")),
        P(None, ("row", "col")),
        P("row", None, "col"),
        P("row", None, "col"),
        P(None, ("row", "col")),
        P(("row", "col")),
        P(None, ("row", "col")),
        P("col", None),
        P("col", None),
    )
    out_specs = (P(("row", "col"), None), P(("row", "col"), None))
    return jax.shard_map(
        per_device, mesh=mesh, in_specs=in_specs, out_specs=out_specs, check_vma=False
    )
```

```python
import functools

import jax
import jax.numpy as jnp
from jax import lax
from jax.experimental import pallas as pl
from jax.experimental.pallas import tpu as pltpu
from jax.sharding import PartitionSpec as P

BS = 256
R = 32

STEP_SIZE = 0.5
REF_FRICTION = 0.6
LIMIT = 16 * 1024 * 1024
F32 = jnp.float32
BF16 = jnp.bfloat16


def dot(a, b):
    return jnp.dot(a, b, preferred_element_type=F32)


def dot_t(a, b):
    return lax.dot_general(a, b, (((0,), (0,)), ((), ())), preferred_element_type=F32)


VMEM = pl.BlockSpec(memory_space=pltpu.VMEM)


def call(kernel, outs, *operands, specs=None, **grid):
    return pl.pallas_call(
        kernel,
        in_specs=specs or [VMEM] * len(operands),
        out_shape=outs,
        compiler_params=pltpu.CompilerParams(vmem_limit_bytes=LIMIT),
        **grid,
    )(*operands)


def rows_at(n, size):
    return pl.ds(pl.multiple_of(n * size, size), size)


HBM = pl.BlockSpec(memory_space=pl.ANY)


def in_hbm(*arrays):
    return [pltpu.with_memory_space_constraint(array, pltpu.HBM) for array in arrays]


def start_copies(pairs, sems, first=0):
    copies = [pltpu.make_async_copy(a, b, sems.at[first + k]) for k, (a, b) in enumerate(pairs)]
    for copy in copies:
        copy.start()
    return copies


def project_kernel(slip_hbm, basis_hbm, coeff_ref, rounded_ref, first_ref, last_ref, slip_ref, basis_ref, sems):
    count = slip_ref.shape[0] // BS
    blocks = [pl.ds(n * BS, BS) for n in range(count)]
    copies = start_copies(
        [(basis_hbm, basis_ref)] + [(slip_hbm.at[at, :], slip_ref.at[at, :]) for at in blocks], sems
    )
    copies[0].wait()
    for n, at in enumerate(blocks):
        copies[1 + n].wait()
        rounded = slip_ref[at, :].astype(BF16)
        rounded_ref[at, :] = rounded
        if n == 0:
            first_ref[...] = rounded
        if n == count - 1:
            last_ref[...] = rounded
        coeff_ref[n * R : (n + 1) * R, :] = dot(basis_ref[:, at], rounded).astype(BF16)


def project(slip, basis_in):
    patches, ens = slip.shape
    count = patches // BS
    edge = jax.ShapeDtypeStruct((BS, ens), BF16)
    return call(
        project_kernel,
        [
            jax.ShapeDtypeStruct((count * R, ens), BF16),
            jax.ShapeDtypeStruct((patches, ens), BF16),
            edge,
            edge,
            jax.ShapeDtypeStruct((patches, ens), F32),
        ],
        *in_hbm(slip, basis_in),
        specs=[HBM] * 2,
        scratch_shapes=[pltpu.VMEM(basis_in.shape, BF16), pltpu.SemaphoreType.DMA((1 + count,))],
    )


def ranks_kernel(
    col_count, rank_hbm, now_hbm, rate_hbm, wide_ref, joined_ref, rank_ref, sems
):
    sources, share, blocks = rank_ref.shape
    ens = now_hbm.shape[1]
    copies = start_copies(
        [
            (rank_hbm, rank_ref),
            (now_hbm, joined_ref.at[:, pl.ds(0, ens)]),
            (rate_hbm, joined_ref.at[:, pl.ds(ens, ens)]),
        ],
        sems,
    )
    width = share * R
    column = lax.broadcasted_iota(jnp.int32, (share, width), 1)
    spread = (lax.div(column, R) == lax.broadcasted_iota(jnp.int32, (share, width), 0)).astype(F32).astype(BF16)
    level = lax.rem(lax.broadcasted_iota(jnp.int32, (blocks, width), 1), R).astype(F32)
    receiver = lax.axis_index("row") * blocks + lax.broadcasted_iota(jnp.int32, (share, blocks), 1)
    copies[0].wait()
    for source in range(sources):
        own = (source * col_count + lax.axis_index("col")) * share + lax.broadcasted_iota(jnp.int32, (share, blocks), 0)
        rank = jnp.where(jnp.abs(receiver - own) > 1, rank_ref[source], 0).astype(F32)
        wide = dot_t(rank.astype(BF16), spread)
        wide_ref[source] = jnp.where(level < wide, wide, 0.0)
    copies[1].wait()
    copies[2].wait()


def side_by_side_kernel(*refs):
    pieces, out_ref = refs[:-1], refs[-1]
    size = pieces[0].shape[0]
    for k, piece in enumerate(pieces):
        out_ref[k * size : (k + 1) * size, :] = piece[...]


def weights_first_kernel(heights, size, *refs):
    sources, after_ref, numbers_ref, matrix_ref = refs[:9], refs[9], refs[10], refs[11]
    vectors, lists, wide, sems = refs[12], refs[13:16], refs[16], refs[17]
    targets = [vectors.at[k] for k in range(6)] + list(lists)
    for copy in start_copies(list(zip(sources, targets)), sems):
        copy.wait()
    fill_weights(heights, size, 0, 0, vectors, lists, numbers_ref, matrix_ref, wide)


def weights_second_kernel(heights, size, *refs):
    sources, near_hbm, state_hbm, low_numbers_ref, after_ref = refs[:9], *refs[9:13]
    numbers_ref, matrix_ref, near_ref, state_ref = refs[13:17]
    vectors, lists, wide, sems = refs[17], refs[18:21], refs[21], refs[22]
    targets = [vectors.at[k] for k in range(6)] + list(lists)
    copies = start_copies(list(zip(sources, targets)), sems)
    large = start_copies([(near_hbm, near_ref), (state_hbm, state_ref)], sems, len(targets))
    half = low_numbers_ref.shape[0]
    numbers_ref[:half, :] = low_numbers_ref[...]
    for copy in copies:
        copy.wait()
    fill_weights(heights, size, half, half, vectors, lists, numbers_ref, matrix_ref, wide)
    for copy in large:
        copy.wait()


def fill_weights(heights, size, start, numbers_start, vectors, lists, numbers_ref, matrix_ref, wide):
    count_ref, bricks_ref, weight_ref = lists
    slots = bricks_ref.shape[0]
    col = lax.axis_index("col")
    height, core = lax.div(col, 2).astype(F32), lax.rem(col, 2).astype(F32)
    lanes = 128
    column = lax.div(lax.broadcasted_iota(jnp.int32, (3 * slots, 3 * slots * lanes), 1), lanes)
    line = lax.broadcasted_iota(jnp.int32, (3 * slots, 3 * slots * lanes), 0)
    spread = (column == line).astype(F32).astype(BF16)

    @pl.loop(0, matrix_ref.shape[0] // BS)
    def _(n):
        at = pl.ds(pl.multiple_of(start + n * BS, BS), BS)
        load, normal, direct, evolution, distance, stiffness = (vectors[k, :, at] for k in range(6))
        rows = [load, normal, 1.0 / direct, 1.0 / evolution, evolution / distance, stiffness, load, normal]
        numbers_at = pl.ds(pl.multiple_of(numbers_start + n * BS, BS), BS)
        numbers_ref[numbers_at, :] = jnp.concatenate(rows, axis=0).T
        bricks = bricks_ref[:, at].astype(F32)
        live = lax.broadcasted_iota(jnp.int32, (slots, BS), 0) < count_ref[:, at]
        weights = jnp.where(live, weight_ref[:, at], 0.0)
        merged = jnp.zeros((slots, BS), F32)
        for k in range(slots):
            merged = merged + jnp.where(bricks == bricks[k : k + 1], weights[k : k + 1], 0.0)
        shares = merged / jnp.sum(weights, axis=0, keepdims=True)
        owner = jnp.floor((bricks + 0.5) * (1.0 / size))
        chip = jnp.floor(owner * 0.5 + 0.25)
        away = height - chip
        away = jnp.where(away < 0, away + heights, away)
        other = jnp.where(owner - 2.0 * chip == core, 0.0, float(heights))
        place = jnp.where(live, (other + away - owner) * size + bricks, -1.0)
        high = jnp.floor((place + 0.5) * (1.0 / lanes))
        columns = jnp.concatenate([high, place - high * lanes, shares], axis=0).astype(BF16)
        wide[...] = dot_t(columns, spread).astype(BF16)
        group = 16

        @pl.loop(0, BS // group, unroll=2)
        def _(m):
            part = rows_at(m, group)
            to = pl.ds(pl.multiple_of(n * BS + m * group, group), group)
            column_of = lambda k: wide[part, k * lanes : (k + 1) * lanes]
            lane = lax.broadcasted_iota(jnp.int32, (group, lanes), 1).astype(F32).astype(BF16)
            none = jnp.full((group, lanes), -1.0, BF16)
            highs = [jnp.where(column_of(slots + k) == lane, column_of(k), none) for k in range(slots)]
            values = [column_of(2 * slots + k) for k in range(slots)]
            for piece in range(matrix_ref.shape[1] // lanes):
                here = jnp.full((group, lanes), float(piece), BF16)
                tile = jnp.zeros((group, lanes), BF16)
                for k in range(slots):
                    tile = jnp.where(highs[k] == here, values[k], tile)
                matrix_ref[to, piece * lanes : (piece + 1) * lanes] = tile


def couple_kernel(sources, heights, flip, matrix_ref, *refs):
    coeffs, out_ref = refs[:sources], refs[sources]
    share = coeffs[0].shape[0]
    row, col = lax.axis_index("row"), lax.axis_index("col")
    height, core = lax.div(col, 2), lax.rem(col + flip, 2)

    @pl.loop(0, heights)
    def _(d):
        at = rows_at(2 * lax.rem(height + d, heights) + core, share)
        total = None
        for step in range(sources):
            term = dot(matrix_ref[lax.rem(row + (sources - step), sources), at, :], coeffs[step][...])
            total = term if total is None else total + term
        out_ref[rows_at(d, share), :] = total.astype(out_ref.dtype)


def couple(flip, matrix, coeffs, heights, kind):
    share, ens = coeffs[0].shape
    return call(
        functools.partial(couple_kernel, len(coeffs), heights, flip),
        jax.ShapeDtypeStruct((heights * share, ens), kind),
        matrix,
        *coeffs,
    )


def chip_sum_kernel(kept_ref, sent_ref, *outs):
    share = outs[0].shape[0]
    for d, out_ref in enumerate(outs):

        @pl.loop(0, share // 32)
        def _(n):
            at = pl.ds(pl.multiple_of(d * share + n * 32, 32), 32)
            out_ref[rows_at(n, 32), :] = (kept_ref[at, :] + sent_ref[at, :].astype(F32)).astype(BF16)


def chip_sum(kept, sent, heights):
    rows, ens = kept.shape
    return list(call(chip_sum_kernel, [jax.ShapeDtypeStruct((rows // heights, ens), BF16)] * heights, kept, sent))


def near_tau(n, slip, numbers, near_ref, rounded_ref):
    count = rounded_ref.shape[0] // BS
    at = rows_at(n, BS)
    none = jnp.zeros((BS, rounded_ref.shape[1]), BF16)
    before = jnp.where(n == 0, none, rounded_ref[rows_at(jnp.maximum(n - 1, 0), BS), :])
    after = jnp.where(n == count - 1, none, rounded_ref[rows_at(jnp.minimum(n + 1, count - 1), BS), :])
    near = dot(near_ref[0, at, :], before) + dot(near_ref[1, at, :], rounded_ref[at, :]) + dot(near_ref[2, at, :], after)
    return numbers[:, 0:1] - numbers[:, 5:6] * slip - near


def prepare_first_kernel(
    low_ref, high_ref, own_ref, other_ref, slip_ref, state_ref, numbers_ref, near_ref, rounded_ref,
    shift_ref, scale_ref, rest_ref, scale_mid_ref,
):
    half = own_ref.shape[0]
    ens = slip_ref.shape[1]
    blocks = low_ref.shape[0] // BS

    def block(matrix_ref, m, n):
        at, own_at = rows_at(n, BS), rows_at(m, BS)
        total = dot(matrix_ref[own_at, :half], own_ref[...]) + dot(matrix_ref[own_at, half:], other_ref[...])
        numbers = numbers_ref[at, :]
        normal, inv_direct, inv_evolution, ratio = (numbers[:, k : k + 1] for k in range(1, 5))
        base = total[:, :ens]
        scale = inv_direct / (normal - base)
        scale_ref[at, :] = scale
        scale_mid_ref[at, :] = inv_direct / (normal - (base + STEP_SIZE * total[:, ens:]))
        state = state_ref[at, :]
        tau = near_tau(n, slip_ref[at, :], numbers, near_ref, rounded_ref)
        shift_ref[at, :] = tau * scale - state * inv_direct
        rest_ref[at, :] = state + (STEP_SIZE * ratio) * jnp.exp((REF_FRICTION - state) * inv_evolution)

    @pl.loop(0, blocks)
    def _(m):
        block(low_ref, m, m)

    @pl.loop(0, blocks)
    def _(m):
        block(high_ref, m, blocks + m)


def far_speed(n, shift_ref, scale_ref, basis_ref, near_ref, before_ref, after_ref, parts, outer):
    at = rows_at(n, BS)
    levels = rows_at(n, R)
    far = parts[0][levels, :].astype(F32)
    for part in parts[1:]:
        far = far + part[levels, :].astype(F32)
    outer[...] = dot_t(basis_ref[:, at], far.astype(BF16))

    @pl.when(n == 0)
    def _():
        outer[...] += dot(near_ref[0, at, :], before_ref[...])

    @pl.when(n == near_ref.shape[1] // BS - 1)
    def _():
        outer[...] += dot(near_ref[2, at, :], after_ref[...])

    return jnp.exp(shift_ref[at, :] - scale_ref[at, :] * outer[...])


def finish_first_kernel(
    heights, shift_ref, scale_ref, rest_ref, slip_ref, numbers_ref, basis_out_ref, basis_in_ref, near_ref, *refs
):
    parts, before_ref, after_ref = refs[:heights], refs[heights], refs[heights + 1]
    slip_mid_ref, state_mid_ref, rounded_ref, coeff_ref, first_ref, last_ref, outer = refs[heights + 2 :]

    @pl.loop(0, slip_ref.shape[0] // BS)
    def _(n):
        at = rows_at(n, BS)
        speed = far_speed(
            n, shift_ref, scale_ref, basis_out_ref, near_ref, before_ref, after_ref, parts, outer
        )
        slip_mid = slip_ref[at, :] + STEP_SIZE * speed
        slip_mid_ref[at, :] = slip_mid
        state_mid_ref[at, :] = rest_ref[at, :] - (STEP_SIZE * numbers_ref[at, 4:5]) * speed
        rounded = slip_mid.astype(BF16)
        rounded_ref[at, :] = rounded
        coeff_ref[rows_at(n, R), :] = dot(basis_in_ref[:, at], rounded).astype(BF16)

    first_ref[...] = rounded_ref[:BS]
    last_ref[...] = rounded_ref[-BS:]


def prepare_second_kernel(
    slip_ref, state_ref, slip_mid_ref, state_mid_ref, scale_ref, numbers_ref, near_ref, rounded_ref,
    shift_ref, slip_rest_ref, rest_ref,
):
    @pl.loop(0, slip_ref.shape[0] // BS)
    def _(n):
        at = rows_at(n, BS)
        numbers = numbers_ref[at, :]
        inv_direct, inv_evolution, ratio = (numbers[:, k : k + 1] for k in range(2, 5))
        slip = slip_mid_ref[at, :]
        state = state_mid_ref[at, :]
        tau = near_tau(n, slip, numbers, near_ref, rounded_ref)
        shift_ref[at, :] = tau * scale_ref[at, :] - state * inv_direct
        slip_rest_ref[at, :] = 0.5 * (slip_ref[at, :] + slip)
        friction = jnp.exp((REF_FRICTION - state) * inv_evolution)
        rest_ref[at, :] = 0.5 * (state_ref[at, :] + state) + (0.5 * STEP_SIZE * ratio) * friction


def finish_second_kernel(
    heights, shift_ref, scale_ref, rest_ref, slip_rest_ref, numbers_ref, basis_out_ref, near_ref, *refs
):
    parts, before_ref, after_ref = refs[:heights], refs[heights], refs[heights + 1]
    slip_out_ref, state_out_ref, outer = refs[heights + 2 :]
    n = pl.program_id(0)
    at = rows_at(n, BS)
    speed = far_speed(n, shift_ref, scale_ref, basis_out_ref, near_ref, before_ref, after_ref, parts, outer)
    slip_out_ref[...] = slip_rest_ref[at, :] + (0.5 * STEP_SIZE) * speed
    state_out_ref[...] = rest_ref[at, :] - (0.5 * STEP_SIZE * numbers_ref[at, 4:5]) * speed


def masked_coupling(coupling, wide):
    rows, sources, width = coupling.shape
    blocks = rows // R
    keep = jnp.arange(R, dtype=jnp.int32).astype(F32)[None, None, :, None] < wide[:, :, None, :]
    matrix = jnp.transpose(coupling, (1, 0, 2)).reshape(sources, blocks, R, width)
    masked = jnp.where(keep, matrix, jnp.zeros((), BF16)).reshape(sources, rows, width)
    return pltpu.with_memory_space_constraint(masked, pltpu.VMEM)


def per_device(
    slip,
    state,
    tau_load,
    normal_stress,
    direct_effect,
    evolution_effect,
    slip_distance,
    self_stiffness,
    near_blocks,
    basis_in,
    basis_out,
    coupling,
    block_rank,
    adj_bricks,
    adj_count,
    adj_weight,
    pressure_now,
    pressure_rate,
):
    row_count = lax.axis_size("row")
    col_count = lax.axis_size("col")
    row_index = lax.axis_index("row")
    col_index = lax.axis_index("col")
    heights = col_count // 2
    height, core = col_index // 2, col_index % 2
    both = ("row", "col")
    devices = row_count * col_count

    def to_row(array, d):
        return lax.ppermute(array, "row", [(i, (i + d) % row_count) for i in range(row_count)])

    def to_height(array, d):
        pairs = [(2 * z + k, 2 * ((z + d) % heights) + k) for z in range(heights) for k in range(2)]
        return lax.ppermute(array, "col", pairs)

    def to_core(array):
        return lax.ppermute(array, "col", [(2 * z + k, 2 * z + 1 - k) for z in range(heights) for k in range(2)])

    def halo(first, last):
        up = [(i, i + 1) for i in range(devices - 1)]
        down = [(j, i) for i, j in up]
        return lax.ppermute(last, both, up), lax.ppermute(first, both, down)

    patches, ens = slip.shape
    slots = adj_bricks.shape[0]
    size = pressure_now.shape[0]
    share = coupling.shape[2]
    def far_parts(coeffs, first, last):
        sent = to_core(couple(1, masked, coeffs, heights, BF16))
        kept = couple(0, masked, coeffs, heights, F32)
        pieces = chip_sum(kept, sent, heights)
        pieces, first, last = lax.optimization_barrier((pieces, first, last))
        parts = pieces[:1] + [to_height(pieces[d], d) for d in range(1, heights)]
        return parts, *halo(first, last)

    def row_coeffs(coeff):
        return [coeff] + [to_row(coeff, d) for d in range(1, row_count)]

    full = jax.ShapeDtypeStruct((patches, ens), F32)
    half = jax.ShapeDtypeStruct((patches, ens), BF16)
    edge = jax.ShapeDtypeStruct((BS, ens), BF16)
    per_patch = [tau_load, normal_stress, direct_effect, evolution_effect, slip_distance, self_stiffness]

    ranks = jnp.transpose(block_rank, (1, 2, 0))
    wide, joined = call(
        functools.partial(ranks_kernel, col_count),
        [
            jax.ShapeDtypeStruct((ranks.shape[0], ranks.shape[2], share), F32),
            jax.ShapeDtypeStruct((size, 2 * ens), BF16),
        ],
        *in_hbm(ranks, pressure_now, pressure_rate),
        specs=[HBM] * 3,
        scratch_shapes=[pltpu.VMEM(ranks.shape, jnp.int32), pltpu.SemaphoreType.DMA((3,))],
    )
    own = call(
        side_by_side_kernel,
        jax.ShapeDtypeStruct((heights * size, 2 * ens), BF16),
        joined,
        *[to_height(joined, d) for d in range(1, heights)],
    )
    other = to_core(own)
    masked = masked_coupling(coupling, wide)
    masked, slip = lax.optimization_barrier((masked, slip))
    coeff, rounded, first, last, slip = project(slip, basis_in)
    coeffs = row_coeffs(coeff)
    brick_lists = [adj_count[None], adj_bricks, adj_weight]
    part = jax.ShapeDtypeStruct((patches // 2, 2 * heights * size), BF16)
    per_patch_lists = [array[None] for array in per_patch] + brick_lists
    list_scratch = [
        pltpu.VMEM((6, 1, patches), F32),
        pltpu.VMEM((1, patches), jnp.int32),
        pltpu.VMEM(adj_bricks.shape, jnp.int32),
        pltpu.VMEM(adj_weight.shape, F32),
        pltpu.VMEM((BS, 3 * slots * 128), BF16),
    ]
    numbers, low = call(
        functools.partial(weights_first_kernel, heights, size),
        [jax.ShapeDtypeStruct((patches // 2, 8), F32), part],
        *in_hbm(*per_patch_lists),
        coeff,
        specs=[HBM] * 9 + [VMEM],
        scratch_shapes=list_scratch + [pltpu.SemaphoreType.DMA((9,))],
    )
    coeffs, low = lax.optimization_barrier((coeffs, low))
    parts, before, after = far_parts(coeffs, first, last)
    numbers, high, near, state = call(
        functools.partial(weights_second_kernel, heights, size),
        [
            jax.ShapeDtypeStruct((patches, 8), F32),
            part,
            jax.ShapeDtypeStruct(near_blocks.shape, BF16),
            full,
        ],
        *in_hbm(*per_patch_lists, near_blocks, state),
        numbers,
        parts[0],
        specs=[HBM] * 11 + [VMEM] * 2,
        scratch_shapes=list_scratch + [pltpu.SemaphoreType.DMA((11,))],
    )
    shift, scale, rest, scale_mid = call(
        prepare_first_kernel, [full] * 4, low, high, own, other, slip, state, numbers, near, rounded
    )
    slip_mid, state_mid, rounded, coeff, first, last = call(
        functools.partial(finish_first_kernel, heights),
        [full, full, half, jax.ShapeDtypeStruct((patches // BS * R, ens), BF16), edge, edge],
        shift, scale, rest, slip, numbers, basis_out, basis_in, near, *parts, before, after,
        scratch_shapes=[pltpu.VMEM((BS, ens), F32)],
    )
    coeffs = row_coeffs(coeff)
    parts, before, after = far_parts(coeffs, first, last)
    shift, slip_rest, rest = call(
        prepare_second_kernel, [full] * 3,
        slip, state, slip_mid, state_mid, scale_mid, numbers, near, rounded,
    )
    slip_out, state_out = call(
        functools.partial(finish_second_kernel, heights),
        [full] * 2,
        shift, scale_mid, rest, slip_rest, numbers, basis_out, near, *parts, before, after,
        grid=(patches // BS,),
        out_specs=[pl.BlockSpec((BS, ens), lambda n: (n, 0))] * 2,
        scratch_shapes=[pltpu.VMEM((BS, ens), F32)],
    )
    return (slip_out, state_out)


def solution(mesh):
    in_specs = (
        P(("row", "col"), None),
        P(("row", "col"), None),
        P(("row", "col")),
        P(("row", "col")),
        P(("row", "col")),
        P(("row", "col")),
        P(("row", "col")),
        P(("row", "col")),
        P(None, ("row", "col"), None),
        P(None, ("row", "col")),
        P(None, ("row", "col")),
        P("row", None, "col"),
        P("row", None, "col"),
        P(None, ("row", "col")),
        P(("row", "col")),
        P(None, ("row", "col")),
        P("col", None),
        P("col", None),
    )
    out_specs = (P(("row", "col"), None), P(("row", "col"), None))
    return jax.shard_map(
        per_device, mesh=mesh, in_specs=in_specs, out_specs=out_specs, check_vma=False
    )
```

```python
import functools

import jax
import jax.numpy as jnp
from jax import lax
from jax.experimental import pallas as pl
from jax.experimental.pallas import tpu as pltpu
from jax.sharding import PartitionSpec as P

BS = 256
R = 32

STEP_SIZE = 0.5
REF_FRICTION = 0.6
LIMIT = 16 * 1024 * 1024
F32 = jnp.float32
BF16 = jnp.bfloat16


def dot(a, b):
    return jnp.dot(a, b, preferred_element_type=F32)


def dot_t(a, b):
    return lax.dot_general(a, b, (((0,), (0,)), ((), ())), preferred_element_type=F32)


VMEM = pl.BlockSpec(memory_space=pltpu.VMEM)


def call(kernel, outs, *operands, specs=None, **grid):
    return pl.pallas_call(
        kernel,
        in_specs=specs or [VMEM] * len(operands),
        out_shape=outs,
        compiler_params=pltpu.CompilerParams(vmem_limit_bytes=LIMIT),
        **grid,
    )(*operands)


def rows_at(n, size):
    return pl.ds(pl.multiple_of(n * size, size), size)


HBM = pl.BlockSpec(memory_space=pl.ANY)


def in_hbm(*arrays):
    return [pltpu.with_memory_space_constraint(array, pltpu.HBM) for array in arrays]


def start_copies(pairs, sems, first=0):
    copies = [pltpu.make_async_copy(a, b, sems.at[first + k]) for k, (a, b) in enumerate(pairs)]
    for copy in copies:
        copy.start()
    return copies


def fill_edges(rounded_ref, pair_ref, cross_ref):
    even = lax.rem(lax.axis_index("col"), 2) == 0
    first, last = rounded_ref[:BS], rounded_ref[-BS:]
    pair_ref[...] = jnp.where(even, last, first)
    cross_ref[...] = jnp.where(even, first, last)


def project_kernel(slip_hbm, basis_hbm, coeff_ref, rounded_ref, pair_ref, cross_ref, slip_ref, basis_ref, sems):
    count = slip_ref.shape[0] // BS
    blocks = [pl.ds(n * BS, BS) for n in range(count)]
    copies = start_copies(
        [(basis_hbm, basis_ref)] + [(slip_hbm.at[at, :], slip_ref.at[at, :]) for at in blocks], sems
    )
    copies[0].wait()
    for n, at in enumerate(blocks):
        copies[1 + n].wait()
        rounded = slip_ref[at, :].astype(BF16)
        rounded_ref[at, :] = rounded
        coeff_ref[n * R : (n + 1) * R, :] = dot(basis_ref[:, at], rounded).astype(BF16)
    fill_edges(rounded_ref, pair_ref, cross_ref)


def project(slip, basis_in):
    patches, ens = slip.shape
    count = patches // BS
    edge = jax.ShapeDtypeStruct((BS, ens), BF16)
    return call(
        project_kernel,
        [
            jax.ShapeDtypeStruct((count * R, ens), BF16),
            jax.ShapeDtypeStruct((patches, ens), BF16),
            edge,
            edge,
            jax.ShapeDtypeStruct((patches, ens), F32),
        ],
        *in_hbm(slip, basis_in),
        specs=[HBM] * 2,
        scratch_shapes=[pltpu.VMEM(basis_in.shape, BF16), pltpu.SemaphoreType.DMA((1 + count,))],
    )


def ranks_kernel(
    col_count, rank_hbm, now_hbm, rate_hbm, wide_ref, joined_ref, rank_ref, sems
):
    sources, share, blocks = rank_ref.shape
    ens = now_hbm.shape[1]
    copies = start_copies(
        [
            (rank_hbm, rank_ref),
            (now_hbm, joined_ref.at[:, pl.ds(0, ens)]),
            (rate_hbm, joined_ref.at[:, pl.ds(ens, ens)]),
        ],
        sems,
    )
    width = share * R
    column = lax.broadcasted_iota(jnp.int32, (share, width), 1)
    spread = (lax.div(column, R) == lax.broadcasted_iota(jnp.int32, (share, width), 0)).astype(F32).astype(BF16)
    level = lax.rem(lax.broadcasted_iota(jnp.int32, (blocks, width), 1), R).astype(F32)
    receiver = lax.axis_index("row") * blocks + lax.broadcasted_iota(jnp.int32, (share, blocks), 1)
    copies[0].wait()
    for source in range(sources):
        own = (source * col_count + lax.axis_index("col")) * share + lax.broadcasted_iota(jnp.int32, (share, blocks), 0)
        rank = jnp.where(jnp.abs(receiver - own) > 1, rank_ref[source], 0).astype(F32)
        wide = dot_t(rank.astype(BF16), spread)
        wide_ref[source] = jnp.where(level < wide, wide, 0.0)
    copies[1].wait()
    copies[2].wait()


def side_by_side_kernel(*refs):
    pieces, out_ref = refs[:-1], refs[-1]
    size = pieces[0].shape[0]
    for k, piece in enumerate(pieces):
        out_ref[k * size : (k + 1) * size, :] = piece[...]


def weights_kernel(heights, size, start, *refs):
    begun = start > 0
    sources, rest = refs[:9], refs[9:]
    near_hbm, state_hbm, begun_ref = rest[:3] if begun else (None, None, None)
    rest = rest[4:] if begun else rest[1:]
    numbers_ref, matrix_ref = rest[:2]
    near_ref, state_ref = rest[2:4] if begun else (None, None)
    vectors, lists, sems = rest[-5], rest[-4:-1], rest[-1]
    targets = [vectors.at[k] for k in range(6)] + list(lists)
    copies = start_copies(list(zip(sources, targets)), sems)
    large = [(near_hbm, near_ref), (state_hbm, state_ref)] if begun else []
    large = start_copies(large, sems, len(targets))
    if begun:
        numbers_ref[:start, :] = begun_ref[...]
    count_ref, bricks_ref, weight_ref = lists
    slots = bricks_ref.shape[0]
    col = lax.axis_index("col")
    height, core = lax.div(col, 2).astype(F32), lax.rem(col, 2).astype(F32)
    group, lanes, unrolled = 16, 128, 8
    for copy in copies:
        copy.wait()

    @pl.loop(0, matrix_ref.shape[1] // lanes)
    def _(n):
        own_at = rows_at(n, lanes)
        at = pl.ds(pl.multiple_of(start + n * lanes, lanes), lanes)
        load, normal, direct, evolution, distance, stiffness = (vectors[k, :, at] for k in range(6))
        rows = [load, normal, 1.0 / direct, 1.0 / evolution, evolution / distance, stiffness, load, normal]
        numbers_ref[at if begun else own_at, :] = jnp.concatenate(rows, axis=0).T
        bricks = bricks_ref[:, at].astype(F32)
        live = lax.broadcasted_iota(jnp.int32, (slots, lanes), 0) < count_ref[:, at]
        weights = jnp.where(live, weight_ref[:, at], 0.0)
        merged = jnp.zeros((slots, lanes), F32)
        for k in range(slots):
            merged = merged + jnp.where(bricks == bricks[k : k + 1], weights[k : k + 1], 0.0)
        shares = merged / jnp.sum(weights, axis=0, keepdims=True)
        owner = jnp.floor((bricks + 0.5) * (1.0 / size))
        chip = jnp.floor(owner * 0.5 + 0.25)
        away = height - chip
        away = jnp.where(away < 0, away + heights, away)
        other = jnp.where(owner - 2.0 * chip == core, 0.0, float(heights))
        place = jnp.where(live, (other + away - owner) * size + bricks, -1.0)
        high = jnp.floor((place + 0.5) * (1.0 / group))
        low = place - high * group
        spread = lambda rows, k: jnp.broadcast_to(rows[k : k + 1], (group, lanes)).astype(BF16)
        line = lax.broadcasted_iota(jnp.int32, (group, lanes), 0).astype(F32).astype(BF16)
        none = jnp.full((group, lanes), -1.0, BF16)
        highs = [jnp.where(spread(low, k) == line, spread(high, k), none) for k in range(slots)]
        values = [spread(shares, k) for k in range(slots)]

        @pl.loop(0, matrix_ref.shape[0] // (group * unrolled))
        def _(m):
            first = jnp.full((group, lanes), (m * unrolled).astype(F32)).astype(BF16)
            for step in range(unrolled):
                here = first + jnp.asarray(step, BF16)
                tile = jnp.zeros((group, lanes), BF16)
                for k in range(slots):
                    tile = jnp.where(highs[k] == here, values[k], tile)
                to = pl.ds(pl.multiple_of((m * unrolled + step) * group, group), group)
                matrix_ref[to, own_at] = tile

    for copy in large:
        copy.wait()


def couple_kernel(sources, heights, flip, matrix_ref, *refs):
    coeffs, edges, out_ref = refs[:sources], refs[sources:-1], refs[-1]
    share = coeffs[0].shape[0]
    row, col = lax.axis_index("row"), lax.axis_index("col")
    height, core = lax.div(col, 2), lax.rem(col + flip, 2)

    @pl.loop(0, heights)
    def _(d):
        at = rows_at(2 * lax.rem(height + d, heights) + core, share)
        total = None
        for step in range(sources):
            term = dot(matrix_ref[lax.rem(row + (sources - step), sources), at, :], coeffs[step][...])
            total = term if total is None else total + term
        out_ref[rows_at(d, share), :] = total.astype(out_ref.dtype)

    for edge in edges:
        out_ref[heights * share :, :] = edge[...]


def couple(flip, matrix, coeffs, heights, kind, *edges):
    share, ens = coeffs[0].shape
    return call(
        functools.partial(couple_kernel, len(coeffs), heights, flip),
        jax.ShapeDtypeStruct((heights * share + len(edges) * BS, ens), kind),
        matrix,
        *coeffs,
        *edges,
    )


def chip_sum_kernel(kept_ref, sent_ref, *outs):
    share = outs[0].shape[0]
    for d, out_ref in enumerate(outs):

        @pl.loop(0, share // 32)
        def _(n):
            at = pl.ds(pl.multiple_of(d * share + n * 32, 32), 32)
            out_ref[rows_at(n, 32), :] = (kept_ref[at, :] + sent_ref[at, :].astype(F32)).astype(BF16)


def chip_sum(kept, sent, heights):
    rows, ens = kept.shape
    return list(call(chip_sum_kernel, [jax.ShapeDtypeStruct((rows // heights, ens), BF16)] * heights, kept, sent))


def near_tau(n, slip, numbers, near_ref, rounded_ref):
    count = rounded_ref.shape[0] // BS
    at = rows_at(n, BS)
    none = jnp.zeros((BS, rounded_ref.shape[1]), BF16)
    before = jnp.where(n == 0, none, rounded_ref[rows_at(jnp.maximum(n - 1, 0), BS), :])
    after = jnp.where(n == count - 1, none, rounded_ref[rows_at(jnp.minimum(n + 1, count - 1), BS), :])
    near = dot(near_ref[0, at, :], before) + dot(near_ref[1, at, :], rounded_ref[at, :]) + dot(near_ref[2, at, :], after)
    return numbers[:, 0:1] - numbers[:, 5:6] * slip - near


def prepare_first_kernel(
    low_ref, high_ref, own_ref, other_ref, slip_ref, state_ref, numbers_ref, near_ref, rounded_ref,
    shift_ref, scale_ref, rest_ref, scale_mid_ref,
):
    half = own_ref.shape[0]
    ens = slip_ref.shape[1]
    blocks = low_ref.shape[1] // BS

    def block(matrix_ref, m, n):
        at, own_at = rows_at(n, BS), rows_at(m, BS)
        total = dot_t(matrix_ref[:half, own_at], own_ref[...]) + dot_t(matrix_ref[half:, own_at], other_ref[...])
        numbers = numbers_ref[at, :]
        normal, inv_direct, inv_evolution, ratio = (numbers[:, k : k + 1] for k in range(1, 5))
        base = total[:, :ens]
        scale = inv_direct / (normal - base)
        scale_ref[at, :] = scale
        scale_mid_ref[at, :] = inv_direct / (normal - (base + STEP_SIZE * total[:, ens:]))
        state = state_ref[at, :]
        tau = near_tau(n, slip_ref[at, :], numbers, near_ref, rounded_ref)
        shift_ref[at, :] = tau * scale - state * inv_direct
        rest_ref[at, :] = state + (STEP_SIZE * ratio) * jnp.exp((REF_FRICTION - state) * inv_evolution)

    @pl.loop(0, blocks)
    def _(m):
        block(low_ref, m, m)

    @pl.loop(0, blocks)
    def _(m):
        block(high_ref, m, blocks + m)


def over_blocks(block, basis_ref, near_ref, parts, pair_ref, cross_ref):
    count = near_ref.shape[1] // BS

    def far(n):
        levels = rows_at(n, R)
        total = parts[0][levels, :].astype(F32)
        for part in parts[1:]:
            total = total + part[levels, :].astype(F32)
        return dot_t(basis_ref[:, rows_at(n, BS)], total.astype(BF16))

    even = lax.rem(lax.axis_index("col"), 2) == 0
    pair, cross = pair_ref[-BS:], cross_ref[...]
    block(0, far(0) + dot(near_ref[0, :BS, :], jnp.where(even, cross, pair)))

    @pl.loop(1, count - 1, unroll=2)
    def _(n):
        block(n, far(n))

    block(count - 1, far(count - 1) + dot(near_ref[2, -BS:, :], jnp.where(even, pair, cross)))


def finish_first_kernel(
    heights, shift_ref, scale_ref, rest_ref, slip_ref, numbers_ref, basis_out_ref, basis_in_ref, near_ref, *refs
):
    parts, pair_ref, cross_ref = refs[:heights], refs[heights], refs[heights + 1]
    slip_mid_ref, state_mid_ref, rounded_ref, coeff_ref, pair_out, cross_out = refs[heights + 2 :]

    def block(n, outer):
        at = rows_at(n, BS)
        speed = jnp.exp(shift_ref[at, :] - scale_ref[at, :] * outer)
        slip_mid = slip_ref[at, :] + STEP_SIZE * speed
        slip_mid_ref[at, :] = slip_mid
        state_mid_ref[at, :] = rest_ref[at, :] - (STEP_SIZE * numbers_ref[at, 4:5]) * speed
        rounded = slip_mid.astype(BF16)
        rounded_ref[at, :] = rounded
        coeff_ref[rows_at(n, R), :] = dot(basis_in_ref[:, at], rounded).astype(BF16)

    over_blocks(block, basis_out_ref, near_ref, parts, pair_ref, cross_ref)
    fill_edges(rounded_ref, pair_out, cross_out)


def prepare_second_kernel(
    slip_ref, state_ref, slip_mid_ref, state_mid_ref, scale_ref, numbers_ref, near_ref, rounded_ref,
    shift_ref, slip_rest_ref, rest_ref,
):
    @pl.loop(0, slip_ref.shape[0] // BS)
    def _(n):
        at = rows_at(n, BS)
        numbers = numbers_ref[at, :]
        inv_direct, inv_evolution, ratio = (numbers[:, k : k + 1] for k in range(2, 5))
        slip = slip_mid_ref[at, :]
        state = state_mid_ref[at, :]
        tau = near_tau(n, slip, numbers, near_ref, rounded_ref)
        shift_ref[at, :] = tau * scale_ref[at, :] - state * inv_direct
        slip_rest_ref[at, :] = 0.5 * (slip_ref[at, :] + slip)
        friction = jnp.exp((REF_FRICTION - state) * inv_evolution)
        rest_ref[at, :] = 0.5 * (state_ref[at, :] + state) + (0.5 * STEP_SIZE * ratio) * friction


def finish_second_kernel(
    heights, shift_ref, scale_ref, rest_ref, slip_rest_ref, numbers_ref, basis_out_ref, near_ref, *refs
):
    parts, pair_ref, cross_ref = refs[:heights], refs[heights], refs[heights + 1]
    slip_hbm, state_hbm, slip_ref, state_ref, sems = refs[heights + 2 :]

    def copies(n):
        at = rows_at(n, BS)
        return [
            pltpu.make_async_copy(slip_ref.at[at, :], slip_hbm.at[at, :], sems.at[0, n]),
            pltpu.make_async_copy(state_ref.at[at, :], state_hbm.at[at, :], sems.at[1, n]),
        ]

    def block(n, outer):
        at = rows_at(n, BS)
        speed = jnp.exp(shift_ref[at, :] - scale_ref[at, :] * outer)
        slip_ref[at, :] = slip_rest_ref[at, :] + (0.5 * STEP_SIZE) * speed
        state_ref[at, :] = rest_ref[at, :] - (0.5 * STEP_SIZE * numbers_ref[at, 4:5]) * speed
        for copy in copies(n):
            copy.start()

    over_blocks(block, basis_out_ref, near_ref, parts, pair_ref, cross_ref)

    @pl.loop(0, slip_ref.shape[0] // BS)
    def _(n):
        for copy in copies(n):
            copy.wait()


def masked_coupling(coupling, wide):
    rows, sources, width = coupling.shape
    blocks = rows // R
    keep = jnp.arange(R, dtype=jnp.int32).astype(F32)[None, None, :, None] < wide[:, :, None, :]
    matrix = jnp.transpose(coupling, (1, 0, 2)).reshape(sources, blocks, R, width)
    masked = jnp.where(keep, matrix, jnp.zeros((), BF16)).reshape(sources, rows, width)
    return pltpu.with_memory_space_constraint(masked, pltpu.VMEM)


def per_device(
    slip,
    state,
    tau_load,
    normal_stress,
    direct_effect,
    evolution_effect,
    slip_distance,
    self_stiffness,
    near_blocks,
    basis_in,
    basis_out,
    coupling,
    block_rank,
    adj_bricks,
    adj_count,
    adj_weight,
    pressure_now,
    pressure_rate,
):
    row_count = lax.axis_size("row")
    col_count = lax.axis_size("col")
    row_index = lax.axis_index("row")
    col_index = lax.axis_index("col")
    heights = col_count // 2
    height, core = col_index // 2, col_index % 2
    both = ("row", "col")
    devices = row_count * col_count

    def to_row(array, d):
        return lax.ppermute(array, "row", [(i, (i + d) % row_count) for i in range(row_count)])

    def to_height(array, d):
        pairs = [(2 * z + k, 2 * ((z + d) % heights) + k) for z in range(heights) for k in range(2)]
        return lax.ppermute(array, "col", pairs)

    def to_core(array):
        return lax.ppermute(array, "col", [(2 * z + k, 2 * z + 1 - k) for z in range(heights) for k in range(2)])

    def to_chip(array):
        ends = [(i, i + 1) for i in range(1, devices - 1, 2)]
        return lax.ppermute(array, both, ends + [(j, i) for i, j in ends])

    patches, ens = slip.shape
    slots = adj_bricks.shape[0]
    size = pressure_now.shape[0]
    share = coupling.shape[2]
    def far_parts(coeffs, pair, cross):
        sent = to_core(couple(1, masked, coeffs, heights, BF16, pair))
        kept = couple(0, masked, coeffs, heights, F32)
        pieces = chip_sum(kept, sent, heights)
        pieces, cross = lax.optimization_barrier((pieces, cross))
        parts = pieces[:1] + [to_height(pieces[d], d) for d in range(1, heights)]
        return parts + [sent, to_chip(cross)]

    def row_coeffs(coeff):
        return [coeff] + [to_row(coeff, d) for d in range(1, row_count)]

    full = jax.ShapeDtypeStruct((patches, ens), F32)
    half = jax.ShapeDtypeStruct((patches, ens), BF16)
    edge = jax.ShapeDtypeStruct((BS, ens), BF16)
    per_patch = [tau_load, normal_stress, direct_effect, evolution_effect, slip_distance, self_stiffness]

    ranks = jnp.transpose(block_rank, (1, 2, 0))
    wide, joined = call(
        functools.partial(ranks_kernel, col_count),
        [
            jax.ShapeDtypeStruct((ranks.shape[0], ranks.shape[2], share), F32),
            jax.ShapeDtypeStruct((size, 2 * ens), BF16),
        ],
        *in_hbm(ranks, pressure_now, pressure_rate),
        specs=[HBM] * 3,
        scratch_shapes=[pltpu.VMEM(ranks.shape, jnp.int32), pltpu.SemaphoreType.DMA((3,))],
    )
    fields = [joined] + [to_height(joined, d) for d in range(1, heights)]
    masked = masked_coupling(coupling, wide)
    masked, slip = lax.optimization_barrier((masked, slip))
    coeff, rounded, pair, cross, slip = project(slip, basis_in)
    coeffs = row_coeffs(coeff)
    brick_lists = [adj_count[None], adj_bricks, adj_weight]
    columns = [array[None] for array in per_patch] + brick_lists
    start = patches // 2
    part = jax.ShapeDtypeStruct((2 * heights * size, start), BF16)
    scratch = [
        pltpu.VMEM((6, 1, patches), F32),
        pltpu.VMEM((1, patches), jnp.int32),
        pltpu.VMEM(adj_bricks.shape, jnp.int32),
        pltpu.VMEM(adj_weight.shape, F32),
        pltpu.SemaphoreType.DMA((11,)),
    ]
    numbers, low = call(
        functools.partial(weights_kernel, heights, size, 0),
        [jax.ShapeDtypeStruct((start, 8), F32), part],
        *in_hbm(*columns),
        coeff,
        specs=[HBM] * 9 + [VMEM],
        scratch_shapes=scratch,
    )
    fields, coeffs, low = lax.optimization_barrier((fields, coeffs, low))
    own = call(
        side_by_side_kernel, jax.ShapeDtypeStruct((heights * size, 2 * ens), BF16), *fields
    )
    other = to_core(own)
    outer = far_parts(coeffs, pair, cross)
    numbers, high, near, state = call(
        functools.partial(weights_kernel, heights, size, start),
        [jax.ShapeDtypeStruct((patches, 8), F32), part, jax.ShapeDtypeStruct(near_blocks.shape, BF16), full],
        *in_hbm(*columns, near_blocks, state),
        numbers,
        outer[0],
        specs=[HBM] * 11 + [VMEM] * 2,
        scratch_shapes=scratch,
    )
    shift, scale, rest, scale_mid = call(
        prepare_first_kernel, [full] * 4, low, high, own, other, slip, state, numbers, near, rounded
    )
    slip_mid, state_mid, rounded, coeff, pair, cross = call(
        functools.partial(finish_first_kernel, heights),
        [full, full, half, jax.ShapeDtypeStruct((patches // BS * R, ens), BF16), edge, edge],
        shift, scale, rest, slip, numbers, basis_out, basis_in, near, *outer,
    )
    coeffs = row_coeffs(coeff)
    outer = far_parts(coeffs, pair, cross)
    shift, slip_rest, rest = call(
        prepare_second_kernel, [full] * 3,
        slip, state, slip_mid, state_mid, scale_mid, numbers, near, rounded,
    )
    slip_out, state_out = call(
        functools.partial(finish_second_kernel, heights),
        [full] * 2,
        shift, scale_mid, rest, slip_rest, numbers, basis_out, near, *outer,
        out_specs=[HBM] * 2,
        scratch_shapes=[
            pltpu.VMEM((patches, ens), F32),
            pltpu.VMEM((patches, ens), F32),
            pltpu.SemaphoreType.DMA((2, patches // BS)),
        ],
    )
    return (slip_out, state_out)


def solution(mesh):
    in_specs = (
        P(("row", "col"), None),
        P(("row", "col"), None),
        P(("row", "col")),
        P(("row", "col")),
        P(("row", "col")),
        P(("row", "col")),
        P(("row", "col")),
        P(("row", "col")),
        P(None, ("row", "col"), None),
        P(None, ("row", "col")),
        P(None, ("row", "col")),
        P("row", None, "col"),
        P("row", None, "col"),
        P(None, ("row", "col")),
        P(("row", "col")),
        P(None, ("row", "col")),
        P("col", None),
        P("col", None),
    )
    out_specs = (P(("row", "col"), None), P(("row", "col"), None))
    return jax.shard_map(
        per_device, mesh=mesh, in_specs=in_specs, out_specs=out_specs, check_vma=False
    )
```

```python
import functools

import jax
import jax.numpy as jnp
from jax import lax
from jax.experimental import pallas as pl
from jax.experimental.pallas import tpu as pltpu
from jax.sharding import PartitionSpec as P

BS = 256
R = 32

STEP_SIZE = 0.5
REF_FRICTION = 0.6
LIMIT = 16 * 1024 * 1024
F32 = jnp.float32
BF16 = jnp.bfloat16


def dot(a, b):
    return jnp.dot(a, b, preferred_element_type=F32)


def dot_t(a, b):
    return lax.dot_general(a, b, (((0,), (0,)), ((), ())), preferred_element_type=F32)


VMEM = pl.BlockSpec(memory_space=pltpu.VMEM)


def call(kernel, outs, *operands, specs=None, **grid):
    return pl.pallas_call(
        kernel,
        in_specs=specs or [VMEM] * len(operands),
        out_shape=outs,
        compiler_params=pltpu.CompilerParams(vmem_limit_bytes=LIMIT),
        **grid,
    )(*operands)


def rows_at(n, size):
    return pl.ds(pl.multiple_of(n * size, size), size)


HBM = pl.BlockSpec(memory_space=pl.ANY)


def in_hbm(*arrays):
    return [pltpu.with_memory_space_constraint(array, pltpu.HBM) for array in arrays]


def start_copies(pairs, sems, first=0):
    copies = [pltpu.make_async_copy(a, b, sems.at[first + k]) for k, (a, b) in enumerate(pairs)]
    for copy in copies:
        copy.start()
    return copies


def fill_edges(first, last, pair_ref, cross_ref):
    even = lax.rem(lax.axis_index("col"), 2) == 0
    pair_ref[...] = jnp.where(even, last, first)
    cross_ref[...] = jnp.where(even, first, last)


def project_kernel(slip_hbm, basis_hbm, coeff_ref, rounded_ref, slip_ref, basis_ref, sems):
    count = slip_ref.shape[0] // BS
    blocks = [pl.ds(n * BS, BS) for n in range(count)]
    copies = start_copies(
        [(basis_hbm, basis_ref)] + [(slip_hbm.at[at, :], slip_ref.at[at, :]) for at in blocks], sems
    )
    copies[0].wait()
    for n, at in enumerate(blocks):
        copies[1 + n].wait()
        rounded = slip_ref[at, :].astype(BF16)
        rounded_ref[at, :] = rounded
        coeff_ref[n * R : (n + 1) * R, :] = dot(basis_ref[:, at], rounded).astype(BF16)


def project(slip, basis_in):
    patches, ens = slip.shape
    count = patches // BS
    return call(
        project_kernel,
        [
            jax.ShapeDtypeStruct((count * R, ens), BF16),
            jax.ShapeDtypeStruct((patches, ens), BF16),
            jax.ShapeDtypeStruct((patches, ens), F32),
        ],
        *in_hbm(slip, basis_in),
        specs=[HBM] * 2,
        scratch_shapes=[pltpu.VMEM(basis_in.shape, BF16), pltpu.SemaphoreType.DMA((1 + count,))],
    )


def ranks_kernel(
    col_count, rank_hbm, now_hbm, rate_hbm, slip_hbm, wide_ref, joined_ref, pair_ref, cross_ref, rank_ref, ends, sems
):
    sources, share, blocks = rank_ref.shape
    ens = now_hbm.shape[1]
    copies = start_copies(
        [
            (rank_hbm, rank_ref),
            (now_hbm, joined_ref.at[:, pl.ds(0, ens)]),
            (rate_hbm, joined_ref.at[:, pl.ds(ens, ens)]),
            (slip_hbm.at[pl.ds(0, BS), :], ends.at[0]),
            (slip_hbm.at[pl.ds(slip_hbm.shape[0] - BS, BS), :], ends.at[1]),
        ],
        sems,
    )
    width = share * R
    column = lax.broadcasted_iota(jnp.int32, (share, width), 1)
    spread = (lax.div(column, R) == lax.broadcasted_iota(jnp.int32, (share, width), 0)).astype(F32).astype(BF16)
    level = lax.rem(lax.broadcasted_iota(jnp.int32, (blocks, width), 1), R).astype(F32)
    receiver = lax.axis_index("row") * blocks + lax.broadcasted_iota(jnp.int32, (share, blocks), 1)
    copies[0].wait()
    for source in range(sources):
        own = (source * col_count + lax.axis_index("col")) * share + lax.broadcasted_iota(jnp.int32, (share, blocks), 0)
        rank = jnp.where(jnp.abs(receiver - own) > 1, rank_ref[source], 0).astype(F32)
        wide = dot_t(rank.astype(BF16), spread)
        wide_ref[source] = jnp.where(level < wide, wide, 0.0)
    for copy in copies[1:]:
        copy.wait()
    fill_edges(ends[0].astype(BF16), ends[1].astype(BF16), pair_ref, cross_ref)


def side_by_side_kernel(*refs):
    pieces, out_ref = refs[:-1], refs[-1]
    size = pieces[0].shape[0]
    for k, piece in enumerate(pieces):
        out_ref[k * size : (k + 1) * size, :] = piece[...]


def weights_kernel(heights, size, start, *refs):
    begun = start > 0
    sources, rest = refs[:9], refs[9:]
    near_hbm, state_hbm, begun_ref = rest[:3] if begun else (None, None, None)
    rest = rest[4:] if begun else rest[1:]
    numbers_ref, matrix_ref = rest[:2]
    near_ref, state_ref = rest[2:4] if begun else (None, None)
    vectors, lists, sems = rest[-5], rest[-4:-1], rest[-1]
    targets = [vectors.at[k] for k in range(6)] + list(lists)
    copies = start_copies(list(zip(sources, targets)), sems)
    large = [(near_hbm, near_ref), (state_hbm, state_ref)] if begun else []
    large = start_copies(large, sems, len(targets))
    if begun:
        numbers_ref[:start, :] = begun_ref[...]
    count_ref, bricks_ref, weight_ref = lists
    slots = bricks_ref.shape[0]
    col = lax.axis_index("col")
    height, core = lax.div(col, 2).astype(F32), lax.rem(col, 2).astype(F32)
    group, lanes, unrolled = 16, 128, 8
    for copy in copies:
        copy.wait()

    @pl.loop(0, matrix_ref.shape[1] // lanes)
    def _(n):
        own_at = rows_at(n, lanes)
        at = pl.ds(pl.multiple_of(start + n * lanes, lanes), lanes)
        load, normal, direct, evolution, distance, stiffness = (vectors[k, :, at] for k in range(6))
        rows = [load, normal, 1.0 / direct, 1.0 / evolution, evolution / distance, stiffness, load, normal]
        numbers_ref[at if begun else own_at, :] = jnp.concatenate(rows, axis=0).T
        bricks = bricks_ref[:, at].astype(F32)
        live = lax.broadcasted_iota(jnp.int32, (slots, lanes), 0) < count_ref[:, at]
        weights = jnp.where(live, weight_ref[:, at], 0.0)
        merged = jnp.zeros((slots, lanes), F32)
        for k in range(slots):
            merged = merged + jnp.where(bricks == bricks[k : k + 1], weights[k : k + 1], 0.0)
        shares = merged / jnp.sum(weights, axis=0, keepdims=True)
        owner = jnp.floor((bricks + 0.5) * (1.0 / size))
        chip = jnp.floor(owner * 0.5 + 0.25)
        away = height - chip
        away = jnp.where(away < 0, away + heights, away)
        other = jnp.where(owner - 2.0 * chip == core, 0.0, float(heights))
        place = jnp.where(live, (other + away - owner) * size + bricks, -1.0)
        high = jnp.floor((place + 0.5) * (1.0 / group))
        low = place - high * group
        spread = lambda rows, k: jnp.broadcast_to(rows[k : k + 1], (group, lanes)).astype(BF16)
        line = lax.broadcasted_iota(jnp.int32, (group, lanes), 0).astype(F32).astype(BF16)
        none = jnp.full((group, lanes), -1.0, BF16)
        highs = [jnp.where(spread(low, k) == line, spread(high, k), none) for k in range(slots)]
        values = [spread(shares, k) for k in range(slots)]

        @pl.loop(0, matrix_ref.shape[0] // (group * unrolled))
        def _(m):
            first = jnp.full((group, lanes), (m * unrolled).astype(F32)).astype(BF16)
            for step in range(unrolled):
                here = first + jnp.asarray(step, BF16)
                tile = jnp.zeros((group, lanes), BF16)
                for k in range(slots):
                    tile = jnp.where(highs[k] == here, values[k], tile)
                to = pl.ds(pl.multiple_of((m * unrolled + step) * group, group), group)
                matrix_ref[to, own_at] = tile

    for copy in large:
        copy.wait()


def couple_kernel(sources, heights, flip, matrix_ref, *refs):
    coeffs, edges, out_ref = refs[:sources], refs[sources:-1], refs[-1]
    share = coeffs[0].shape[0]
    row, col = lax.axis_index("row"), lax.axis_index("col")
    height, core = lax.div(col, 2), lax.rem(col + flip, 2)

    @pl.loop(0, heights)
    def _(d):
        at = rows_at(2 * lax.rem(height + d, heights) + core, share)
        total = None
        for step in range(sources):
            term = dot(matrix_ref[lax.rem(row + (sources - step), sources), at, :], coeffs[step][...])
            total = term if total is None else total + term
        out_ref[rows_at(d, share), :] = total.astype(out_ref.dtype)

    for edge in edges:
        out_ref[heights * share :, :] = edge[...]


def couple(flip, matrix, coeffs, heights, kind, *edges):
    share, ens = coeffs[0].shape
    return call(
        functools.partial(couple_kernel, len(coeffs), heights, flip),
        jax.ShapeDtypeStruct((heights * share + len(edges) * BS, ens), kind),
        matrix,
        *coeffs,
        *edges,
    )


def chip_sum_kernel(kept_ref, sent_ref, *outs):
    share = outs[0].shape[0]
    for d, out_ref in enumerate(outs):

        @pl.loop(0, share // 32)
        def _(n):
            at = pl.ds(pl.multiple_of(d * share + n * 32, 32), 32)
            out_ref[rows_at(n, 32), :] = (kept_ref[at, :] + sent_ref[at, :].astype(F32)).astype(BF16)


def chip_sum(kept, sent, heights):
    rows, ens = kept.shape
    return list(call(chip_sum_kernel, [jax.ShapeDtypeStruct((rows // heights, ens), BF16)] * heights, kept, sent))


def near_tau(n, slip, numbers, near_ref, rounded_ref):
    count = rounded_ref.shape[0] // BS
    at = rows_at(n, BS)
    none = jnp.zeros((BS, rounded_ref.shape[1]), BF16)
    before = jnp.where(n == 0, none, rounded_ref[rows_at(jnp.maximum(n - 1, 0), BS), :])
    after = jnp.where(n == count - 1, none, rounded_ref[rows_at(jnp.minimum(n + 1, count - 1), BS), :])
    near = dot(near_ref[0, at, :], before) + dot(near_ref[1, at, :], rounded_ref[at, :]) + dot(near_ref[2, at, :], after)
    return numbers[:, 0:1] - numbers[:, 5:6] * slip - near


def prepare_first_kernel(
    low_ref, high_ref, own_ref, other_ref, slip_ref, state_ref, numbers_ref, near_ref, rounded_ref,
    shift_ref, scale_ref, rest_ref, scale_mid_ref,
):
    half = own_ref.shape[0]
    ens = slip_ref.shape[1]
    blocks = low_ref.shape[1] // BS

    def block(matrix_ref, m, n):
        at, own_at = rows_at(n, BS), rows_at(m, BS)
        total = dot_t(matrix_ref[:half, own_at], own_ref[...]) + dot_t(matrix_ref[half:, own_at], other_ref[...])
        numbers = numbers_ref[at, :]
        normal, inv_direct, inv_evolution, ratio = (numbers[:, k : k + 1] for k in range(1, 5))
        base = total[:, :ens]
        scale = inv_direct / (normal - base)
        scale_ref[at, :] = scale
        scale_mid_ref[at, :] = inv_direct / (normal - (base + STEP_SIZE * total[:, ens:]))
        state = state_ref[at, :]
        tau = near_tau(n, slip_ref[at, :], numbers, near_ref, rounded_ref)
        shift_ref[at, :] = tau * scale - state * inv_direct
        rest_ref[at, :] = state + (STEP_SIZE * ratio) * jnp.exp((REF_FRICTION - state) * inv_evolution)

    @pl.loop(0, blocks)
    def _(m):
        block(low_ref, m, m)

    @pl.loop(0, blocks)
    def _(m):
        block(high_ref, m, blocks + m)


def over_blocks(block, basis_ref, near_ref, parts, pair_ref, cross_ref):
    count = near_ref.shape[1] // BS

    def far(n):
        levels = rows_at(n, R)
        total = parts[0][levels, :].astype(F32)
        for part in parts[1:]:
            total = total + part[levels, :].astype(F32)
        return dot_t(basis_ref[:, rows_at(n, BS)], total.astype(BF16))

    even = lax.rem(lax.axis_index("col"), 2) == 0
    pair, cross = pair_ref[-BS:], cross_ref[...]
    block(0, far(0) + dot(near_ref[0, :BS, :], jnp.where(even, cross, pair)))

    @pl.loop(1, count - 1, unroll=3)
    def _(n):
        block(n, far(n))

    block(count - 1, far(count - 1) + dot(near_ref[2, -BS:, :], jnp.where(even, pair, cross)))


def finish_first_kernel(
    heights, shift_ref, scale_ref, slip_ref, basis_out_ref, basis_in_ref, near_ref, *refs
):
    parts, pair_ref, cross_ref = refs[:heights], refs[heights], refs[heights + 1]
    speed_ref, rounded_ref, coeff_ref, pair_out, cross_out = refs[heights + 2 :]

    def block(n, outer):
        at = rows_at(n, BS)
        speed = jnp.exp(shift_ref[at, :] - scale_ref[at, :] * outer)
        speed_ref[at, :] = speed
        rounded = (slip_ref[at, :] + STEP_SIZE * speed).astype(BF16)
        rounded_ref[at, :] = rounded
        coeff_ref[rows_at(n, R), :] = dot(basis_in_ref[:, at], rounded).astype(BF16)

    over_blocks(block, basis_out_ref, near_ref, parts, pair_ref, cross_ref)
    fill_edges(rounded_ref[:BS], rounded_ref[-BS:], pair_out, cross_out)


def prepare_second_kernel(
    slip_ref, state_ref, speed_ref, part_ref, scale_ref, numbers_ref, near_ref, rounded_ref,
    shift_ref, slip_rest_ref, rest_ref,
):
    @pl.loop(0, slip_ref.shape[0] // BS)
    def _(n):
        at = rows_at(n, BS)
        numbers = numbers_ref[at, :]
        inv_direct, inv_evolution, ratio = (numbers[:, k : k + 1] for k in range(2, 5))
        speed = speed_ref[at, :]
        slip = slip_ref[at, :] + STEP_SIZE * speed
        state = part_ref[at, :] - (STEP_SIZE * ratio) * speed
        tau = near_tau(n, slip, numbers, near_ref, rounded_ref)
        shift_ref[at, :] = tau * scale_ref[at, :] - state * inv_direct
        slip_rest_ref[at, :] = 0.5 * (slip_ref[at, :] + slip)
        friction = jnp.exp((REF_FRICTION - state) * inv_evolution)
        rest_ref[at, :] = 0.5 * (state_ref[at, :] + state) + (0.5 * STEP_SIZE * ratio) * friction


def finish_second_kernel(
    heights, shift_ref, scale_ref, rest_ref, slip_rest_ref, numbers_ref, basis_out_ref, near_ref, *refs
):
    parts, pair_ref, cross_ref = refs[:heights], refs[heights], refs[heights + 1]
    slip_hbm, state_hbm, slip_ref, state_ref, sems = refs[heights + 2 :]

    def copies(n):
        at = rows_at(n, BS)
        return [
            pltpu.make_async_copy(slip_ref.at[at, :], slip_hbm.at[at, :], sems.at[0, n]),
            pltpu.make_async_copy(state_ref.at[at, :], state_hbm.at[at, :], sems.at[1, n]),
        ]

    def block(n, outer):
        at = rows_at(n, BS)
        speed = jnp.exp(shift_ref[at, :] - scale_ref[at, :] * outer)
        slip_ref[at, :] = slip_rest_ref[at, :] + (0.5 * STEP_SIZE) * speed
        state_ref[at, :] = rest_ref[at, :] - (0.5 * STEP_SIZE * numbers_ref[at, 4:5]) * speed
        for copy in copies(n):
            copy.start()

    over_blocks(block, basis_out_ref, near_ref, parts, pair_ref, cross_ref)

    @pl.loop(0, slip_ref.shape[0] // BS)
    def _(n):
        for copy in copies(n):
            copy.wait()


def masked_coupling(coupling, wide):
    rows, sources, width = coupling.shape
    blocks = rows // R
    keep = jnp.arange(R, dtype=jnp.int32).astype(F32)[None, None, :, None] < wide[:, :, None, :]
    matrix = jnp.transpose(coupling, (1, 0, 2)).reshape(sources, blocks, R, width)
    masked = jnp.where(keep, matrix, jnp.zeros((), BF16)).reshape(sources, rows, width)
    return pltpu.with_memory_space_constraint(masked, pltpu.VMEM)


def per_device(
    slip,
    state,
    tau_load,
    normal_stress,
    direct_effect,
    evolution_effect,
    slip_distance,
    self_stiffness,
    near_blocks,
    basis_in,
    basis_out,
    coupling,
    block_rank,
    adj_bricks,
    adj_count,
    adj_weight,
    pressure_now,
    pressure_rate,
):
    row_count = lax.axis_size("row")
    col_count = lax.axis_size("col")
    row_index = lax.axis_index("row")
    col_index = lax.axis_index("col")
    heights = col_count // 2
    height, core = col_index // 2, col_index % 2
    both = ("row", "col")
    devices = row_count * col_count

    def to_row(array, d):
        return lax.ppermute(array, "row", [(i, (i + d) % row_count) for i in range(row_count)])

    def to_height(array, d):
        pairs = [(2 * z + k, 2 * ((z + d) % heights) + k) for z in range(heights) for k in range(2)]
        return lax.ppermute(array, "col", pairs)

    def to_core(array):
        return lax.ppermute(array, "col", [(2 * z + k, 2 * z + 1 - k) for z in range(heights) for k in range(2)])

    def to_chip(array):
        ends = [(i, i + 1) for i in range(1, devices - 1, 2)]
        return lax.ppermute(array, both, ends + [(j, i) for i, j in ends])

    patches, ens = slip.shape
    slots = adj_bricks.shape[0]
    size = pressure_now.shape[0]
    share = coupling.shape[2]
    def far_parts(coeffs, pair, cross):
        sent = to_core(couple(1, masked, coeffs, heights, BF16, pair))
        kept = couple(0, masked, coeffs, heights, F32)
        pieces = chip_sum(kept, sent, heights)
        parts = pieces[:1] + [to_height(pieces[d], d) for d in range(1, heights)]
        return parts + [sent, cross]

    def row_coeffs(coeff):
        return [coeff] + [to_row(coeff, d) for d in range(1, row_count)]

    full = jax.ShapeDtypeStruct((patches, ens), F32)
    half = jax.ShapeDtypeStruct((patches, ens), BF16)
    edge = jax.ShapeDtypeStruct((BS, ens), BF16)
    per_patch = [tau_load, normal_stress, direct_effect, evolution_effect, slip_distance, self_stiffness]

    ranks = jnp.transpose(block_rank, (1, 2, 0))
    wide, joined, pair, cross = call(
        functools.partial(ranks_kernel, col_count),
        [
            jax.ShapeDtypeStruct((ranks.shape[0], ranks.shape[2], share), F32),
            jax.ShapeDtypeStruct((size, 2 * ens), BF16),
            edge,
            edge,
        ],
        *in_hbm(ranks, pressure_now, pressure_rate, slip),
        specs=[HBM] * 4,
        scratch_shapes=[
            pltpu.VMEM(ranks.shape, jnp.int32),
            pltpu.VMEM((2, BS, ens), F32),
            pltpu.SemaphoreType.DMA((5,)),
        ],
    )
    fields = [joined] + [to_height(joined, d) for d in range(1, heights)]
    masked = masked_coupling(coupling, wide)
    masked, slip = lax.optimization_barrier((masked, slip))
    coeff, rounded, slip = project(slip, basis_in)
    coeffs = row_coeffs(coeff)
    brick_lists = [adj_count[None], adj_bricks, adj_weight]
    columns = [array[None] for array in per_patch] + brick_lists
    start = patches // 2
    part = jax.ShapeDtypeStruct((2 * heights * size, start), BF16)
    scratch = [
        pltpu.VMEM((6, 1, patches), F32),
        pltpu.VMEM((1, patches), jnp.int32),
        pltpu.VMEM(adj_bricks.shape, jnp.int32),
        pltpu.VMEM(adj_weight.shape, F32),
        pltpu.SemaphoreType.DMA((11,)),
    ]
    numbers, low = call(
        functools.partial(weights_kernel, heights, size, 0),
        [jax.ShapeDtypeStruct((start, 8), F32), part],
        *in_hbm(*columns),
        coeff,
        specs=[HBM] * 9 + [VMEM],
        scratch_shapes=scratch,
    )
    fields, cross, coeffs, low = lax.optimization_barrier((fields, to_chip(cross), coeffs, low))
    own = call(
        side_by_side_kernel, jax.ShapeDtypeStruct((heights * size, 2 * ens), BF16), *fields
    )
    other = to_core(own)
    outer = far_parts(coeffs, pair, cross)
    numbers, high, near, state = call(
        functools.partial(weights_kernel, heights, size, start),
        [jax.ShapeDtypeStruct((patches, 8), F32), part, jax.ShapeDtypeStruct(near_blocks.shape, BF16), full],
        *in_hbm(*columns, near_blocks, state),
        numbers,
        outer[0],
        specs=[HBM] * 11 + [VMEM] * 2,
        scratch_shapes=scratch,
    )
    shift, scale, rest, scale_mid = call(
        prepare_first_kernel, [full] * 4, low, high, own, other, slip, state, numbers, near, rounded
    )
    speed, rounded, coeff, pair, cross = call(
        functools.partial(finish_first_kernel, heights),
        [full, half, jax.ShapeDtypeStruct((patches // BS * R, ens), BF16), edge, edge],
        shift, scale, slip, basis_out, basis_in, near, *outer,
    )
    coeffs, cross = lax.optimization_barrier((row_coeffs(coeff), to_chip(cross)))
    outer = far_parts(coeffs, pair, cross)
    shift, slip_rest, rest = call(
        prepare_second_kernel, [full] * 3,
        slip, state, speed, rest, scale_mid, numbers, near, rounded,
    )
    slip_out, state_out = call(
        functools.partial(finish_second_kernel, heights),
        [full] * 2,
        shift, scale_mid, rest, slip_rest, numbers, basis_out, near, *outer,
        out_specs=[HBM] * 2,
        scratch_shapes=[
            pltpu.VMEM((patches, ens), F32),
            pltpu.VMEM((patches, ens), F32),
            pltpu.SemaphoreType.DMA((2, patches // BS)),
        ],
    )
    return (slip_out, state_out)


def solution(mesh):
    in_specs = (
        P(("row", "col"), None),
        P(("row", "col"), None),
        P(("row", "col")),
        P(("row", "col")),
        P(("row", "col")),
        P(("row", "col")),
        P(("row", "col")),
        P(("row", "col")),
        P(None, ("row", "col"), None),
        P(None, ("row", "col")),
        P(None, ("row", "col")),
        P("row", None, "col"),
        P("row", None, "col"),
        P(None, ("row", "col")),
        P(("row", "col")),
        P(None, ("row", "col")),
        P("col", None),
        P("col", None),
    )
    out_specs = (P(("row", "col"), None), P(("row", "col"), None))
    return jax.shard_map(
        per_device, mesh=mesh, in_specs=in_specs, out_specs=out_specs, check_vma=False
    )
```

```python
import functools

import jax
import jax.numpy as jnp
from jax import lax
from jax.experimental import pallas as pl
from jax.experimental.pallas import tpu as pltpu
from jax.sharding import PartitionSpec as P

BS = 256
R = 32

STEP_SIZE = 0.5
REF_FRICTION = 0.6
LIMIT = 16 * 1024 * 1024
F32 = jnp.float32
BF16 = jnp.bfloat16


def dot(a, b):
    return jnp.dot(a, b, preferred_element_type=F32)


def dot_t(a, b):
    return lax.dot_general(a, b, (((0,), (0,)), ((), ())), preferred_element_type=F32)


VMEM = pl.BlockSpec(memory_space=pltpu.VMEM)


def call(kernel, outs, *operands, specs=None, **grid):
    return pl.pallas_call(
        kernel,
        in_specs=specs or [VMEM] * len(operands),
        out_shape=outs,
        compiler_params=pltpu.CompilerParams(vmem_limit_bytes=LIMIT),
        **grid,
    )(*operands)


def rows_at(n, size):
    return pl.ds(pl.multiple_of(n * size, size), size)


HBM = pl.BlockSpec(memory_space=pl.ANY)


def in_hbm(*arrays):
    return [pltpu.with_memory_space_constraint(array, pltpu.HBM) for array in arrays]


def start_copies(pairs, sems, first=0):
    copies = [pltpu.make_async_copy(a, b, sems.at[first + k]) for k, (a, b) in enumerate(pairs)]
    for copy in copies:
        copy.start()
    return copies


def fill_edges(first, last, pair_ref, cross_ref):
    even = lax.rem(lax.axis_index("col"), 2) == 0
    pair_ref[...] = jnp.where(even, last, first)
    cross_ref[...] = jnp.where(even, first, last)


def project_kernel(slip_hbm, basis_hbm, coeff_ref, rounded_ref, pair_ref, cross_ref, slip_ref, basis_ref, sems):
    count = slip_ref.shape[0] // BS
    blocks = [pl.ds(n * BS, BS) for n in range(count)]
    copies = start_copies(
        [(basis_hbm, basis_ref)] + [(slip_hbm.at[at, :], slip_ref.at[at, :]) for at in blocks], sems
    )
    copies[0].wait()
    for n, at in enumerate(blocks):
        copies[1 + n].wait()
        rounded = slip_ref[at, :].astype(BF16)
        rounded_ref[at, :] = rounded
        coeff_ref[n * R : (n + 1) * R, :] = dot(basis_ref[:, at], rounded).astype(BF16)
    fill_edges(rounded_ref[:BS], rounded_ref[-BS:], pair_ref, cross_ref)


def project(slip, basis_in):
    patches, ens = slip.shape
    count = patches // BS
    edge = jax.ShapeDtypeStruct((BS, ens), BF16)
    return call(
        project_kernel,
        [
            jax.ShapeDtypeStruct((count * R, ens), BF16),
            jax.ShapeDtypeStruct((patches, ens), BF16),
            edge,
            edge,
            jax.ShapeDtypeStruct((patches, ens), F32),
        ],
        *in_hbm(slip, basis_in),
        specs=[HBM] * 2,
        scratch_shapes=[pltpu.VMEM(basis_in.shape, BF16), pltpu.SemaphoreType.DMA((1 + count,))],
    )


def ranks_kernel(
    col_count, rank_hbm, now_hbm, rate_hbm, wide_ref, joined_ref, rank_ref, sems
):
    sources, share, blocks = rank_ref.shape
    ens = now_hbm.shape[1]
    copies = start_copies(
        [
            (rank_hbm, rank_ref),
            (now_hbm, joined_ref.at[:, pl.ds(0, ens)]),
            (rate_hbm, joined_ref.at[:, pl.ds(ens, ens)]),
        ],
        sems,
    )
    width = share * R
    column = lax.broadcasted_iota(jnp.int32, (share, width), 1)
    spread = (lax.div(column, R) == lax.broadcasted_iota(jnp.int32, (share, width), 0)).astype(F32).astype(BF16)
    level = lax.rem(lax.broadcasted_iota(jnp.int32, (blocks, width), 1), R).astype(F32)
    receiver = lax.axis_index("row") * blocks + lax.broadcasted_iota(jnp.int32, (share, blocks), 1)
    copies[0].wait()
    for source in range(sources):
        own = (source * col_count + lax.axis_index("col")) * share + lax.broadcasted_iota(jnp.int32, (share, blocks), 0)
        rank = jnp.where(jnp.abs(receiver - own) > 1, rank_ref[source], 0).astype(F32)
        wide = dot_t(rank.astype(BF16), spread)
        wide_ref[source] = jnp.where(level < wide, wide, 0.0)
    copies[1].wait()
    copies[2].wait()


def side_by_side_kernel(*refs):
    pieces, out_ref = refs[:-1], refs[-1]
    size = pieces[0].shape[0]
    for k, piece in enumerate(pieces):
        out_ref[k * size : (k + 1) * size, :] = piece[...]


def weights_kernel(heights, size, start, *refs):
    begun = start > 0
    sources, rest = refs[:9], refs[9:]
    near_hbm, state_hbm, begun_ref = rest[:3] if begun else (None, None, None)
    rest = rest[4:] if begun else rest[1:]
    numbers_ref, matrix_ref = rest[:2]
    near_ref, state_ref = rest[2:4] if begun else (None, None)
    vectors, lists, sems = rest[-5], rest[-4:-1], rest[-1]
    targets = [vectors.at[k] for k in range(6)] + list(lists)
    copies = start_copies(list(zip(sources, targets)), sems)
    large = [(near_hbm, near_ref), (state_hbm, state_ref)] if begun else []
    large = start_copies(large, sems, len(targets))
    if begun:
        numbers_ref[:start, :] = begun_ref[...]
    count_ref, bricks_ref, weight_ref = lists
    slots = bricks_ref.shape[0]
    col = lax.axis_index("col")
    height, core = lax.div(col, 2).astype(F32), lax.rem(col, 2).astype(F32)
    group, lanes, unrolled = 16, 128, 8
    for copy in copies:
        copy.wait()

    @pl.loop(0, matrix_ref.shape[1] // lanes)
    def _(n):
        own_at = rows_at(n, lanes)
        at = pl.ds(pl.multiple_of(start + n * lanes, lanes), lanes)
        load, normal, direct, evolution, distance, stiffness = (vectors[k, :, at] for k in range(6))
        rows = [load, normal, 1.0 / direct, 1.0 / evolution, evolution / distance, stiffness, load, normal]
        numbers_ref[at if begun else own_at, :] = jnp.concatenate(rows, axis=0).T
        bricks = bricks_ref[:, at].astype(F32)
        live = lax.broadcasted_iota(jnp.int32, (slots, lanes), 0) < count_ref[:, at]
        weights = jnp.where(live, weight_ref[:, at], 0.0)
        merged = jnp.zeros((slots, lanes), F32)
        for k in range(slots):
            merged = merged + jnp.where(bricks == bricks[k : k + 1], weights[k : k + 1], 0.0)
        shares = merged / jnp.sum(weights, axis=0, keepdims=True)
        owner = jnp.floor((bricks + 0.5) * (1.0 / size))
        chip = jnp.floor(owner * 0.5 + 0.25)
        away = height - chip
        away = jnp.where(away < 0, away + heights, away)
        other = jnp.where(owner - 2.0 * chip == core, 0.0, float(heights))
        place = jnp.where(live, (other + away - owner) * size + bricks, -1.0)
        high = jnp.floor((place + 0.5) * (1.0 / group))
        low = place - high * group
        spread = lambda rows, k: jnp.broadcast_to(rows[k : k + 1], (group, lanes)).astype(BF16)
        line = lax.broadcasted_iota(jnp.int32, (group, lanes), 0).astype(F32).astype(BF16)
        none = jnp.full((group, lanes), -1.0, BF16)
        highs = [jnp.where(spread(low, k) == line, spread(high, k), none) for k in range(slots)]
        values = [spread(shares, k) for k in range(slots)]

        @pl.loop(0, matrix_ref.shape[0] // (group * unrolled))
        def _(m):
            first = jnp.full((group, lanes), (m * unrolled).astype(F32)).astype(BF16)
            for step in range(unrolled):
                here = first + jnp.asarray(step, BF16)
                tile = jnp.zeros((group, lanes), BF16)
                for k in range(slots):
                    tile = jnp.where(highs[k] == here, values[k], tile)
                to = pl.ds(pl.multiple_of((m * unrolled + step) * group, group), group)
                matrix_ref[to, own_at] = tile

    for copy in large:
        copy.wait()


def couple_kernel(sources, heights, flip, matrix_ref, *refs):
    coeffs, edges, out_ref = refs[:sources], refs[sources:-1], refs[-1]
    share = coeffs[0].shape[0]
    row, col = lax.axis_index("row"), lax.axis_index("col")
    height, core = lax.div(col, 2), lax.rem(col + flip, 2)

    @pl.loop(0, heights, unroll=True)
    def _(d):
        partner = lax.rem(d, 2) * (1 - 2 * lax.rem(height, 2))
        at = rows_at(2 * lax.rem(height + partner + d - lax.rem(d, 2) + heights, heights) + core, share)
        total = None
        for step in range(sources):
            term = dot(matrix_ref[lax.rem(row + (sources - step), sources), at, :], coeffs[step][...])
            total = term if total is None else total + term
        out_ref[rows_at(d, share), :] = total.astype(out_ref.dtype)

    for edge in edges:
        out_ref[heights * share :, :] = edge[...]


def couple(flip, matrix, coeffs, heights, kind, *edges):
    share, ens = coeffs[0].shape
    return call(
        functools.partial(couple_kernel, len(coeffs), heights, flip),
        jax.ShapeDtypeStruct((heights * share + len(edges) * BS, ens), kind),
        matrix,
        *coeffs,
        *edges,
    )


def chip_sum_kernel(kept_ref, sent_ref, own_ref, direct_ref, pass_ref, keep_ref):
    share = own_ref.shape[0]
    group = 32
    for place in range(2 + 2 * (keep_ref.shape[0] // share)):
        far = place // 2 - 1
        out_ref = (own_ref, direct_ref)[place % 2] if far < 0 else (keep_ref, pass_ref)[place % 2]

        @pl.loop(0, share // group)
        def _(n):
            at = pl.ds(pl.multiple_of(place * share + n * group, group), group)
            to = pl.ds(pl.multiple_of(max(far, 0) * share + n * group, group), group)
            out_ref[to, :] = (kept_ref[at, :] + sent_ref[at, :].astype(F32)).astype(out_ref.dtype)


def chip_sum(kept, sent, heights):
    rows, ens = kept.shape
    share = rows // heights
    far = (heights // 2 - 1) * share
    shapes = [(share, BF16), (share, BF16), (far, BF16), (far, F32)]
    return call(chip_sum_kernel, [jax.ShapeDtypeStruct((n, ens), kind) for n, kind in shapes], kept, sent)


def pair_sum_kernel(keep_ref, came_ref, *outs):
    share = outs[0].shape[0]
    group = 32
    for far, out_ref in enumerate(outs):

        @pl.loop(0, share // group)
        def _(n):
            at = pl.ds(pl.multiple_of(far * share + n * group, group), group)
            out_ref[rows_at(n, group), :] = (keep_ref[at, :] + came_ref[at, :].astype(F32)).astype(BF16)


def near_tau(n, slip, numbers, near_ref, rounded_ref):
    count = rounded_ref.shape[0] // BS
    at = rows_at(n, BS)
    none = jnp.zeros((BS, rounded_ref.shape[1]), BF16)
    before = jnp.where(n == 0, none, rounded_ref[rows_at(jnp.maximum(n - 1, 0), BS), :])
    after = jnp.where(n == count - 1, none, rounded_ref[rows_at(jnp.minimum(n + 1, count - 1), BS), :])
    near = dot(near_ref[0, at, :], before) + dot(near_ref[1, at, :], rounded_ref[at, :]) + dot(near_ref[2, at, :], after)
    return numbers[:, 0:1] - numbers[:, 5:6] * slip - near


def prepare_first_kernel(
    low_ref, high_ref, own_ref, other_ref, slip_ref, state_ref, numbers_ref, near_ref, rounded_ref,
    shift_ref, scale_ref, rest_ref, scale_mid_ref,
):
    half = own_ref.shape[0]
    ens = slip_ref.shape[1]
    blocks = low_ref.shape[1] // BS

    def block(matrix_ref, m, n):
        at, own_at = rows_at(n, BS), rows_at(m, BS)
        total = dot_t(matrix_ref[:half, own_at], own_ref[...]) + dot_t(matrix_ref[half:, own_at], other_ref[...])
        numbers = numbers_ref[at, :]
        normal, inv_direct, inv_evolution, ratio = (numbers[:, k : k + 1] for k in range(1, 5))
        base = total[:, :ens]
        scale = inv_direct / (normal - base)
        scale_ref[at, :] = scale
        scale_mid_ref[at, :] = inv_direct / (normal - (base + STEP_SIZE * total[:, ens:]))
        state = state_ref[at, :]
        tau = near_tau(n, slip_ref[at, :], numbers, near_ref, rounded_ref)
        shift_ref[at, :] = tau * scale - state * inv_direct
        rest_ref[at, :] = state + (STEP_SIZE * ratio) * jnp.exp((REF_FRICTION - state) * inv_evolution)

    @pl.loop(0, blocks)
    def _(m):
        block(low_ref, m, m)

    @pl.loop(0, blocks)
    def _(m):
        block(high_ref, m, blocks + m)


def over_blocks(block, basis_ref, near_ref, parts, pair_ref, cross_ref):
    count = near_ref.shape[1] // BS

    def far(n):
        levels = rows_at(n, R)
        total = parts[0][levels, :].astype(F32)
        for part in parts[1:]:
            total = total + part[levels, :].astype(F32)
        return dot_t(basis_ref[:, rows_at(n, BS)], total.astype(BF16))

    even = lax.rem(lax.axis_index("col"), 2) == 0
    pair, cross = pair_ref[-BS:], cross_ref[...]
    block(0, far(0) + dot(near_ref[0, :BS, :], jnp.where(even, cross, pair)))

    @pl.loop(1, count - 1, unroll=True)
    def _(n):
        block(n, far(n))

    block(count - 1, far(count - 1) + dot(near_ref[2, -BS:, :], jnp.where(even, pair, cross)))


def finish_first_kernel(
    count, shift_ref, scale_ref, slip_ref, basis_out_ref, basis_in_ref, near_ref, *refs
):
    parts, pair_ref, cross_ref = refs[:count], refs[count], refs[count + 1]
    speed_ref, rounded_ref, coeff_ref, pair_out, cross_out = refs[count + 2 :]

    def block(n, outer):
        at = rows_at(n, BS)
        speed = jnp.exp(shift_ref[at, :] - scale_ref[at, :] * outer)
        speed_ref[at, :] = speed
        rounded = (slip_ref[at, :] + STEP_SIZE * speed).astype(BF16)
        rounded_ref[at, :] = rounded
        coeff_ref[rows_at(n, R), :] = dot(basis_in_ref[:, at], rounded).astype(BF16)

    over_blocks(block, basis_out_ref, near_ref, parts, pair_ref, cross_ref)
    fill_edges(rounded_ref[:BS], rounded_ref[-BS:], pair_out, cross_out)


def prepare_second_kernel(
    slip_ref, state_ref, speed_ref, part_ref, scale_ref, numbers_ref, near_ref, rounded_ref,
    shift_ref, slip_rest_ref, rest_ref,
):
    @pl.loop(0, slip_ref.shape[0] // BS)
    def _(n):
        at = rows_at(n, BS)
        numbers = numbers_ref[at, :]
        inv_direct, inv_evolution, ratio = (numbers[:, k : k + 1] for k in range(2, 5))
        speed = speed_ref[at, :]
        slip = slip_ref[at, :] + STEP_SIZE * speed
        state = part_ref[at, :] - (STEP_SIZE * ratio) * speed
        tau = near_tau(n, slip, numbers, near_ref, rounded_ref)
        shift_ref[at, :] = tau * scale_ref[at, :] - state * inv_direct
        slip_rest_ref[at, :] = 0.5 * (slip_ref[at, :] + slip)
        friction = jnp.exp((REF_FRICTION - state) * inv_evolution)
        rest_ref[at, :] = 0.5 * (state_ref[at, :] + state) + (0.5 * STEP_SIZE * ratio) * friction


def finish_second_kernel(
    count, shift_ref, scale_ref, rest_ref, slip_rest_ref, numbers_ref, basis_out_ref, near_ref, *refs
):
    parts, pair_ref, cross_ref = refs[:count], refs[count], refs[count + 1]
    slip_hbm, state_hbm, slip_ref, state_ref, sems = refs[count + 2 :]

    def copies(n):
        at = rows_at(n, BS)
        return [
            pltpu.make_async_copy(slip_ref.at[at, :], slip_hbm.at[at, :], sems.at[0, n]),
            pltpu.make_async_copy(state_ref.at[at, :], state_hbm.at[at, :], sems.at[1, n]),
        ]

    def block(n, outer):
        at = rows_at(n, BS)
        speed = jnp.exp(shift_ref[at, :] - scale_ref[at, :] * outer)
        slip_ref[at, :] = slip_rest_ref[at, :] + (0.5 * STEP_SIZE) * speed
        state_ref[at, :] = rest_ref[at, :] - (0.5 * STEP_SIZE * numbers_ref[at, 4:5]) * speed
        for copy in copies(n):
            copy.start()

    over_blocks(block, basis_out_ref, near_ref, parts, pair_ref, cross_ref)

    @pl.loop(0, slip_ref.shape[0] // BS)
    def _(n):
        for copy in copies(n):
            copy.wait()


def masked_coupling(coupling, wide):
    rows, sources, width = coupling.shape
    blocks = rows // R
    keep = jnp.arange(R, dtype=jnp.int32).astype(F32)[None, None, :, None] < wide[:, :, None, :]
    matrix = jnp.transpose(coupling, (1, 0, 2)).reshape(sources, blocks, R, width)
    masked = jnp.where(keep, matrix, jnp.zeros((), BF16)).reshape(sources, rows, width)
    return pltpu.with_memory_space_constraint(masked, pltpu.VMEM)


def per_device(
    slip,
    state,
    tau_load,
    normal_stress,
    direct_effect,
    evolution_effect,
    slip_distance,
    self_stiffness,
    near_blocks,
    basis_in,
    basis_out,
    coupling,
    block_rank,
    adj_bricks,
    adj_count,
    adj_weight,
    pressure_now,
    pressure_rate,
):
    row_count = lax.axis_size("row")
    col_count = lax.axis_size("col")
    row_index = lax.axis_index("row")
    col_index = lax.axis_index("col")
    heights = col_count // 2
    height, core = col_index // 2, col_index % 2
    both = ("row", "col")
    devices = row_count * col_count

    def to_row(array, d):
        return lax.ppermute(array, "row", [(i, (i + d) % row_count) for i in range(row_count)])

    def to_height(array, d):
        pairs = [(2 * z + k, 2 * ((z + d) % heights) + k) for z in range(heights) for k in range(2)]
        return lax.ppermute(array, "col", pairs)

    def to_core(array):
        return lax.ppermute(array, "col", [(2 * z + k, 2 * z + 1 - k) for z in range(heights) for k in range(2)])

    def to_chip(array):
        ends = [(i, i + 1) for i in range(1, devices - 1, 2)]
        return lax.ppermute(array, both, ends + [(j, i) for i, j in ends])

    patches, ens = slip.shape
    slots = adj_bricks.shape[0]
    size = pressure_now.shape[0]
    share = coupling.shape[2]
    def to_partner(array):
        pairs = [(2 * z + k, 2 * (z + 1 - 2 * (z % 2)) + k) for z in range(heights) for k in range(2)]
        return lax.ppermute(array, "col", pairs)

    def first_step(coeffs, pair, cross):
        sent = to_core(couple(1, masked, coeffs, heights, BF16, pair))
        kept = couple(0, masked, coeffs, heights, F32)
        own, direct, passed, keep = chip_sum(kept, sent, heights)
        own, cross = lax.optimization_barrier((own, cross))
        return own, to_partner(passed), to_partner(direct), keep, [sent, to_chip(cross)]

    def second_step(own, came, direct, keep, edges):
        sums = call(pair_sum_kernel, [jax.ShapeDtypeStruct((share, ens), BF16)] * (heights // 2 - 1), keep, came)
        return [to_height(part, 2 * (d + 1)) for d, part in enumerate(sums)] + [own, direct] + edges

    def row_coeffs(coeff):
        return [coeff] + [to_row(coeff, d) for d in range(1, row_count)]

    full = jax.ShapeDtypeStruct((patches, ens), F32)
    half = jax.ShapeDtypeStruct((patches, ens), BF16)
    edge = jax.ShapeDtypeStruct((BS, ens), BF16)
    per_patch = [tau_load, normal_stress, direct_effect, evolution_effect, slip_distance, self_stiffness]

    ranks = jnp.transpose(block_rank, (1, 2, 0))
    wide, joined = call(
        functools.partial(ranks_kernel, col_count),
        [
            jax.ShapeDtypeStruct((ranks.shape[0], ranks.shape[2], share), F32),
            jax.ShapeDtypeStruct((size, 2 * ens), BF16),
        ],
        *in_hbm(ranks, pressure_now, pressure_rate),
        specs=[HBM] * 3,
        scratch_shapes=[pltpu.VMEM(ranks.shape, jnp.int32), pltpu.SemaphoreType.DMA((3,))],
    )
    fields = [joined] + [to_height(joined, d) for d in range(1, heights)]
    masked = masked_coupling(coupling, wide)
    masked, slip = lax.optimization_barrier((masked, slip))
    coeff, rounded, pair, cross, slip = project(slip, basis_in)
    coeffs = row_coeffs(coeff)
    brick_lists = [adj_count[None], adj_bricks, adj_weight]
    columns = [array[None] for array in per_patch] + brick_lists
    start = patches // 2
    part = jax.ShapeDtypeStruct((2 * heights * size, start), BF16)
    scratch = [
        pltpu.VMEM((6, 1, patches), F32),
        pltpu.VMEM((1, patches), jnp.int32),
        pltpu.VMEM(adj_bricks.shape, jnp.int32),
        pltpu.VMEM(adj_weight.shape, F32),
        pltpu.SemaphoreType.DMA((11,)),
    ]
    numbers, low = call(
        functools.partial(weights_kernel, heights, size, 0),
        [jax.ShapeDtypeStruct((start, 8), F32), part],
        *in_hbm(*columns),
        coeff,
        specs=[HBM] * 9 + [VMEM],
        scratch_shapes=scratch,
    )
    fields, coeffs, low = lax.optimization_barrier((fields, coeffs, low))
    own = call(
        side_by_side_kernel, jax.ShapeDtypeStruct((heights * size, 2 * ens), BF16), *fields
    )
    other = to_core(own)
    own_part, came, direct, keep, edges = first_step(coeffs, pair, cross)
    numbers, high, near, state = call(
        functools.partial(weights_kernel, heights, size, start),
        [jax.ShapeDtypeStruct((patches, 8), F32), part, jax.ShapeDtypeStruct(near_blocks.shape, BF16), full],
        *in_hbm(*columns, near_blocks, state),
        numbers,
        own_part,
        specs=[HBM] * 11 + [VMEM] * 2,
        scratch_shapes=scratch,
    )
    came, high = lax.optimization_barrier((came, high))
    outer = second_step(own_part, came, direct, keep, edges)
    shift, scale, rest, scale_mid = call(
        prepare_first_kernel, [full] * 4, low, high, own, other, slip, state, numbers, near, rounded
    )
    speed, rounded, coeff, pair, cross = call(
        functools.partial(finish_first_kernel, len(outer) - 2),
        [full, half, jax.ShapeDtypeStruct((patches // BS * R, ens), BF16), edge, edge],
        shift, scale, slip, basis_out, basis_in, near, *outer,
    )
    coeffs = row_coeffs(coeff)
    outer = second_step(*first_step(coeffs, pair, cross))
    shift, slip_rest, rest = call(
        prepare_second_kernel, [full] * 3,
        slip, state, speed, rest, scale_mid, numbers, near, rounded,
    )
    slip_out, state_out = call(
        functools.partial(finish_second_kernel, len(outer) - 2),
        [full] * 2,
        shift, scale_mid, rest, slip_rest, numbers, basis_out, near, *outer,
        out_specs=[HBM] * 2,
        scratch_shapes=[
            pltpu.VMEM((patches, ens), F32),
            pltpu.VMEM((patches, ens), F32),
            pltpu.SemaphoreType.DMA((2, patches // BS)),
        ],
    )
    return (slip_out, state_out)


def solution(mesh):
    in_specs = (
        P(("row", "col"), None),
        P(("row", "col"), None),
        P(("row", "col")),
        P(("row", "col")),
        P(("row", "col")),
        P(("row", "col")),
        P(("row", "col")),
        P(("row", "col")),
        P(None, ("row", "col"), None),
        P(None, ("row", "col")),
        P(None, ("row", "col")),
        P("row", None, "col"),
        P("row", None, "col"),
        P(None, ("row", "col")),
        P(("row", "col")),
        P(None, ("row", "col")),
        P("col", None),
        P("col", None),
    )
    out_specs = (P(("row", "col"), None), P(("row", "col"), None))
    return jax.shard_map(
        per_device, mesh=mesh, in_specs=in_specs, out_specs=out_specs, check_vma=False
    )
```

```python
import functools

import jax
import jax.numpy as jnp
from jax import lax
from jax.experimental import pallas as pl
from jax.experimental.pallas import tpu as pltpu
from jax.sharding import PartitionSpec as P

BS = 256
R = 32

STEP_SIZE = 0.5
REF_FRICTION = 0.6
LIMIT = 16 * 1024 * 1024
F32 = jnp.float32
BF16 = jnp.bfloat16


def dot(a, b):
    return jnp.dot(a, b, preferred_element_type=F32)


def dot_t(a, b):
    return lax.dot_general(a, b, (((0,), (0,)), ((), ())), preferred_element_type=F32)


VMEM = pl.BlockSpec(memory_space=pltpu.VMEM)


def call(kernel, outs, *operands, specs=None, **grid):
    return pl.pallas_call(
        kernel,
        in_specs=specs or [VMEM] * len(operands),
        out_shape=outs,
        compiler_params=pltpu.CompilerParams(vmem_limit_bytes=LIMIT),
        **grid,
    )(*operands)


def rows_at(n, size):
    return pl.ds(pl.multiple_of(n * size, size), size)


HBM = pl.BlockSpec(memory_space=pl.ANY)


def in_hbm(*arrays):
    return [pltpu.with_memory_space_constraint(array, pltpu.HBM) for array in arrays]


def start_copies(pairs, sems, first=0):
    copies = [pltpu.make_async_copy(a, b, sems.at[first + k]) for k, (a, b) in enumerate(pairs)]
    for copy in copies:
        copy.start()
    return copies


def fill_edges(first, last, pair_ref, cross_ref):
    even = lax.rem(lax.axis_index("col"), 2) == 0
    pair_ref[...] = jnp.where(even, last, first)
    cross_ref[...] = jnp.where(even, first, last)


def project_kernel(slip_hbm, basis_hbm, coeff_ref, rounded_ref, pair_ref, cross_ref, slip_ref, basis_ref, sems):
    count = slip_ref.shape[0] // BS
    blocks = [pl.ds(n * BS, BS) for n in range(count)]
    copies = start_copies(
        [(basis_hbm, basis_ref)] + [(slip_hbm.at[at, :], slip_ref.at[at, :]) for at in blocks], sems
    )
    copies[0].wait()
    for n, at in enumerate(blocks):
        copies[1 + n].wait()
        rounded = slip_ref[at, :].astype(BF16)
        rounded_ref[at, :] = rounded
        coeff_ref[n * R : (n + 1) * R, :] = dot(basis_ref[:, at], rounded).astype(BF16)
    fill_edges(rounded_ref[:BS], rounded_ref[-BS:], pair_ref, cross_ref)


def project(slip, basis_in):
    patches, ens = slip.shape
    count = patches // BS
    edge = jax.ShapeDtypeStruct((BS, ens), BF16)
    return call(
        project_kernel,
        [
            jax.ShapeDtypeStruct((count * R, ens), BF16),
            jax.ShapeDtypeStruct((patches, ens), BF16),
            edge,
            edge,
            jax.ShapeDtypeStruct((patches, ens), F32),
        ],
        *in_hbm(slip, basis_in),
        specs=[HBM] * 2,
        scratch_shapes=[pltpu.VMEM(basis_in.shape, BF16), pltpu.SemaphoreType.DMA((1 + count,))],
    )


def ranks_kernel(
    col_count, rank_hbm, now_hbm, rate_hbm, wide_ref, joined_ref, rank_ref, sems
):
    sources, share, blocks = rank_ref.shape
    ens = now_hbm.shape[1]
    copies = start_copies(
        [
            (rank_hbm, rank_ref),
            (now_hbm, joined_ref.at[:, pl.ds(0, ens)]),
            (rate_hbm, joined_ref.at[:, pl.ds(ens, ens)]),
        ],
        sems,
    )
    width = share * R
    column = lax.broadcasted_iota(jnp.int32, (share, width), 1)
    spread = (lax.div(column, R) == lax.broadcasted_iota(jnp.int32, (share, width), 0)).astype(F32).astype(BF16)
    level = lax.rem(lax.broadcasted_iota(jnp.int32, (blocks, width), 1), R).astype(F32)
    receiver = lax.axis_index("row") * blocks + lax.broadcasted_iota(jnp.int32, (share, blocks), 1)
    copies[0].wait()
    for source in range(sources):
        own = (source * col_count + lax.axis_index("col")) * share + lax.broadcasted_iota(jnp.int32, (share, blocks), 0)
        rank = jnp.where(jnp.abs(receiver - own) > 1, rank_ref[source], 0).astype(F32)
        wide = dot_t(rank.astype(BF16), spread)
        wide_ref[source] = jnp.where(level < wide, wide, 0.0)
    copies[1].wait()
    copies[2].wait()


def side_by_side_kernel(*refs):
    pieces, out_ref = refs[:-1], refs[-1]
    size = pieces[0].shape[0]
    for k, piece in enumerate(pieces):
        out_ref[k * size : (k + 1) * size, :] = piece[...]


def weights_kernel(heights, size, start, *refs):
    begun = start > 0
    sources, rest = refs[:9], refs[9:]
    near_hbm, state_hbm, begun_ref = rest[:3] if begun else (None, None, None)
    rest = rest[4:] if begun else rest[1:]
    numbers_ref, matrix_ref = rest[:2]
    near_ref, state_ref = rest[2:4] if begun else (None, None)
    vectors, lists, sems = rest[-5], rest[-4:-1], rest[-1]
    targets = [vectors.at[k] for k in range(6)] + list(lists)
    copies = start_copies(list(zip(sources, targets)), sems)
    large = [(near_hbm, near_ref), (state_hbm, state_ref)] if begun else []
    large = start_copies(large, sems, len(targets))
    if begun:
        numbers_ref[:start, :] = begun_ref[...]
    count_ref, bricks_ref, weight_ref = lists
    slots = bricks_ref.shape[0]
    col = lax.axis_index("col")
    height, core = lax.div(col, 2).astype(F32), lax.rem(col, 2).astype(F32)
    group, lanes, unrolled = 16, 128, 8
    for copy in copies:
        copy.wait()

    @pl.loop(0, matrix_ref.shape[1] // lanes)
    def _(n):
        own_at = rows_at(n, lanes)
        at = pl.ds(pl.multiple_of(start + n * lanes, lanes), lanes)
        load, normal, direct, evolution, distance, stiffness = (vectors[k, :, at] for k in range(6))
        rows = [load, normal, 1.0 / direct, 1.0 / evolution, evolution / distance, stiffness, load, normal]
        numbers_ref[at if begun else own_at, :] = jnp.concatenate(rows, axis=0).T
        bricks = bricks_ref[:, at].astype(F32)
        live = lax.broadcasted_iota(jnp.int32, (slots, lanes), 0) < count_ref[:, at]
        weights = jnp.where(live, weight_ref[:, at], 0.0)
        merged = jnp.zeros((slots, lanes), F32)
        for k in range(slots):
            merged = merged + jnp.where(bricks == bricks[k : k + 1], weights[k : k + 1], 0.0)
        shares = merged / jnp.sum(weights, axis=0, keepdims=True)
        owner = jnp.floor((bricks + 0.5) * (1.0 / size))
        chip = jnp.floor(owner * 0.5 + 0.25)
        away = height - chip
        away = jnp.where(away < 0, away + heights, away)
        other = jnp.where(owner - 2.0 * chip == core, 0.0, float(heights))
        place = jnp.where(live, (other + away - owner) * size + bricks, -1.0)
        high = jnp.floor((place + 0.5) * (1.0 / group))
        low = place - high * group
        spread = lambda rows, k: jnp.broadcast_to(rows[k : k + 1], (group, lanes)).astype(BF16)
        line = lax.broadcasted_iota(jnp.int32, (group, lanes), 0).astype(F32).astype(BF16)
        none = jnp.full((group, lanes), -1.0, BF16)
        highs = [jnp.where(spread(low, k) == line, spread(high, k), none) for k in range(slots)]
        values = [spread(shares, k) for k in range(slots)]

        @pl.loop(0, matrix_ref.shape[0] // (group * unrolled))
        def _(m):
            first = jnp.full((group, lanes), (m * unrolled).astype(F32)).astype(BF16)
            for step in range(unrolled):
                here = first + jnp.asarray(step, BF16)
                tile = jnp.zeros((group, lanes), BF16)
                for k in range(slots):
                    tile = jnp.where(highs[k] == here, values[k], tile)
                to = pl.ds(pl.multiple_of((m * unrolled + step) * group, group), group)
                matrix_ref[to, own_at] = tile

    for copy in large:
        copy.wait()


def couple_kernel(sources, heights, flip, matrix_ref, *refs):
    coeffs, edges, out_ref = refs[:sources], refs[sources:-1], refs[-1]
    share = coeffs[0].shape[0]
    row, col = lax.axis_index("row"), lax.axis_index("col")
    height, core = lax.div(col, 2), lax.rem(col + flip, 2)

    @pl.loop(0, heights, unroll=True)
    def _(d):
        partner = lax.rem(d, 2) * (1 - 2 * lax.rem(height, 2))
        at = rows_at(2 * lax.rem(height + partner + d - lax.rem(d, 2) + heights, heights) + core, share)
        total = None
        for step in range(sources):
            term = dot(matrix_ref[lax.rem(row + (sources - step), sources), at, :], coeffs[step][...])
            total = term if total is None else total + term
        out_ref[rows_at(d, share), :] = total.astype(out_ref.dtype)

    for edge in edges:
        out_ref[heights * share :, :] = edge[...]


def couple(flip, matrix, coeffs, heights, kind, *edges):
    share, ens = coeffs[0].shape
    return call(
        functools.partial(couple_kernel, len(coeffs), heights, flip),
        jax.ShapeDtypeStruct((heights * share + len(edges) * BS, ens), kind),
        matrix,
        *coeffs,
        *edges,
    )


def chip_sum_kernel(kept_ref, sent_ref, own_ref, direct_ref, pass_ref, keep_ref):
    share = own_ref.shape[0]
    group = 32
    for place in range(2 + 2 * (keep_ref.shape[0] // share)):
        far = place // 2 - 1
        out_ref = (own_ref, direct_ref)[place % 2] if far < 0 else (keep_ref, pass_ref)[place % 2]

        @pl.loop(0, share // group)
        def _(n):
            at = pl.ds(pl.multiple_of(place * share + n * group, group), group)
            to = pl.ds(pl.multiple_of(max(far, 0) * share + n * group, group), group)
            out_ref[to, :] = (kept_ref[at, :] + sent_ref[at, :].astype(F32)).astype(out_ref.dtype)


def chip_sum(kept, sent, heights):
    rows, ens = kept.shape
    share = rows // heights
    far = (heights // 2 - 1) * share
    shapes = [(share, BF16), (share, BF16), (far, BF16), (far, F32)]
    return call(chip_sum_kernel, [jax.ShapeDtypeStruct((n, ens), kind) for n, kind in shapes], kept, sent)


def pair_sum_kernel(keep_ref, came_ref, *outs):
    share = outs[0].shape[0]
    group = 32
    for far, out_ref in enumerate(outs):

        @pl.loop(0, share // group)
        def _(n):
            at = pl.ds(pl.multiple_of(far * share + n * group, group), group)
            out_ref[rows_at(n, group), :] = (keep_ref[at, :] + came_ref[at, :].astype(F32)).astype(BF16)


def near_tau(n, slip, numbers, near_ref, rounded_ref):
    count = rounded_ref.shape[0] // BS
    at = rows_at(n, BS)
    none = jnp.zeros((BS, rounded_ref.shape[1]), BF16)
    before = jnp.where(n == 0, none, rounded_ref[rows_at(jnp.maximum(n - 1, 0), BS), :])
    after = jnp.where(n == count - 1, none, rounded_ref[rows_at(jnp.minimum(n + 1, count - 1), BS), :])
    near = dot(near_ref[0, at, :], before) + dot(near_ref[1, at, :], rounded_ref[at, :]) + dot(near_ref[2, at, :], after)
    return numbers[:, 0:1] - numbers[:, 5:6] * slip - near


def prepare_first_kernel(
    low_ref, high_ref, own_ref, other_ref, slip_ref, state_ref, numbers_ref, near_ref, rounded_ref,
    shift_ref, scale_ref, rest_ref, scale_mid_ref,
):
    half = own_ref.shape[0]
    ens = slip_ref.shape[1]
    blocks = low_ref.shape[1] // BS

    def block(matrix_ref, m, n):
        at, own_at = rows_at(n, BS), rows_at(m, BS)
        total = dot_t(matrix_ref[:half, own_at], own_ref[...]) + dot_t(matrix_ref[half:, own_at], other_ref[...])
        numbers = numbers_ref[at, :]
        normal, inv_direct, inv_evolution, ratio = (numbers[:, k : k + 1] for k in range(1, 5))
        base = total[:, :ens]
        scale = inv_direct / (normal - base)
        scale_ref[at, :] = scale
        scale_mid_ref[at, :] = inv_direct / (normal - (base + STEP_SIZE * total[:, ens:]))
        state = state_ref[at, :]
        tau = near_tau(n, slip_ref[at, :], numbers, near_ref, rounded_ref)
        shift_ref[at, :] = tau * scale - state * inv_direct
        rest_ref[at, :] = state + (STEP_SIZE * ratio) * jnp.exp((REF_FRICTION - state) * inv_evolution)

    @pl.loop(0, blocks)
    def _(m):
        block(low_ref, m, m)

    @pl.loop(0, blocks)
    def _(m):
        block(high_ref, m, blocks + m)


def over_blocks(block, basis_ref, near_ref, parts, pair_ref, cross_ref):
    count = near_ref.shape[1] // BS

    def far(n):
        levels = rows_at(n, R)
        total = parts[0][levels, :].astype(F32)
        for part in parts[1:]:
            total = total + part[levels, :].astype(F32)
        return dot_t(basis_ref[:, rows_at(n, BS)], total.astype(BF16))

    even = lax.rem(lax.axis_index("col"), 2) == 0
    pair, cross = pair_ref[-BS:], cross_ref[...]
    block(0, far(0) + dot(near_ref[0, :BS, :], jnp.where(even, cross, pair)))

    @pl.loop(1, count - 1, unroll=True)
    def _(n):
        block(n, far(n))

    block(count - 1, far(count - 1) + dot(near_ref[2, -BS:, :], jnp.where(even, pair, cross)))


def finish_first_kernel(
    count, shift_ref, scale_ref, slip_ref, basis_out_ref, basis_in_ref, near_ref, *refs
):
    parts, pair_ref, cross_ref = refs[:count], refs[count], refs[count + 1]
    speed_ref, rounded_ref, coeff_ref, pair_out, cross_out = refs[count + 2 :]

    def block(n, outer):
        at = rows_at(n, BS)
        speed = jnp.exp(shift_ref[at, :] - scale_ref[at, :] * outer)
        speed_ref[at, :] = speed
        rounded = (slip_ref[at, :] + STEP_SIZE * speed).astype(BF16)
        rounded_ref[at, :] = rounded
        coeff_ref[rows_at(n, R), :] = dot(basis_in_ref[:, at], rounded).astype(BF16)

    over_blocks(block, basis_out_ref, near_ref, parts, pair_ref, cross_ref)
    fill_edges(rounded_ref[:BS], rounded_ref[-BS:], pair_out, cross_out)


def prepare_second_kernel(
    slip_ref, state_ref, speed_ref, part_ref, scale_ref, numbers_ref, near_ref, rounded_ref,
    shift_ref, slip_rest_ref, rest_ref,
):
    @pl.loop(0, slip_ref.shape[0] // BS)
    def _(n):
        at = rows_at(n, BS)
        numbers = numbers_ref[at, :]
        inv_direct, inv_evolution, ratio = (numbers[:, k : k + 1] for k in range(2, 5))
        speed = speed_ref[at, :]
        slip = slip_ref[at, :] + STEP_SIZE * speed
        state = part_ref[at, :] - (STEP_SIZE * ratio) * speed
        tau = near_tau(n, slip, numbers, near_ref, rounded_ref)
        shift_ref[at, :] = tau * scale_ref[at, :] - state * inv_direct
        slip_rest_ref[at, :] = 0.5 * (slip_ref[at, :] + slip)
        friction = jnp.exp((REF_FRICTION - state) * inv_evolution)
        rest_ref[at, :] = 0.5 * (state_ref[at, :] + state) + (0.5 * STEP_SIZE * ratio) * friction


def finish_second_kernel(
    count, shift_ref, scale_ref, rest_ref, slip_rest_ref, numbers_ref, basis_out_ref, near_ref, *refs
):
    parts, pair_ref, cross_ref = refs[:count], refs[count], refs[count + 1]
    slip_hbm, state_hbm, slip_ref, state_ref, sems = refs[count + 2 :]

    def copies(n):
        at = rows_at(n, BS)
        return [
            pltpu.make_async_copy(slip_ref.at[at, :], slip_hbm.at[at, :], sems.at[0, n]),
            pltpu.make_async_copy(state_ref.at[at, :], state_hbm.at[at, :], sems.at[1, n]),
        ]

    def block(n, outer):
        at = rows_at(n, BS)
        speed = jnp.exp(shift_ref[at, :] - scale_ref[at, :] * outer)
        slip_ref[at, :] = slip_rest_ref[at, :] + (0.5 * STEP_SIZE) * speed
        state_ref[at, :] = rest_ref[at, :] - (0.5 * STEP_SIZE * numbers_ref[at, 4:5]) * speed
        for copy in copies(n):
            copy.start()

    over_blocks(block, basis_out_ref, near_ref, parts, pair_ref, cross_ref)

    @pl.loop(0, slip_ref.shape[0] // BS)
    def _(n):
        for copy in copies(n):
            copy.wait()


def masked_coupling(coupling, wide):
    rows, sources, width = coupling.shape
    blocks = rows // R
    keep = jnp.arange(R, dtype=jnp.int32).astype(F32)[None, None, :, None] < wide[:, :, None, :]
    matrix = jnp.transpose(coupling, (1, 0, 2)).reshape(sources, blocks, R, width)
    masked = jnp.where(keep, matrix, jnp.zeros((), BF16)).reshape(sources, rows, width)
    return pltpu.with_memory_space_constraint(masked, pltpu.VMEM)


def per_device(
    slip,
    state,
    tau_load,
    normal_stress,
    direct_effect,
    evolution_effect,
    slip_distance,
    self_stiffness,
    near_blocks,
    basis_in,
    basis_out,
    coupling,
    block_rank,
    adj_bricks,
    adj_count,
    adj_weight,
    pressure_now,
    pressure_rate,
):
    row_count = lax.axis_size("row")
    col_count = lax.axis_size("col")
    row_index = lax.axis_index("row")
    col_index = lax.axis_index("col")
    heights = col_count // 2
    height, core = col_index // 2, col_index % 2
    both = ("row", "col")
    devices = row_count * col_count

    def to_row(array, d):
        return lax.ppermute(array, "row", [(i, (i + d) % row_count) for i in range(row_count)])

    def to_height(array, d):
        pairs = [(2 * z + k, 2 * ((z + d) % heights) + k) for z in range(heights) for k in range(2)]
        return lax.ppermute(array, "col", pairs)

    def to_core(array):
        return lax.ppermute(array, "col", [(2 * z + k, 2 * z + 1 - k) for z in range(heights) for k in range(2)])

    def to_chip(array):
        ends = [(i, i + 1) for i in range(1, devices - 1, 2)]
        return lax.ppermute(array, both, ends + [(j, i) for i, j in ends])

    patches, ens = slip.shape
    slots = adj_bricks.shape[0]
    size = pressure_now.shape[0]
    share = coupling.shape[2]
    def to_partner(array):
        pairs = [(2 * z + k, 2 * (z + 1 - 2 * (z % 2)) + k) for z in range(heights) for k in range(2)]
        return lax.ppermute(array, "col", pairs)

    def first_step(coeffs, pair, cross):
        sent = to_core(couple(1, masked, coeffs, heights, BF16, pair))
        kept = couple(0, masked, coeffs, heights, F32)
        own, direct, passed, keep = chip_sum(kept, sent, heights)
        return own, to_partner(passed), to_partner(direct), keep, sent, cross

    def second_step(own, came, direct, keep, sent, cross):
        sums = call(pair_sum_kernel, [jax.ShapeDtypeStruct((share, ens), BF16)] * (heights // 2 - 1), keep, came)
        sums, cross = lax.optimization_barrier((sums, cross))
        return [to_height(part, 2 * (d + 1)) for d, part in enumerate(sums)] + [own, direct, sent, to_chip(cross)]

    def row_coeffs(coeff):
        return [coeff] + [to_row(coeff, d) for d in range(1, row_count)]

    full = jax.ShapeDtypeStruct((patches, ens), F32)
    half = jax.ShapeDtypeStruct((patches, ens), BF16)
    edge = jax.ShapeDtypeStruct((BS, ens), BF16)
    per_patch = [tau_load, normal_stress, direct_effect, evolution_effect, slip_distance, self_stiffness]

    ranks = jnp.transpose(block_rank, (1, 2, 0))
    wide, joined = call(
        functools.partial(ranks_kernel, col_count),
        [
            jax.ShapeDtypeStruct((ranks.shape[0], ranks.shape[2], share), F32),
            jax.ShapeDtypeStruct((size, 2 * ens), BF16),
        ],
        *in_hbm(ranks, pressure_now, pressure_rate),
        specs=[HBM] * 3,
        scratch_shapes=[pltpu.VMEM(ranks.shape, jnp.int32), pltpu.SemaphoreType.DMA((3,))],
    )
    fields = [joined] + [to_height(joined, d) for d in range(1, heights)]
    masked = masked_coupling(coupling, wide)
    masked, slip = lax.optimization_barrier((masked, slip))
    coeff, rounded, pair, cross, slip = project(slip, basis_in)
    coeffs = row_coeffs(coeff)
    brick_lists = [adj_count[None], adj_bricks, adj_weight]
    columns = [array[None] for array in per_patch] + brick_lists
    start = patches // 2
    part = jax.ShapeDtypeStruct((2 * heights * size, start), BF16)
    scratch = [
        pltpu.VMEM((6, 1, patches), F32),
        pltpu.VMEM((1, patches), jnp.int32),
        pltpu.VMEM(adj_bricks.shape, jnp.int32),
        pltpu.VMEM(adj_weight.shape, F32),
        pltpu.SemaphoreType.DMA((11,)),
    ]
    numbers, low = call(
        functools.partial(weights_kernel, heights, size, 0),
        [jax.ShapeDtypeStruct((start, 8), F32), part],
        *in_hbm(*columns),
        coeff,
        specs=[HBM] * 9 + [VMEM],
        scratch_shapes=scratch,
    )
    fields, coeffs, low = lax.optimization_barrier((fields, coeffs, low))
    own = call(
        side_by_side_kernel, jax.ShapeDtypeStruct((heights * size, 2 * ens), BF16), *fields
    )
    other = to_core(own)
    own_part, came, direct, keep, sent, cross = first_step(coeffs, pair, cross)
    numbers, high, near, state = call(
        functools.partial(weights_kernel, heights, size, start),
        [jax.ShapeDtypeStruct((patches, 8), F32), part, jax.ShapeDtypeStruct(near_blocks.shape, BF16), full],
        *in_hbm(*columns, near_blocks, state),
        numbers,
        own_part,
        specs=[HBM] * 11 + [VMEM] * 2,
        scratch_shapes=scratch,
    )
    came, high = lax.optimization_barrier((came, high))
    outer = second_step(own_part, came, direct, keep, sent, cross)
    shift, scale, rest, scale_mid = call(
        prepare_first_kernel, [full] * 4, low, high, own, other, slip, state, numbers, near, rounded
    )
    speed, rounded, coeff, pair, cross = call(
        functools.partial(finish_first_kernel, len(outer) - 2),
        [full, half, jax.ShapeDtypeStruct((patches // BS * R, ens), BF16), edge, edge],
        shift, scale, slip, basis_out, basis_in, near, *outer,
    )
    coeffs = row_coeffs(coeff)
    outer = second_step(*first_step(coeffs, pair, cross))
    shift, slip_rest, rest = call(
        prepare_second_kernel, [full] * 3,
        slip, state, speed, rest, scale_mid, numbers, near, rounded,
    )
    slip_out, state_out = call(
        functools.partial(finish_second_kernel, len(outer) - 2),
        [full] * 2,
        shift, scale_mid, rest, slip_rest, numbers, basis_out, near, *outer,
        out_specs=[HBM] * 2,
        scratch_shapes=[
            pltpu.VMEM((patches, ens), F32),
            pltpu.VMEM((patches, ens), F32),
            pltpu.SemaphoreType.DMA((2, patches // BS)),
        ],
    )
    return (slip_out, state_out)


def solution(mesh):
    in_specs = (
        P(("row", "col"), None),
        P(("row", "col"), None),
        P(("row", "col")),
        P(("row", "col")),
        P(("row", "col")),
        P(("row", "col")),
        P(("row", "col")),
        P(("row", "col")),
        P(None, ("row", "col"), None),
        P(None, ("row", "col")),
        P(None, ("row", "col")),
        P("row", None, "col"),
        P("row", None, "col"),
        P(None, ("row", "col")),
        P(("row", "col")),
        P(None, ("row", "col")),
        P("col", None),
        P("col", None),
    )
    out_specs = (P(("row", "col"), None), P(("row", "col"), None))
    return jax.shard_map(
        per_device, mesh=mesh, in_specs=in_specs, out_specs=out_specs, check_vma=False
    )
```

```python
import functools

import jax
import jax.numpy as jnp
from jax import lax
from jax.experimental import pallas as pl
from jax.experimental.pallas import tpu as pltpu
from jax.sharding import PartitionSpec as P

BS = 256
R = 32

STEP_SIZE = 0.5
REF_FRICTION = 0.6
LIMIT = 16 * 1024 * 1024
F32 = jnp.float32
BF16 = jnp.bfloat16


def dot(a, b):
    return jnp.dot(a, b, preferred_element_type=F32)


def dot_t(a, b):
    return lax.dot_general(a, b, (((0,), (0,)), ((), ())), preferred_element_type=F32)


VMEM = pl.BlockSpec(memory_space=pltpu.VMEM)


def call(kernel, outs, *operands, specs=None, **grid):
    return pl.pallas_call(
        kernel,
        in_specs=specs or [VMEM] * len(operands),
        out_shape=outs,
        compiler_params=pltpu.CompilerParams(vmem_limit_bytes=LIMIT),
        **grid,
    )(*operands)


def rows_at(n, size):
    return pl.ds(pl.multiple_of(n * size, size), size)


HBM = pl.BlockSpec(memory_space=pl.ANY)


def in_hbm(*arrays):
    return [pltpu.with_memory_space_constraint(array, pltpu.HBM) for array in arrays]


def start_copies(pairs, sems, first=0):
    copies = [pltpu.make_async_copy(a, b, sems.at[first + k]) for k, (a, b) in enumerate(pairs)]
    for copy in copies:
        copy.start()
    return copies


def fill_edges(first, last, pair_ref, cross_ref):
    even = lax.rem(lax.axis_index("col"), 2) == 0
    pair_ref[...] = jnp.where(even, last, first)
    cross_ref[...] = jnp.where(even, first, last)


def project_kernel(slip_hbm, basis_hbm, coeff_ref, rounded_ref, pair_ref, cross_ref, slip_ref, basis_ref, sems):
    count = slip_ref.shape[0] // BS
    blocks = [pl.ds(n * BS, BS) for n in range(count)]
    copies = start_copies(
        [(basis_hbm, basis_ref)] + [(slip_hbm.at[at, :], slip_ref.at[at, :]) for at in blocks], sems
    )
    copies[0].wait()
    for n, at in enumerate(blocks):
        copies[1 + n].wait()
        rounded = slip_ref[at, :].astype(BF16)
        rounded_ref[at, :] = rounded
        coeff_ref[n * R : (n + 1) * R, :] = dot(basis_ref[:, at], rounded).astype(BF16)
    fill_edges(rounded_ref[:BS], rounded_ref[-BS:], pair_ref, cross_ref)


def project(slip, basis_in):
    patches, ens = slip.shape
    count = patches // BS
    edge = jax.ShapeDtypeStruct((BS, ens), BF16)
    return call(
        project_kernel,
        [
            jax.ShapeDtypeStruct((count * R, ens), BF16),
            jax.ShapeDtypeStruct((patches, ens), BF16),
            edge,
            edge,
            jax.ShapeDtypeStruct((patches, ens), F32),
        ],
        *in_hbm(slip, basis_in),
        specs=[HBM] * 2,
        scratch_shapes=[pltpu.VMEM(basis_in.shape, BF16), pltpu.SemaphoreType.DMA((1 + count,))],
    )


def ranks_kernel(
    col_count, rank_hbm, now_hbm, rate_hbm, wide_ref, joined_ref, rank_ref, sems
):
    sources, share, blocks = rank_ref.shape
    ens = now_hbm.shape[1]
    copies = start_copies(
        [
            (rank_hbm, rank_ref),
            (now_hbm, joined_ref.at[:, pl.ds(0, ens)]),
            (rate_hbm, joined_ref.at[:, pl.ds(ens, ens)]),
        ],
        sems,
    )
    width = share * R
    column = lax.broadcasted_iota(jnp.int32, (share, width), 1)
    spread = (lax.div(column, R) == lax.broadcasted_iota(jnp.int32, (share, width), 0)).astype(F32).astype(BF16)
    level = lax.rem(lax.broadcasted_iota(jnp.int32, (blocks, width), 1), R).astype(F32)
    receiver = lax.axis_index("row") * blocks + lax.broadcasted_iota(jnp.int32, (share, blocks), 1)
    copies[0].wait()
    for source in range(sources):
        own = (source * col_count + lax.axis_index("col")) * share + lax.broadcasted_iota(jnp.int32, (share, blocks), 0)
        rank = jnp.where(jnp.abs(receiver - own) > 1, rank_ref[source], 0).astype(F32)
        wide = dot_t(rank.astype(BF16), spread)
        wide_ref[source] = jnp.where(level < wide, wide, 0.0)
    copies[1].wait()
    copies[2].wait()


def side_by_side_kernel(*refs):
    pieces, out_ref = refs[:-1], refs[-1]
    size = pieces[0].shape[0]
    for k, piece in enumerate(pieces):
        out_ref[k * size : (k + 1) * size, :] = piece[...]


def weights_kernel(heights, size, start, *refs):
    begun = start > 0
    sources, rest = refs[:9], refs[9:]
    near_hbm, state_hbm, begun_ref = rest[:3] if begun else (None, None, None)
    rest = rest[4:] if begun else rest[1:]
    numbers_ref, matrix_ref = rest[:2]
    near_ref, state_ref = rest[2:4] if begun else (None, None)
    vectors, lists, sems = rest[-5], rest[-4:-1], rest[-1]
    targets = [vectors.at[k] for k in range(6)] + list(lists)
    copies = start_copies(list(zip(sources, targets)), sems)
    large = [(near_hbm, near_ref), (state_hbm, state_ref)] if begun else []
    large = start_copies(large, sems, len(targets))
    if begun:
        numbers_ref[:start, :] = begun_ref[...]
    count_ref, bricks_ref, weight_ref = lists
    slots = bricks_ref.shape[0]
    col = lax.axis_index("col")
    height, core = lax.div(col, 2).astype(F32), lax.rem(col, 2).astype(F32)
    group, lanes, unrolled = 16, 128, 8
    for copy in copies:
        copy.wait()

    @pl.loop(0, matrix_ref.shape[1] // lanes)
    def _(n):
        own_at = rows_at(n, lanes)
        at = pl.ds(pl.multiple_of(start + n * lanes, lanes), lanes)
        load, normal, direct, evolution, distance, stiffness = (vectors[k, :, at] for k in range(6))
        rows = [load, normal, 1.0 / direct, 1.0 / evolution, evolution / distance, stiffness, load, normal]
        numbers_ref[at if begun else own_at, :] = jnp.concatenate(rows, axis=0).T
        bricks = bricks_ref[:, at].astype(F32)
        live = lax.broadcasted_iota(jnp.int32, (slots, lanes), 0) < count_ref[:, at]
        weights = jnp.where(live, weight_ref[:, at], 0.0)
        merged = jnp.zeros((slots, lanes), F32)
        for k in range(slots):
            merged = merged + jnp.where(bricks == bricks[k : k + 1], weights[k : k + 1], 0.0)
        shares = merged / jnp.sum(weights, axis=0, keepdims=True)
        owner = jnp.floor((bricks + 0.5) * (1.0 / size))
        chip = jnp.floor(owner * 0.5 + 0.25)
        away = height - chip
        away = jnp.where(away < 0, away + heights, away)
        other = jnp.where(owner - 2.0 * chip == core, 0.0, float(heights))
        place = jnp.where(live, (other + away - owner) * size + bricks, -1.0)
        high = jnp.floor((place + 0.5) * (1.0 / group))
        low = place - high * group
        spread = lambda rows, k: jnp.broadcast_to(rows[k : k + 1], (group, lanes)).astype(BF16)
        line = lax.broadcasted_iota(jnp.int32, (group, lanes), 0).astype(F32).astype(BF16)
        none = jnp.full((group, lanes), -1.0, BF16)
        highs = [jnp.where(spread(low, k) == line, spread(high, k), none) for k in range(slots)]
        values = [spread(shares, k) for k in range(slots)]

        @pl.loop(0, matrix_ref.shape[0] // (group * unrolled))
        def _(m):
            first = jnp.full((group, lanes), (m * unrolled).astype(F32)).astype(BF16)
            for step in range(unrolled):
                here = first + jnp.asarray(step, BF16)
                tile = jnp.zeros((group, lanes), BF16)
                for k in range(slots):
                    tile = jnp.where(highs[k] == here, values[k], tile)
                to = pl.ds(pl.multiple_of((m * unrolled + step) * group, group), group)
                matrix_ref[to, own_at] = tile

    for copy in large:
        copy.wait()


def couple_kernel(sources, heights, flip, matrix_ref, *refs):
    coeffs, edges, out_ref = refs[:sources], refs[sources:-1], refs[-1]
    share = coeffs[0].shape[0]
    row, col = lax.axis_index("row"), lax.axis_index("col")
    height, core = lax.div(col, 2), lax.rem(col + flip, 2)

    @pl.loop(0, heights, unroll=True)
    def _(d):
        partner = lax.rem(d, 2) * (1 - 2 * lax.rem(height, 2))
        at = rows_at(2 * lax.rem(height + partner + d - lax.rem(d, 2) + heights, heights) + core, share)
        total = None
        for step in range(sources):
            term = dot(matrix_ref[lax.rem(row + (sources - step), sources), at, :], coeffs[step][...])
            total = term if total is None else total + term
        out_ref[rows_at(d, share), :] = total.astype(out_ref.dtype)

    for edge in edges:
        out_ref[heights * share :, :] = edge[...]


def couple(flip, matrix, coeffs, heights, kind, *edges):
    share, ens = coeffs[0].shape
    return call(
        functools.partial(couple_kernel, len(coeffs), heights, flip),
        jax.ShapeDtypeStruct((heights * share + len(edges) * BS, ens), kind),
        matrix,
        *coeffs,
        *edges,
    )


def chip_sum_kernel(kept_ref, sent_ref, own_ref, direct_ref, pass_ref, keep_ref):
    share = own_ref.shape[0]
    group = 32
    for place in range(2 + 2 * (keep_ref.shape[0] // share)):
        far = place // 2 - 1
        out_ref = (own_ref, direct_ref)[place % 2] if far < 0 else (keep_ref, pass_ref)[place % 2]

        @pl.loop(0, share // group)
        def _(n):
            at = pl.ds(pl.multiple_of(place * share + n * group, group), group)
            to = pl.ds(pl.multiple_of(max(far, 0) * share + n * group, group), group)
            out_ref[to, :] = (kept_ref[at, :] + sent_ref[at, :].astype(F32)).astype(out_ref.dtype)


def chip_sum(kept, sent, heights):
    rows, ens = kept.shape
    share = rows // heights
    far = (heights // 2 - 1) * share
    shapes = [(share, BF16), (share, BF16), (far, BF16), (far, F32)]
    return call(chip_sum_kernel, [jax.ShapeDtypeStruct((n, ens), kind) for n, kind in shapes], kept, sent)


def pair_sum_kernel(keep_ref, came_ref, *outs):
    share = outs[0].shape[0]
    group = 32
    for far, out_ref in enumerate(outs):

        @pl.loop(0, share // group)
        def _(n):
            at = pl.ds(pl.multiple_of(far * share + n * group, group), group)
            out_ref[rows_at(n, group), :] = (keep_ref[at, :] + came_ref[at, :].astype(F32)).astype(BF16)


def near_tau(n, slip, numbers, near_ref, rounded_ref):
    count = rounded_ref.shape[0] // BS
    at = rows_at(n, BS)
    none = jnp.zeros((BS, rounded_ref.shape[1]), BF16)
    before = jnp.where(n == 0, none, rounded_ref[rows_at(jnp.maximum(n - 1, 0), BS), :])
    after = jnp.where(n == count - 1, none, rounded_ref[rows_at(jnp.minimum(n + 1, count - 1), BS), :])
    near = dot(near_ref[0, at, :], before) + dot(near_ref[1, at, :], rounded_ref[at, :]) + dot(near_ref[2, at, :], after)
    return numbers[:, 0:1] - numbers[:, 5:6] * slip - near


def prepare_first_kernel(
    low_ref, high_ref, own_ref, other_ref, slip_ref, state_ref, numbers_ref, near_ref, rounded_ref,
    shift_ref, scale_ref, rest_ref, scale_mid_ref,
):
    half = own_ref.shape[0]
    ens = slip_ref.shape[1]
    blocks = low_ref.shape[1] // BS

    def block(matrix_ref, m, n):
        at, own_at = rows_at(n, BS), rows_at(m, BS)
        total = dot_t(matrix_ref[:half, own_at], own_ref[...]) + dot_t(matrix_ref[half:, own_at], other_ref[...])
        numbers = numbers_ref[at, :]
        normal, inv_direct, inv_evolution, ratio = (numbers[:, k : k + 1] for k in range(1, 5))
        base = total[:, :ens]
        scale = inv_direct / (normal - base)
        scale_ref[at, :] = scale
        scale_mid_ref[at, :] = inv_direct / (normal - (base + STEP_SIZE * total[:, ens:]))
        state = state_ref[at, :]
        tau = near_tau(n, slip_ref[at, :], numbers, near_ref, rounded_ref)
        shift_ref[at, :] = tau * scale - state * inv_direct
        rest_ref[at, :] = state + (STEP_SIZE * ratio) * jnp.exp((REF_FRICTION - state) * inv_evolution)

    @pl.loop(0, blocks)
    def _(m):
        block(low_ref, m, m)

    @pl.loop(0, blocks)
    def _(m):
        block(high_ref, m, blocks + m)


def over_blocks(block, basis_ref, near_ref, parts, pair_ref, cross_ref):
    count = near_ref.shape[1] // BS

    def far(n):
        levels = rows_at(n, R)
        total = parts[0][levels, :].astype(F32)
        for part in parts[1:]:
            total = total + part[levels, :].astype(F32)
        return dot_t(basis_ref[:, rows_at(n, BS)], total.astype(BF16))

    even = lax.rem(lax.axis_index("col"), 2) == 0
    pair, cross = pair_ref[-BS:], cross_ref[...]
    block(0, far(0) + dot(near_ref[0, :BS, :], jnp.where(even, cross, pair)))

    @pl.loop(1, count - 1, unroll=True)
    def _(n):
        block(n, far(n))

    block(count - 1, far(count - 1) + dot(near_ref[2, -BS:, :], jnp.where(even, pair, cross)))


def finish_first_kernel(
    count, shift_ref, scale_ref, slip_ref, basis_out_ref, basis_in_ref, near_ref, *refs
):
    parts, pair_ref, cross_ref = refs[:count], refs[count], refs[count + 1]
    speed_ref, rounded_ref, coeff_ref, pair_out, cross_out = refs[count + 2 :]

    def block(n, outer):
        at = rows_at(n, BS)
        speed = jnp.exp(shift_ref[at, :] - scale_ref[at, :] * outer)
        speed_ref[at, :] = speed
        rounded = (slip_ref[at, :] + STEP_SIZE * speed).astype(BF16)
        rounded_ref[at, :] = rounded
        coeff_ref[rows_at(n, R), :] = dot(basis_in_ref[:, at], rounded).astype(BF16)

    over_blocks(block, basis_out_ref, near_ref, parts, pair_ref, cross_ref)
    fill_edges(rounded_ref[:BS], rounded_ref[-BS:], pair_out, cross_out)


def prepare_second_kernel(
    slip_ref, state_ref, speed_ref, part_ref, scale_ref, numbers_ref, near_ref, rounded_ref,
    shift_ref, slip_rest_ref, rest_ref,
):
    @pl.loop(0, slip_ref.shape[0] // BS)
    def _(n):
        at = rows_at(n, BS)
        numbers = numbers_ref[at, :]
        inv_direct, inv_evolution, ratio = (numbers[:, k : k + 1] for k in range(2, 5))
        speed = speed_ref[at, :]
        slip = slip_ref[at, :] + STEP_SIZE * speed
        state = part_ref[at, :] - (STEP_SIZE * ratio) * speed
        tau = near_tau(n, slip, numbers, near_ref, rounded_ref)
        shift_ref[at, :] = tau * scale_ref[at, :] - state * inv_direct
        slip_rest_ref[at, :] = 0.5 * (slip_ref[at, :] + slip)
        friction = jnp.exp((REF_FRICTION - state) * inv_evolution)
        rest_ref[at, :] = 0.5 * (state_ref[at, :] + state) + (0.5 * STEP_SIZE * ratio) * friction


def finish_second_kernel(
    count, shift_ref, scale_ref, rest_ref, slip_rest_ref, numbers_ref, basis_out_ref, near_ref, *refs
):
    parts, pair_ref, cross_ref = refs[:count], refs[count], refs[count + 1]
    slip_hbm, state_hbm, slip_ref, state_ref, sems = refs[count + 2 :]

    def copies(n):
        at = rows_at(n, BS)
        return [
            pltpu.make_async_copy(slip_ref.at[at, :], slip_hbm.at[at, :], sems.at[0, n]),
            pltpu.make_async_copy(state_ref.at[at, :], state_hbm.at[at, :], sems.at[1, n]),
        ]

    def block(n, outer):
        at = rows_at(n, BS)
        speed = jnp.exp(shift_ref[at, :] - scale_ref[at, :] * outer)
        slip_ref[at, :] = slip_rest_ref[at, :] + (0.5 * STEP_SIZE) * speed
        state_ref[at, :] = rest_ref[at, :] - (0.5 * STEP_SIZE * numbers_ref[at, 4:5]) * speed
        for copy in copies(n):
            copy.start()

    over_blocks(block, basis_out_ref, near_ref, parts, pair_ref, cross_ref)

    @pl.loop(0, slip_ref.shape[0] // BS)
    def _(n):
        for copy in copies(n):
            copy.wait()


def masked_coupling(coupling, wide):
    rows, sources, width = coupling.shape
    blocks = rows // R
    keep = jnp.arange(R, dtype=jnp.int32).astype(F32)[None, None, :, None] < wide[:, :, None, :]
    matrix = jnp.transpose(coupling, (1, 0, 2)).reshape(sources, blocks, R, width)
    masked = jnp.where(keep, matrix, jnp.zeros((), BF16)).reshape(sources, rows, width)
    return pltpu.with_memory_space_constraint(masked, pltpu.VMEM)


def per_device(
    slip,
    state,
    tau_load,
    normal_stress,
    direct_effect,
    evolution_effect,
    slip_distance,
    self_stiffness,
    near_blocks,
    basis_in,
    basis_out,
    coupling,
    block_rank,
    adj_bricks,
    adj_count,
    adj_weight,
    pressure_now,
    pressure_rate,
):
    row_count = lax.axis_size("row")
    col_count = lax.axis_size("col")
    row_index = lax.axis_index("row")
    col_index = lax.axis_index("col")
    heights = col_count // 2
    height, core = col_index // 2, col_index % 2
    both = ("row", "col")
    devices = row_count * col_count

    def to_row(array, d):
        return lax.ppermute(array, "row", [(i, (i + d) % row_count) for i in range(row_count)])

    def to_height(array, d):
        pairs = [(2 * z + k, 2 * ((z + d) % heights) + k) for z in range(heights) for k in range(2)]
        return lax.ppermute(array, "col", pairs)

    def to_core(array):
        return lax.ppermute(array, "col", [(2 * z + k, 2 * z + 1 - k) for z in range(heights) for k in range(2)])

    def to_chip(array):
        ends = [(i, i + 1) for i in range(1, devices - 1, 2)]
        return lax.ppermute(array, both, ends + [(j, i) for i, j in ends])

    patches, ens = slip.shape
    slots = adj_bricks.shape[0]
    size = pressure_now.shape[0]
    share = coupling.shape[2]
    def to_partner(array):
        pairs = [(2 * z + k, 2 * (z + 1 - 2 * (z % 2)) + k) for z in range(heights) for k in range(2)]
        return lax.ppermute(array, "col", pairs)

    def first_step(coeffs, pair, cross, later):
        sent = to_core(couple(1, masked, coeffs, heights, BF16, pair))
        kept = couple(0, masked, coeffs, heights, F32)
        own, direct, passed, keep = chip_sum(kept, sent, heights)
        if not later:
            own, cross = lax.optimization_barrier((own, cross))
        return own, to_partner(passed), to_partner(direct), keep, sent, cross if later else to_chip(cross)

    def second_step(own, came, direct, keep, sent, cross, later):
        sums = call(pair_sum_kernel, [jax.ShapeDtypeStruct((share, ens), BF16)] * (heights // 2 - 1), keep, came)
        if later:
            sums, cross = lax.optimization_barrier((sums, cross))
            cross = to_chip(cross)
        return [to_height(part, 2 * (d + 1)) for d, part in enumerate(sums)] + [own, direct, sent, cross]

    def row_coeffs(coeff):
        return [coeff] + [to_row(coeff, d) for d in range(1, row_count)]

    full = jax.ShapeDtypeStruct((patches, ens), F32)
    half = jax.ShapeDtypeStruct((patches, ens), BF16)
    edge = jax.ShapeDtypeStruct((BS, ens), BF16)
    per_patch = [tau_load, normal_stress, direct_effect, evolution_effect, slip_distance, self_stiffness]

    ranks = jnp.transpose(block_rank, (1, 2, 0))
    wide, joined = call(
        functools.partial(ranks_kernel, col_count),
        [
            jax.ShapeDtypeStruct((ranks.shape[0], ranks.shape[2], share), F32),
            jax.ShapeDtypeStruct((size, 2 * ens), BF16),
        ],
        *in_hbm(ranks, pressure_now, pressure_rate),
        specs=[HBM] * 3,
        scratch_shapes=[pltpu.VMEM(ranks.shape, jnp.int32), pltpu.SemaphoreType.DMA((3,))],
    )
    fields = [joined] + [to_height(joined, d) for d in range(1, heights)]
    masked = masked_coupling(coupling, wide)
    masked, slip = lax.optimization_barrier((masked, slip))
    coeff, rounded, pair, cross, slip = project(slip, basis_in)
    coeffs = row_coeffs(coeff)
    brick_lists = [adj_count[None], adj_bricks, adj_weight]
    columns = [array[None] for array in per_patch] + brick_lists
    start = patches // 2
    part = jax.ShapeDtypeStruct((2 * heights * size, start), BF16)
    scratch = [
        pltpu.VMEM((6, 1, patches), F32),
        pltpu.VMEM((1, patches), jnp.int32),
        pltpu.VMEM(adj_bricks.shape, jnp.int32),
        pltpu.VMEM(adj_weight.shape, F32),
        pltpu.SemaphoreType.DMA((11,)),
    ]
    numbers, low = call(
        functools.partial(weights_kernel, heights, size, 0),
        [jax.ShapeDtypeStruct((start, 8), F32), part],
        *in_hbm(*columns),
        coeff,
        specs=[HBM] * 9 + [VMEM],
        scratch_shapes=scratch,
    )
    fields, coeffs, low = lax.optimization_barrier((fields, coeffs, low))
    own = call(
        side_by_side_kernel, jax.ShapeDtypeStruct((heights * size, 2 * ens), BF16), *fields
    )
    other = to_core(own)
    own_part, came, direct, keep, sent, cross = first_step(coeffs, pair, cross, True)
    numbers, high, near, state = call(
        functools.partial(weights_kernel, heights, size, start),
        [jax.ShapeDtypeStruct((patches, 8), F32), part, jax.ShapeDtypeStruct(near_blocks.shape, BF16), full],
        *in_hbm(*columns, near_blocks, state),
        numbers,
        own_part,
        specs=[HBM] * 11 + [VMEM] * 2,
        scratch_shapes=scratch,
    )
    came, high = lax.optimization_barrier((came, high))
    outer = second_step(own_part, came, direct, keep, sent, cross, True)
    shift, scale, rest, scale_mid = call(
        prepare_first_kernel, [full] * 4, low, high, own, other, slip, state, numbers, near, rounded
    )
    speed, rounded, coeff, pair, cross = call(
        functools.partial(finish_first_kernel, len(outer) - 2),
        [full, half, jax.ShapeDtypeStruct((patches // BS * R, ens), BF16), edge, edge],
        shift, scale, slip, basis_out, basis_in, near, *outer,
    )
    coeffs = row_coeffs(coeff)
    outer = second_step(*first_step(coeffs, pair, cross, False), False)
    shift, slip_rest, rest = call(
        prepare_second_kernel, [full] * 3,
        slip, state, speed, rest, scale_mid, numbers, near, rounded,
    )
    slip_out, state_out = call(
        functools.partial(finish_second_kernel, len(outer) - 2),
        [full] * 2,
        shift, scale_mid, rest, slip_rest, numbers, basis_out, near, *outer,
        out_specs=[HBM] * 2,
        scratch_shapes=[
            pltpu.VMEM((patches, ens), F32),
            pltpu.VMEM((patches, ens), F32),
            pltpu.SemaphoreType.DMA((2, patches // BS)),
        ],
    )
    return (slip_out, state_out)


def solution(mesh):
    in_specs = (
        P(("row", "col"), None),
        P(("row", "col"), None),
        P(("row", "col")),
        P(("row", "col")),
        P(("row", "col")),
        P(("row", "col")),
        P(("row", "col")),
        P(("row", "col")),
        P(None, ("row", "col"), None),
        P(None, ("row", "col")),
        P(None, ("row", "col")),
        P("row", None, "col"),
        P("row", None, "col"),
        P(None, ("row", "col")),
        P(("row", "col")),
        P(None, ("row", "col")),
        P("col", None),
        P("col", None),
    )
    out_specs = (P(("row", "col"), None), P(("row", "col"), None))
    return jax.shard_map(
        per_device, mesh=mesh, in_specs=in_specs, out_specs=out_specs, check_vma=False
    )
```

```python
import functools

import jax
import jax.numpy as jnp
from jax import lax
from jax.experimental import pallas as pl
from jax.experimental.pallas import tpu as pltpu
from jax.sharding import PartitionSpec as P

BS = 256
R = 32

STEP_SIZE = 0.5
REF_FRICTION = 0.6
LIMIT = 16 * 1024 * 1024
F32 = jnp.float32
BF16 = jnp.bfloat16


def dot(a, b):
    return jnp.dot(a, b, preferred_element_type=F32)


def dot_t(a, b):
    return lax.dot_general(a, b, (((0,), (0,)), ((), ())), preferred_element_type=F32)


VMEM = pl.BlockSpec(memory_space=pltpu.VMEM)


def call(kernel, outs, *operands, specs=None, **grid):
    return pl.pallas_call(
        kernel,
        in_specs=specs or [VMEM] * len(operands),
        out_shape=outs,
        compiler_params=pltpu.CompilerParams(vmem_limit_bytes=LIMIT),
        **grid,
    )(*operands)


def rows_at(n, size):
    return pl.ds(pl.multiple_of(n * size, size), size)


HBM = pl.BlockSpec(memory_space=pl.ANY)


def in_hbm(*arrays):
    return [pltpu.with_memory_space_constraint(array, pltpu.HBM) for array in arrays]


def start_copies(pairs, sems, first=0):
    copies = [pltpu.make_async_copy(a, b, sems.at[first + k]) for k, (a, b) in enumerate(pairs)]
    for copy in copies:
        copy.start()
    return copies


def fill_edges(first, last, pair_ref, cross_ref):
    even = lax.rem(lax.axis_index("col"), 2) == 0
    pair_ref[...] = jnp.where(even, last, first)
    cross_ref[...] = jnp.where(even, first, last)


def project_kernel(slip_ref, basis_ref, coeff_ref, rounded_ref, pair_ref, cross_ref):
    for n in range(slip_ref.shape[0] // BS):
        at = pl.ds(n * BS, BS)
        rounded = slip_ref[at, :].astype(BF16)
        rounded_ref[at, :] = rounded
        coeff_ref[n * R : (n + 1) * R, :] = dot(basis_ref[:, at], rounded).astype(BF16)
    fill_edges(rounded_ref[:BS], rounded_ref[-BS:], pair_ref, cross_ref)


def project(slip, basis_in):
    patches, ens = slip.shape
    edge = jax.ShapeDtypeStruct((BS, ens), BF16)
    return call(
        project_kernel,
        [
            jax.ShapeDtypeStruct((patches // BS * R, ens), BF16),
            jax.ShapeDtypeStruct((patches, ens), BF16),
            edge,
            edge,
        ],
        slip,
        basis_in,
    )


def ranks_kernel(
    col_count, rank_hbm, now_hbm, rate_hbm, wide_ref, joined_ref, rank_ref, sems
):
    sources, share, blocks = rank_ref.shape
    ens = now_hbm.shape[1]
    copies = start_copies(
        [
            (rank_hbm, rank_ref),
            (now_hbm, joined_ref.at[:, pl.ds(0, ens)]),
            (rate_hbm, joined_ref.at[:, pl.ds(ens, ens)]),
        ],
        sems,
    )
    width = share * R
    column = lax.broadcasted_iota(jnp.int32, (share, width), 1)
    spread = (lax.div(column, R) == lax.broadcasted_iota(jnp.int32, (share, width), 0)).astype(F32).astype(BF16)
    level = lax.rem(lax.broadcasted_iota(jnp.int32, (blocks, width), 1), R).astype(F32)
    receiver = lax.axis_index("row") * blocks + lax.broadcasted_iota(jnp.int32, (share, blocks), 1)
    copies[0].wait()
    for source in range(sources):
        own = (source * col_count + lax.axis_index("col")) * share + lax.broadcasted_iota(jnp.int32, (share, blocks), 0)
        rank = jnp.where(jnp.abs(receiver - own) > 1, rank_ref[source], 0).astype(F32)
        wide = dot_t(rank.astype(BF16), spread)
        wide_ref[source] = jnp.where(level < wide, wide, 0.0)
    copies[1].wait()
    copies[2].wait()


def side_by_side_kernel(*refs):
    pieces, out_ref = refs[:-1], refs[-1]
    size = pieces[0].shape[0]
    for k, piece in enumerate(pieces):
        out_ref[k * size : (k + 1) * size, :] = piece[...]


def weights_kernel(heights, size, start, *refs):
    begun = start > 0
    sources, rest = refs[:9], refs[9:]
    near_hbm, state_hbm, begun_ref = rest[:3] if begun else (None, None, None)
    rest = rest[4:] if begun else rest[1:]
    numbers_ref, matrix_ref = rest[:2]
    near_ref, state_ref = rest[2:4] if begun else (None, None)
    vectors, lists, sems = rest[-5], rest[-4:-1], rest[-1]
    targets = [vectors.at[k] for k in range(6)] + list(lists)
    copies = start_copies(list(zip(sources, targets)), sems)
    large = [(near_hbm, near_ref), (state_hbm, state_ref)] if begun else []
    large = start_copies(large, sems, len(targets))
    if begun:
        numbers_ref[:start, :] = begun_ref[...]
    count_ref, bricks_ref, weight_ref = lists
    slots = bricks_ref.shape[0]
    col = lax.axis_index("col")
    height, core = lax.div(col, 2).astype(F32), lax.rem(col, 2).astype(F32)
    group, lanes, unrolled = 16, 128, 8
    for copy in copies:
        copy.wait()

    @pl.loop(0, matrix_ref.shape[1] // lanes)
    def _(n):
        own_at = rows_at(n, lanes)
        at = pl.ds(pl.multiple_of(start + n * lanes, lanes), lanes)
        load, normal, direct, evolution, distance, stiffness = (vectors[k, :, at] for k in range(6))
        rows = [load, normal, 1.0 / direct, 1.0 / evolution, evolution / distance, stiffness, load, normal]
        numbers_ref[at if begun else own_at, :] = jnp.concatenate(rows, axis=0).T
        bricks = bricks_ref[:, at].astype(F32)
        live = lax.broadcasted_iota(jnp.int32, (slots, lanes), 0) < count_ref[:, at]
        weights = jnp.where(live, weight_ref[:, at], 0.0)
        merged = jnp.zeros((slots, lanes), F32)
        for k in range(slots):
            merged = merged + jnp.where(bricks == bricks[k : k + 1], weights[k : k + 1], 0.0)
        shares = merged / jnp.sum(weights, axis=0, keepdims=True)
        owner = jnp.floor((bricks + 0.5) * (1.0 / size))
        chip = jnp.floor(owner * 0.5 + 0.25)
        away = height - chip
        away = jnp.where(away < 0, away + heights, away)
        other = jnp.where(owner - 2.0 * chip == core, 0.0, float(heights))
        place = jnp.where(live, (other + away - owner) * size + bricks, -1.0)
        high = jnp.floor((place + 0.5) * (1.0 / group))
        low = place - high * group
        spread = lambda rows, k: jnp.broadcast_to(rows[k : k + 1], (group, lanes)).astype(BF16)
        line = lax.broadcasted_iota(jnp.int32, (group, lanes), 0).astype(F32).astype(BF16)
        none = jnp.full((group, lanes), -1.0, BF16)
        highs = [jnp.where(spread(low, k) == line, spread(high, k), none) for k in range(slots)]
        values = [spread(shares, k) for k in range(slots)]

        @pl.loop(0, matrix_ref.shape[0] // (group * unrolled))
        def _(m):
            first = jnp.full((group, lanes), (m * unrolled).astype(F32)).astype(BF16)
            for step in range(unrolled):
                here = first + jnp.asarray(step, BF16)
                tile = jnp.zeros((group, lanes), BF16)
                for k in range(slots):
                    tile = jnp.where(highs[k] == here, values[k], tile)
                to = pl.ds(pl.multiple_of((m * unrolled + step) * group, group), group)
                matrix_ref[to, own_at] = tile

    for copy in large:
        copy.wait()


def couple_kernel(sources, heights, flip, matrix_ref, *refs):
    coeffs, edges, out_ref = refs[:sources], refs[sources:-1], refs[-1]
    share = coeffs[0].shape[0]
    row, col = lax.axis_index("row"), lax.axis_index("col")
    height, core = lax.div(col, 2), lax.rem(col + flip, 2)

    @pl.loop(0, heights, unroll=True)
    def _(d):
        partner = lax.rem(d, 2) * (1 - 2 * lax.rem(height, 2))
        at = rows_at(2 * lax.rem(height + partner + d - lax.rem(d, 2) + heights, heights) + core, share)
        total = None
        for step in range(sources):
            term = dot(matrix_ref[lax.rem(row + (sources - step), sources), at, :], coeffs[step][...])
            total = term if total is None else total + term
        out_ref[rows_at(d, share), :] = total.astype(out_ref.dtype)

    for edge in edges:
        out_ref[heights * share :, :] = edge[...]


def couple(flip, matrix, coeffs, heights, kind, *edges):
    share, ens = coeffs[0].shape
    return call(
        functools.partial(couple_kernel, len(coeffs), heights, flip),
        jax.ShapeDtypeStruct((heights * share + len(edges) * BS, ens), kind),
        matrix,
        *coeffs,
        *edges,
    )


def chip_sum_kernel(kept_ref, sent_ref, own_ref, direct_ref, pass_ref, keep_ref):
    share = own_ref.shape[0]
    group = 32
    for place in range(2 + 2 * (keep_ref.shape[0] // share)):
        far = place // 2 - 1
        out_ref = (own_ref, direct_ref)[place % 2] if far < 0 else (keep_ref, pass_ref)[place % 2]

        @pl.loop(0, share // group)
        def _(n):
            at = pl.ds(pl.multiple_of(place * share + n * group, group), group)
            to = pl.ds(pl.multiple_of(max(far, 0) * share + n * group, group), group)
            out_ref[to, :] = (kept_ref[at, :] + sent_ref[at, :].astype(F32)).astype(out_ref.dtype)


def chip_sum(kept, sent, heights):
    rows, ens = kept.shape
    share = rows // heights
    far = (heights // 2 - 1) * share
    shapes = [(share, BF16), (share, BF16), (far, BF16), (far, F32)]
    return call(chip_sum_kernel, [jax.ShapeDtypeStruct((n, ens), kind) for n, kind in shapes], kept, sent)


def pair_sum_kernel(keep_ref, came_ref, *outs):
    share = outs[0].shape[0]
    group = 32
    for far, out_ref in enumerate(outs):

        @pl.loop(0, share // group)
        def _(n):
            at = pl.ds(pl.multiple_of(far * share + n * group, group), group)
            out_ref[rows_at(n, group), :] = (keep_ref[at, :] + came_ref[at, :].astype(F32)).astype(BF16)


def near_tau(n, slip, numbers, near_ref, rounded_ref):
    count = rounded_ref.shape[0] // BS
    at = rows_at(n, BS)
    none = jnp.zeros((BS, rounded_ref.shape[1]), BF16)
    before = jnp.where(n == 0, none, rounded_ref[rows_at(jnp.maximum(n - 1, 0), BS), :])
    after = jnp.where(n == count - 1, none, rounded_ref[rows_at(jnp.minimum(n + 1, count - 1), BS), :])
    near = dot(near_ref[0, at, :], before) + dot(near_ref[1, at, :], rounded_ref[at, :]) + dot(near_ref[2, at, :], after)
    return numbers[:, 0:1] - numbers[:, 5:6] * slip - near


def prepare_first_kernel(
    low_ref, high_ref, own_ref, other_ref, slip_ref, state_ref, numbers_ref, near_ref, rounded_ref,
    shift_ref, scale_ref, rest_ref, scale_mid_ref,
):
    half = own_ref.shape[0]
    ens = slip_ref.shape[1]
    blocks = low_ref.shape[1] // BS

    def block(matrix_ref, m, n):
        at, own_at = rows_at(n, BS), rows_at(m, BS)
        total = dot_t(matrix_ref[:half, own_at], own_ref[...]) + dot_t(matrix_ref[half:, own_at], other_ref[...])
        numbers = numbers_ref[at, :]
        normal, inv_direct, inv_evolution, ratio = (numbers[:, k : k + 1] for k in range(1, 5))
        base = total[:, :ens]
        scale = inv_direct / (normal - base)
        scale_ref[at, :] = scale
        scale_mid_ref[at, :] = inv_direct / (normal - (base + STEP_SIZE * total[:, ens:]))
        state = state_ref[at, :]
        tau = near_tau(n, slip_ref[at, :], numbers, near_ref, rounded_ref)
        shift_ref[at, :] = tau * scale - state * inv_direct
        rest_ref[at, :] = state + (STEP_SIZE * ratio) * jnp.exp((REF_FRICTION - state) * inv_evolution)

    @pl.loop(0, blocks)
    def _(m):
        block(low_ref, m, m)

    @pl.loop(0, blocks)
    def _(m):
        block(high_ref, m, blocks + m)


def over_blocks(block, basis_ref, near_ref, parts, pair_ref, cross_ref):
    count = near_ref.shape[1] // BS

    def far(n):
        levels = rows_at(n, R)
        total = parts[0][levels, :].astype(F32)
        for part in parts[1:]:
            total = total + part[levels, :].astype(F32)
        return dot_t(basis_ref[:, rows_at(n, BS)], total.astype(BF16))

    even = lax.rem(lax.axis_index("col"), 2) == 0
    pair, cross = pair_ref[-BS:], cross_ref[...]
    block(0, far(0) + dot(near_ref[0, :BS, :], jnp.where(even, cross, pair)))

    @pl.loop(1, count - 1, unroll=True)
    def _(n):
        block(n, far(n))

    block(count - 1, far(count - 1) + dot(near_ref[2, -BS:, :], jnp.where(even, pair, cross)))


def finish_first_kernel(
    count, shift_ref, scale_ref, slip_ref, basis_out_ref, basis_in_ref, near_ref, *refs
):
    parts, pair_ref, cross_ref = refs[:count], refs[count], refs[count + 1]
    speed_ref, rounded_ref, coeff_ref, pair_out, cross_out = refs[count + 2 :]

    def block(n, outer):
        at = rows_at(n, BS)
        speed = jnp.exp(shift_ref[at, :] - scale_ref[at, :] * outer)
        speed_ref[at, :] = speed
        rounded = (slip_ref[at, :] + STEP_SIZE * speed).astype(BF16)
        rounded_ref[at, :] = rounded
        coeff_ref[rows_at(n, R), :] = dot(basis_in_ref[:, at], rounded).astype(BF16)

    over_blocks(block, basis_out_ref, near_ref, parts, pair_ref, cross_ref)
    fill_edges(rounded_ref[:BS], rounded_ref[-BS:], pair_out, cross_out)


def prepare_second_kernel(
    slip_ref, state_ref, speed_ref, part_ref, scale_ref, numbers_ref, near_ref, rounded_ref,
    shift_ref, slip_rest_ref, rest_ref,
):
    @pl.loop(0, slip_ref.shape[0] // BS)
    def _(n):
        at = rows_at(n, BS)
        numbers = numbers_ref[at, :]
        inv_direct, inv_evolution, ratio = (numbers[:, k : k + 1] for k in range(2, 5))
        speed = speed_ref[at, :]
        slip = slip_ref[at, :] + STEP_SIZE * speed
        state = part_ref[at, :] - (STEP_SIZE * ratio) * speed
        tau = near_tau(n, slip, numbers, near_ref, rounded_ref)
        shift_ref[at, :] = tau * scale_ref[at, :] - state * inv_direct
        slip_rest_ref[at, :] = 0.5 * (slip_ref[at, :] + slip)
        friction = jnp.exp((REF_FRICTION - state) * inv_evolution)
        rest_ref[at, :] = 0.5 * (state_ref[at, :] + state) + (0.5 * STEP_SIZE * ratio) * friction


def finish_second_kernel(
    count, shift_ref, scale_ref, rest_ref, slip_rest_ref, numbers_ref, basis_out_ref, near_ref, *refs
):
    parts, pair_ref, cross_ref = refs[:count], refs[count], refs[count + 1]
    slip_hbm, state_hbm, slip_ref, state_ref, sems = refs[count + 2 :]

    def copies(n):
        at = rows_at(n, BS)
        return [
            pltpu.make_async_copy(slip_ref.at[at, :], slip_hbm.at[at, :], sems.at[0, n]),
            pltpu.make_async_copy(state_ref.at[at, :], state_hbm.at[at, :], sems.at[1, n]),
        ]

    def block(n, outer):
        at = rows_at(n, BS)
        speed = jnp.exp(shift_ref[at, :] - scale_ref[at, :] * outer)
        slip_ref[at, :] = slip_rest_ref[at, :] + (0.5 * STEP_SIZE) * speed
        state_ref[at, :] = rest_ref[at, :] - (0.5 * STEP_SIZE * numbers_ref[at, 4:5]) * speed
        for copy in copies(n):
            copy.start()

    over_blocks(block, basis_out_ref, near_ref, parts, pair_ref, cross_ref)

    @pl.loop(0, slip_ref.shape[0] // BS)
    def _(n):
        for copy in copies(n):
            copy.wait()


def masked_coupling(coupling, wide):
    rows, sources, width = coupling.shape
    blocks = rows // R
    keep = jnp.arange(R, dtype=jnp.int32).astype(F32)[None, None, :, None] < wide[:, :, None, :]
    matrix = jnp.transpose(coupling, (1, 0, 2)).reshape(sources, blocks, R, width)
    masked = jnp.where(keep, matrix, jnp.zeros((), BF16)).reshape(sources, rows, width)
    return pltpu.with_memory_space_constraint(masked, pltpu.VMEM)


def per_device(
    slip,
    state,
    tau_load,
    normal_stress,
    direct_effect,
    evolution_effect,
    slip_distance,
    self_stiffness,
    near_blocks,
    basis_in,
    basis_out,
    coupling,
    block_rank,
    adj_bricks,
    adj_count,
    adj_weight,
    pressure_now,
    pressure_rate,
):
    row_count = lax.axis_size("row")
    col_count = lax.axis_size("col")
    row_index = lax.axis_index("row")
    col_index = lax.axis_index("col")
    heights = col_count // 2
    height, core = col_index // 2, col_index % 2
    both = ("row", "col")
    devices = row_count * col_count

    def to_row(array, d):
        return lax.ppermute(array, "row", [(i, (i + d) % row_count) for i in range(row_count)])

    def to_height(array, d):
        pairs = [(2 * z + k, 2 * ((z + d) % heights) + k) for z in range(heights) for k in range(2)]
        return lax.ppermute(array, "col", pairs)

    def to_core(array):
        return lax.ppermute(array, "col", [(2 * z + k, 2 * z + 1 - k) for z in range(heights) for k in range(2)])

    def to_chip(array):
        ends = [(i, i + 1) for i in range(1, devices - 1, 2)]
        return lax.ppermute(array, both, ends + [(j, i) for i, j in ends])

    patches, ens = slip.shape
    slots = adj_bricks.shape[0]
    size = pressure_now.shape[0]
    share = coupling.shape[2]
    def to_partner(array):
        pairs = [(2 * z + k, 2 * (z + 1 - 2 * (z % 2)) + k) for z in range(heights) for k in range(2)]
        return lax.ppermute(array, "col", pairs)

    def first_step(coeffs, pair, cross, later):
        sent = to_core(couple(1, masked, coeffs, heights, BF16, pair))
        kept = couple(0, masked, coeffs, heights, F32)
        own, direct, passed, keep = chip_sum(kept, sent, heights)
        if not later:
            own, cross = lax.optimization_barrier((own, cross))
        return own, to_partner(passed), to_partner(direct), keep, sent, cross if later else to_chip(cross)

    def second_step(own, came, direct, keep, sent, cross):
        sums = call(pair_sum_kernel, [jax.ShapeDtypeStruct((share, ens), BF16)] * (heights // 2 - 1), keep, came)
        return [to_height(part, 2 * (d + 1)) for d, part in enumerate(sums)] + [own, direct, sent, cross]

    def row_coeffs(coeff):
        return [coeff] + [to_row(coeff, d) for d in range(1, row_count)]

    full = jax.ShapeDtypeStruct((patches, ens), F32)
    half = jax.ShapeDtypeStruct((patches, ens), BF16)
    edge = jax.ShapeDtypeStruct((BS, ens), BF16)
    per_patch = [tau_load, normal_stress, direct_effect, evolution_effect, slip_distance, self_stiffness]

    ranks = jnp.transpose(block_rank, (1, 2, 0))
    wide, joined = call(
        functools.partial(ranks_kernel, col_count),
        [
            jax.ShapeDtypeStruct((ranks.shape[0], ranks.shape[2], share), F32),
            jax.ShapeDtypeStruct((size, 2 * ens), BF16),
        ],
        *in_hbm(ranks, pressure_now, pressure_rate),
        specs=[HBM] * 3,
        scratch_shapes=[pltpu.VMEM(ranks.shape, jnp.int32), pltpu.SemaphoreType.DMA((3,))],
    )
    fields = [joined] + [to_height(joined, d) for d in range(1, heights)]
    masked = masked_coupling(coupling, wide)
    masked, slip = lax.optimization_barrier((masked, slip))
    coeff, rounded, pair, cross = project(slip, basis_in)
    coeffs = row_coeffs(coeff)
    brick_lists = [adj_count[None], adj_bricks, adj_weight]
    columns = [array[None] for array in per_patch] + brick_lists
    start = patches // 2
    part = jax.ShapeDtypeStruct((2 * heights * size, start), BF16)
    scratch = [
        pltpu.VMEM((6, 1, patches), F32),
        pltpu.VMEM((1, patches), jnp.int32),
        pltpu.VMEM(adj_bricks.shape, jnp.int32),
        pltpu.VMEM(adj_weight.shape, F32),
        pltpu.SemaphoreType.DMA((11,)),
    ]
    numbers, low = call(
        functools.partial(weights_kernel, heights, size, 0),
        [jax.ShapeDtypeStruct((start, 8), F32), part],
        *in_hbm(*columns),
        coeff,
        specs=[HBM] * 9 + [VMEM],
        scratch_shapes=scratch,
    )
    fields, coeffs, low = lax.optimization_barrier((fields, coeffs, low))
    own = call(
        side_by_side_kernel, jax.ShapeDtypeStruct((heights * size, 2 * ens), BF16), *fields
    )
    other = to_core(own)
    own_part, came, direct, keep, sent, cross = first_step(coeffs, pair, cross, True)
    numbers, high, near, state = call(
        functools.partial(weights_kernel, heights, size, start),
        [jax.ShapeDtypeStruct((patches, 8), F32), part, jax.ShapeDtypeStruct(near_blocks.shape, BF16), full],
        *in_hbm(*columns, near_blocks, state),
        numbers,
        own_part,
        specs=[HBM] * 11 + [VMEM] * 2,
        scratch_shapes=scratch,
    )
    came, high = lax.optimization_barrier((came, high))
    outer = second_step(own_part, came, direct, keep, sent, cross)
    shift, scale, rest, scale_mid = call(
        prepare_first_kernel, [full] * 4, low, high, own, other, slip, state, numbers, near, rounded
    )
    shift, cross = lax.optimization_barrier((shift, cross))
    outer[-1] = to_chip(cross)
    speed, rounded, coeff, pair, cross = call(
        functools.partial(finish_first_kernel, len(outer) - 2),
        [full, half, jax.ShapeDtypeStruct((patches // BS * R, ens), BF16), edge, edge],
        shift, scale, slip, basis_out, basis_in, near, *outer,
    )
    coeffs = row_coeffs(coeff)
    outer = second_step(*first_step(coeffs, pair, cross, False))
    shift, slip_rest, rest = call(
        prepare_second_kernel, [full] * 3,
        slip, state, speed, rest, scale_mid, numbers, near, rounded,
    )
    slip_out, state_out = call(
        functools.partial(finish_second_kernel, len(outer) - 2),
        [full] * 2,
        shift, scale_mid, rest, slip_rest, numbers, basis_out, near, *outer,
        out_specs=[HBM] * 2,
        scratch_shapes=[
            pltpu.VMEM((patches, ens), F32),
            pltpu.VMEM((patches, ens), F32),
            pltpu.SemaphoreType.DMA((2, patches // BS)),
        ],
    )
    return (slip_out, state_out)


def solution(mesh):
    in_specs = (
        P(("row", "col"), None),
        P(("row", "col"), None),
        P(("row", "col")),
        P(("row", "col")),
        P(("row", "col")),
        P(("row", "col")),
        P(("row", "col")),
        P(("row", "col")),
        P(None, ("row", "col"), None),
        P(None, ("row", "col")),
        P(None, ("row", "col")),
        P("row", None, "col"),
        P("row", None, "col"),
        P(None, ("row", "col")),
        P(("row", "col")),
        P(None, ("row", "col")),
        P("col", None),
        P("col", None),
    )
    out_specs = (P(("row", "col"), None), P(("row", "col"), None))
    return jax.shard_map(
        per_device, mesh=mesh, in_specs=in_specs, out_specs=out_specs, check_vma=False
    )
```

```python
import functools

import jax
import jax.numpy as jnp
from jax import lax
from jax.experimental import pallas as pl
from jax.experimental.pallas import tpu as pltpu
from jax.sharding import PartitionSpec as P

BS = 256
R = 32

STEP_SIZE = 0.5
REF_FRICTION = 0.6
LIMIT = 16 * 1024 * 1024
F32 = jnp.float32
BF16 = jnp.bfloat16


def dot(a, b):
    return jnp.dot(a, b, preferred_element_type=F32)


def dot_t(a, b):
    return lax.dot_general(a, b, (((0,), (0,)), ((), ())), preferred_element_type=F32)


VMEM = pl.BlockSpec(memory_space=pltpu.VMEM)


def call(kernel, outs, *operands, specs=None, **grid):
    return pl.pallas_call(
        kernel,
        in_specs=specs or [VMEM] * len(operands),
        out_shape=outs,
        compiler_params=pltpu.CompilerParams(vmem_limit_bytes=LIMIT),
        **grid,
    )(*operands)


def rows_at(n, size):
    return pl.ds(pl.multiple_of(n * size, size), size)


HBM = pl.BlockSpec(memory_space=pl.ANY)


def in_hbm(*arrays):
    return [pltpu.with_memory_space_constraint(array, pltpu.HBM) for array in arrays]


def start_copies(pairs, sems, first=0):
    copies = [pltpu.make_async_copy(a, b, sems.at[first + k]) for k, (a, b) in enumerate(pairs)]
    for copy in copies:
        copy.start()
    return copies


def fill_edges(first, last, pair_ref, cross_ref):
    even = lax.rem(lax.axis_index("col"), 2) == 0
    pair_ref[...] = jnp.where(even, last, first)
    cross_ref[...] = jnp.where(even, first, last)


def project_kernel(slip_ref, basis_ref, coeff_ref, rounded_ref, pair_ref, cross_ref):
    for n in range(slip_ref.shape[0] // BS):
        at = pl.ds(n * BS, BS)
        rounded = slip_ref[at, :].astype(BF16)
        rounded_ref[at, :] = rounded
        coeff_ref[n * R : (n + 1) * R, :] = dot(basis_ref[:, at], rounded).astype(BF16)
    fill_edges(rounded_ref[:BS], rounded_ref[-BS:], pair_ref, cross_ref)


def project(slip, basis_in):
    patches, ens = slip.shape
    edge = jax.ShapeDtypeStruct((BS, ens), BF16)
    return call(
        project_kernel,
        [
            jax.ShapeDtypeStruct((patches // BS * R, ens), BF16),
            jax.ShapeDtypeStruct((patches, ens), BF16),
            edge,
            edge,
        ],
        slip,
        basis_in,
    )


def ranks_kernel(
    col_count, rank_hbm, now_hbm, rate_hbm, wide_ref, joined_ref, rank_ref, sems
):
    sources, share, blocks = rank_ref.shape
    ens = now_hbm.shape[1]
    copies = start_copies(
        [
            (rank_hbm, rank_ref),
            (now_hbm, joined_ref.at[:, pl.ds(0, ens)]),
            (rate_hbm, joined_ref.at[:, pl.ds(ens, ens)]),
        ],
        sems,
    )
    width = share * R
    column = lax.broadcasted_iota(jnp.int32, (share, width), 1)
    spread = (lax.div(column, R) == lax.broadcasted_iota(jnp.int32, (share, width), 0)).astype(F32).astype(BF16)
    level = lax.rem(lax.broadcasted_iota(jnp.int32, (blocks, width), 1), R).astype(F32)
    receiver = lax.axis_index("row") * blocks + lax.broadcasted_iota(jnp.int32, (share, blocks), 1)
    copies[0].wait()
    for source in range(sources):
        own = (source * col_count + lax.axis_index("col")) * share + lax.broadcasted_iota(jnp.int32, (share, blocks), 0)
        rank = jnp.where(jnp.abs(receiver - own) > 1, rank_ref[source], 0).astype(F32)
        wide = dot_t(rank.astype(BF16), spread)
        wide_ref[source] = jnp.where(level < wide, wide, 0.0)
    copies[1].wait()
    copies[2].wait()


def side_by_side_kernel(*refs):
    pieces, out_ref = refs[:-1], refs[-1]
    size = pieces[0].shape[0]
    for k, piece in enumerate(pieces):
        out_ref[k * size : (k + 1) * size, :] = piece[...]


def weights_kernel(heights, size, start, *refs):
    begun = start > 0
    sources, rest = refs[:9], refs[9:]
    near_hbm, state_hbm, begun_ref = rest[:3] if begun else (None, None, None)
    rest = rest[4:] if begun else rest[1:]
    numbers_ref, matrix_ref = rest[:2]
    near_ref, state_ref = rest[2:4] if begun else (None, None)
    vectors, lists, sems = rest[-5], rest[-4:-1], rest[-1]
    targets = [vectors.at[k] for k in range(6)] + list(lists)
    copies = start_copies(list(zip(sources, targets)), sems)
    large = [(near_hbm, near_ref), (state_hbm, state_ref)] if begun else []
    large = start_copies(large, sems, len(targets))
    if begun:
        numbers_ref[:start, :] = begun_ref[...]
    count_ref, bricks_ref, weight_ref = lists
    slots = bricks_ref.shape[0]
    col = lax.axis_index("col")
    height, core = lax.div(col, 2).astype(F32), lax.rem(col, 2).astype(F32)
    group, lanes, unrolled = 16, 128, 8
    for copy in copies:
        copy.wait()

    @pl.loop(0, matrix_ref.shape[1] // lanes)
    def _(n):
        own_at = rows_at(n, lanes)
        at = pl.ds(pl.multiple_of(start + n * lanes, lanes), lanes)
        load, normal, direct, evolution, distance, stiffness = (vectors[k, :, at] for k in range(6))
        rows = [load, normal, 1.0 / direct, 1.0 / evolution, evolution / distance, stiffness, load, normal]
        numbers_ref[at if begun else own_at, :] = jnp.concatenate(rows, axis=0).T
        bricks = bricks_ref[:, at].astype(F32)
        live = lax.broadcasted_iota(jnp.int32, (slots, lanes), 0) < count_ref[:, at]
        weights = jnp.where(live, weight_ref[:, at], 0.0)
        merged = jnp.zeros((slots, lanes), F32)
        for k in range(slots):
            merged = merged + jnp.where(bricks == bricks[k : k + 1], weights[k : k + 1], 0.0)
        shares = merged / jnp.sum(weights, axis=0, keepdims=True)
        owner = jnp.floor((bricks + 0.5) * (1.0 / size))
        chip = jnp.floor(owner * 0.5 + 0.25)
        away = height - chip
        away = jnp.where(away < 0, away + heights, away)
        other = jnp.where(owner - 2.0 * chip == core, 0.0, float(heights))
        place = jnp.where(live, (other + away - owner) * size + bricks, -1.0)
        high = jnp.floor((place + 0.5) * (1.0 / group))
        low = place - high * group
        spread = lambda rows, k: jnp.broadcast_to(rows[k : k + 1], (group, lanes)).astype(BF16)
        line = lax.broadcasted_iota(jnp.int32, (group, lanes), 0).astype(F32).astype(BF16)
        none = jnp.full((group, lanes), -1.0, BF16)
        highs = [jnp.where(spread(low, k) == line, spread(high, k), none) for k in range(slots)]
        values = [spread(shares, k) for k in range(slots)]

        @pl.loop(0, matrix_ref.shape[0] // (group * unrolled))
        def _(m):
            first = jnp.full((group, lanes), (m * unrolled).astype(F32)).astype(BF16)
            for step in range(unrolled):
                here = first + jnp.asarray(step, BF16)
                tile = jnp.zeros((group, lanes), BF16)
                for k in range(slots):
                    tile = jnp.where(highs[k] == here, values[k], tile)
                to = pl.ds(pl.multiple_of((m * unrolled + step) * group, group), group)
                matrix_ref[to, own_at] = tile

    for copy in large:
        copy.wait()


def couple_kernel(sources, heights, flip, matrix_ref, *refs):
    coeffs, edges, out_ref = refs[:sources], refs[sources:-1], refs[-1]
    share = coeffs[0].shape[0]
    row, col = lax.axis_index("row"), lax.axis_index("col")
    height, core = lax.div(col, 2), lax.rem(col + flip, 2)

    @pl.loop(0, heights, unroll=True)
    def _(d):
        partner = lax.rem(d, 2) * (1 - 2 * lax.rem(height, 2))
        at = rows_at(2 * lax.rem(height + partner + d - lax.rem(d, 2) + heights, heights) + core, share)
        total = None
        for step in range(sources):
            term = dot(matrix_ref[lax.rem(row + (sources - step), sources), at, :], coeffs[step][...])
            total = term if total is None else total + term
        out_ref[rows_at(d, share), :] = total.astype(out_ref.dtype)

    for edge in edges:
        out_ref[heights * share :, :] = edge[...]


def couple(flip, matrix, coeffs, heights, kind, *edges):
    share, ens = coeffs[0].shape
    return call(
        functools.partial(couple_kernel, len(coeffs), heights, flip),
        jax.ShapeDtypeStruct((heights * share + len(edges) * BS, ens), kind),
        matrix,
        *coeffs,
        *edges,
    )


def chip_sum_kernel(kept_ref, sent_ref, own_ref, direct_ref, pass_ref, keep_ref):
    share = own_ref.shape[0]
    group = 32
    for place in range(2 + 2 * (keep_ref.shape[0] // share)):
        far = place // 2 - 1
        out_ref = (own_ref, direct_ref)[place % 2] if far < 0 else (keep_ref, pass_ref)[place % 2]

        @pl.loop(0, share // group)
        def _(n):
            at = pl.ds(pl.multiple_of(place * share + n * group, group), group)
            to = pl.ds(pl.multiple_of(max(far, 0) * share + n * group, group), group)
            out_ref[to, :] = (kept_ref[at, :] + sent_ref[at, :].astype(F32)).astype(out_ref.dtype)


def chip_sum(kept, sent, heights):
    rows, ens = kept.shape
    share = rows // heights
    far = (heights // 2 - 1) * share
    shapes = [(share, BF16), (share, BF16), (far, BF16), (far, F32)]
    return call(chip_sum_kernel, [jax.ShapeDtypeStruct((n, ens), kind) for n, kind in shapes], kept, sent)


def pair_sum_kernel(keep_ref, came_ref, *outs):
    share = outs[0].shape[0]
    group = 32
    for far, out_ref in enumerate(outs):

        @pl.loop(0, share // group)
        def _(n):
            at = pl.ds(pl.multiple_of(far * share + n * group, group), group)
            out_ref[rows_at(n, group), :] = (keep_ref[at, :] + came_ref[at, :].astype(F32)).astype(BF16)


def near_tau(n, slip, numbers, near_ref, rounded_ref):
    count = rounded_ref.shape[0] // BS
    at = rows_at(n, BS)
    none = jnp.zeros((BS, rounded_ref.shape[1]), BF16)
    before = jnp.where(n == 0, none, rounded_ref[rows_at(jnp.maximum(n - 1, 0), BS), :])
    after = jnp.where(n == count - 1, none, rounded_ref[rows_at(jnp.minimum(n + 1, count - 1), BS), :])
    near = dot(near_ref[0, at, :], before) + dot(near_ref[1, at, :], rounded_ref[at, :]) + dot(near_ref[2, at, :], after)
    return numbers[:, 0:1] - numbers[:, 5:6] * slip - near


def prepare_first_kernel(
    low_ref, high_ref, own_ref, other_ref, slip_ref, state_ref, numbers_ref, near_ref, rounded_ref,
    shift_ref, scale_ref, rest_ref, scale_mid_ref,
):
    half = own_ref.shape[0]
    ens = slip_ref.shape[1]
    blocks = low_ref.shape[1] // BS

    def block(matrix_ref, m, n):
        at, own_at = rows_at(n, BS), rows_at(m, BS)
        total = dot_t(matrix_ref[:half, own_at], own_ref[...]) + dot_t(matrix_ref[half:, own_at], other_ref[...])
        numbers = numbers_ref[at, :]
        normal, inv_direct, inv_evolution, ratio = (numbers[:, k : k + 1] for k in range(1, 5))
        base = total[:, :ens]
        scale = inv_direct / (normal - base)
        scale_ref[at, :] = scale
        scale_mid_ref[at, :] = inv_direct / (normal - (base + STEP_SIZE * total[:, ens:]))
        state = state_ref[at, :]
        tau = near_tau(n, slip_ref[at, :], numbers, near_ref, rounded_ref)
        shift_ref[at, :] = tau * scale - state * inv_direct
        rest_ref[at, :] = state + (STEP_SIZE * ratio) * jnp.exp((REF_FRICTION - state) * inv_evolution)

    @pl.loop(0, blocks)
    def _(m):
        block(low_ref, m, m)

    @pl.loop(0, blocks)
    def _(m):
        block(high_ref, m, blocks + m)


def over_blocks(block, basis_ref, near_ref, parts, pair_ref, cross_ref):
    count = near_ref.shape[1] // BS

    def far(n):
        levels = rows_at(n, R)
        total = parts[0][levels, :].astype(F32)
        for part in parts[1:]:
            total = total + part[levels, :].astype(F32)
        return dot_t(basis_ref[:, rows_at(n, BS)], total.astype(BF16))

    even = lax.rem(lax.axis_index("col"), 2) == 0
    pair, cross = pair_ref[-BS:], cross_ref[...]
    block(0, far(0) + dot(near_ref[0, :BS, :], jnp.where(even, cross, pair)))

    @pl.loop(1, count - 1, unroll=True)
    def _(n):
        block(n, far(n))

    block(count - 1, far(count - 1) + dot(near_ref[2, -BS:, :], jnp.where(even, pair, cross)))


def finish_first_kernel(
    count, shift_ref, scale_ref, slip_ref, basis_out_ref, basis_in_ref, near_ref, *refs
):
    parts, pair_ref, cross_ref = refs[:count], refs[count], refs[count + 1]
    speed_ref, rounded_ref, coeff_ref, pair_out, cross_out = refs[count + 2 :]

    def block(n, outer):
        at = rows_at(n, BS)
        speed = jnp.exp(shift_ref[at, :] - scale_ref[at, :] * outer)
        speed_ref[at, :] = speed
        rounded = (slip_ref[at, :] + STEP_SIZE * speed).astype(BF16)
        rounded_ref[at, :] = rounded
        coeff_ref[rows_at(n, R), :] = dot(basis_in_ref[:, at], rounded).astype(BF16)

    over_blocks(block, basis_out_ref, near_ref, parts, pair_ref, cross_ref)
    fill_edges(rounded_ref[:BS], rounded_ref[-BS:], pair_out, cross_out)


def prepare_second_kernel(
    slip_ref, state_ref, speed_ref, part_ref, scale_ref, numbers_ref, near_ref, rounded_ref,
    shift_ref, slip_rest_ref, rest_ref,
):
    @pl.loop(0, slip_ref.shape[0] // BS)
    def _(n):
        at = rows_at(n, BS)
        numbers = numbers_ref[at, :]
        inv_direct, inv_evolution, ratio = (numbers[:, k : k + 1] for k in range(2, 5))
        speed = speed_ref[at, :]
        slip = slip_ref[at, :] + STEP_SIZE * speed
        state = part_ref[at, :] - (STEP_SIZE * ratio) * speed
        tau = near_tau(n, slip, numbers, near_ref, rounded_ref)
        shift_ref[at, :] = tau * scale_ref[at, :] - state * inv_direct
        slip_rest_ref[at, :] = 0.5 * (slip_ref[at, :] + slip)
        friction = jnp.exp((REF_FRICTION - state) * inv_evolution)
        rest_ref[at, :] = 0.5 * (state_ref[at, :] + state) + (0.5 * STEP_SIZE * ratio) * friction


def finish_second_kernel(
    count, shift_ref, scale_ref, rest_ref, slip_rest_ref, numbers_ref, basis_out_ref, near_ref, *refs
):
    parts, pair_ref, cross_ref = refs[:count], refs[count], refs[count + 1]
    slip_hbm, state_hbm, slip_ref, state_ref, sems = refs[count + 2 :]

    def copies(n):
        at = rows_at(n, BS)
        return [
            pltpu.make_async_copy(slip_ref.at[at, :], slip_hbm.at[at, :], sems.at[0, n]),
            pltpu.make_async_copy(state_ref.at[at, :], state_hbm.at[at, :], sems.at[1, n]),
        ]

    def block(n, outer):
        at = rows_at(n, BS)
        speed = jnp.exp(shift_ref[at, :] - scale_ref[at, :] * outer)
        slip_ref[at, :] = slip_rest_ref[at, :] + (0.5 * STEP_SIZE) * speed
        state_ref[at, :] = rest_ref[at, :] - (0.5 * STEP_SIZE * numbers_ref[at, 4:5]) * speed
        for copy in copies(n):
            copy.start()

    over_blocks(block, basis_out_ref, near_ref, parts, pair_ref, cross_ref)

    @pl.loop(0, slip_ref.shape[0] // BS)
    def _(n):
        for copy in copies(n):
            copy.wait()


def masked_coupling(coupling, wide):
    rows, sources, width = coupling.shape
    blocks = rows // R
    keep = jnp.arange(R, dtype=jnp.int32).astype(F32)[None, None, :, None] < wide[:, :, None, :]
    matrix = jnp.transpose(coupling, (1, 0, 2)).reshape(sources, blocks, R, width)
    masked = jnp.where(keep, matrix, jnp.zeros((), BF16)).reshape(sources, rows, width)
    return pltpu.with_memory_space_constraint(masked, pltpu.VMEM)


def per_device(
    slip,
    state,
    tau_load,
    normal_stress,
    direct_effect,
    evolution_effect,
    slip_distance,
    self_stiffness,
    near_blocks,
    basis_in,
    basis_out,
    coupling,
    block_rank,
    adj_bricks,
    adj_count,
    adj_weight,
    pressure_now,
    pressure_rate,
):
    row_count = lax.axis_size("row")
    col_count = lax.axis_size("col")
    row_index = lax.axis_index("row")
    col_index = lax.axis_index("col")
    heights = col_count // 2
    height, core = col_index // 2, col_index % 2
    both = ("row", "col")
    devices = row_count * col_count

    def to_row(array, d):
        return lax.ppermute(array, "row", [(i, (i + d) % row_count) for i in range(row_count)])

    def to_height(array, d):
        pairs = [(2 * z + k, 2 * ((z + d) % heights) + k) for z in range(heights) for k in range(2)]
        return lax.ppermute(array, "col", pairs)

    def to_core(array):
        return lax.ppermute(array, "col", [(2 * z + k, 2 * z + 1 - k) for z in range(heights) for k in range(2)])

    def to_chip(array):
        ends = [(i, i + 1) for i in range(1, devices - 1, 2)]
        return lax.ppermute(array, both, ends + [(j, i) for i, j in ends])

    patches, ens = slip.shape
    slots = adj_bricks.shape[0]
    size = pressure_now.shape[0]
    share = coupling.shape[2]
    def to_partner(array):
        pairs = [(2 * z + k, 2 * (z + 1 - 2 * (z % 2)) + k) for z in range(heights) for k in range(2)]
        return lax.ppermute(array, "col", pairs)

    def first_step(coeffs, pair, cross, later):
        sent = to_core(couple(1, masked, coeffs, heights, BF16, pair))
        kept = couple(0, masked, coeffs, heights, F32)
        own, direct, passed, keep = chip_sum(kept, sent, heights)
        if not later:
            own, cross = lax.optimization_barrier((own, cross))
        return own, to_partner(passed), to_partner(direct), keep, sent, cross if later else to_chip(cross)

    def second_step(own, came, direct, keep, sent, cross, later):
        sums = call(pair_sum_kernel, [jax.ShapeDtypeStruct((share, ens), BF16)] * (heights // 2 - 1), keep, came)
        if later:
            sums, cross = lax.optimization_barrier((sums, cross))
            cross = to_chip(cross)
        return [to_height(part, 2 * (d + 1)) for d, part in enumerate(sums)] + [own, direct, sent, cross]

    def row_coeffs(coeff):
        return [coeff] + [to_row(coeff, d) for d in range(1, row_count)]

    full = jax.ShapeDtypeStruct((patches, ens), F32)
    half = jax.ShapeDtypeStruct((patches, ens), BF16)
    edge = jax.ShapeDtypeStruct((BS, ens), BF16)
    per_patch = [tau_load, normal_stress, direct_effect, evolution_effect, slip_distance, self_stiffness]

    ranks = jnp.transpose(block_rank, (1, 2, 0))
    wide, joined = call(
        functools.partial(ranks_kernel, col_count),
        [
            jax.ShapeDtypeStruct((ranks.shape[0], ranks.shape[2], share), F32),
            jax.ShapeDtypeStruct((size, 2 * ens), BF16),
        ],
        *in_hbm(ranks, pressure_now, pressure_rate),
        specs=[HBM] * 3,
        scratch_shapes=[pltpu.VMEM(ranks.shape, jnp.int32), pltpu.SemaphoreType.DMA((3,))],
    )
    fields = [joined] + [to_height(joined, d) for d in range(1, heights)]
    masked = masked_coupling(coupling, wide)
    masked, slip = lax.optimization_barrier((masked, slip))
    coeff, rounded, pair, cross = project(slip, basis_in)
    coeffs = row_coeffs(coeff)
    brick_lists = [adj_count[None], adj_bricks, adj_weight]
    columns = [array[None] for array in per_patch] + brick_lists
    start = patches // 2
    part = jax.ShapeDtypeStruct((2 * heights * size, start), BF16)
    scratch = [
        pltpu.VMEM((6, 1, patches), F32),
        pltpu.VMEM((1, patches), jnp.int32),
        pltpu.VMEM(adj_bricks.shape, jnp.int32),
        pltpu.VMEM(adj_weight.shape, F32),
        pltpu.SemaphoreType.DMA((11,)),
    ]
    numbers, low = call(
        functools.partial(weights_kernel, heights, size, 0),
        [jax.ShapeDtypeStruct((start, 8), F32), part],
        *in_hbm(*columns),
        coeff,
        specs=[HBM] * 9 + [VMEM],
        scratch_shapes=scratch,
    )
    fields, coeffs, low = lax.optimization_barrier((fields, coeffs, low))
    own = call(
        side_by_side_kernel, jax.ShapeDtypeStruct((heights * size, 2 * ens), BF16), *fields
    )
    other = to_core(own)
    own_part, came, direct, keep, sent, cross = first_step(coeffs, pair, cross, True)
    numbers, high, near, state = call(
        functools.partial(weights_kernel, heights, size, start),
        [jax.ShapeDtypeStruct((patches, 8), F32), part, jax.ShapeDtypeStruct(near_blocks.shape, BF16), full],
        *in_hbm(*columns, near_blocks, state),
        numbers,
        own_part,
        specs=[HBM] * 11 + [VMEM] * 2,
        scratch_shapes=scratch,
    )
    came, high = lax.optimization_barrier((came, high))
    outer = second_step(own_part, came, direct, keep, sent, cross, True)
    shift, scale, rest, scale_mid = call(
        prepare_first_kernel, [full] * 4, low, high, own, other, slip, state, numbers, near, rounded
    )
    speed, rounded, coeff, pair, cross = call(
        functools.partial(finish_first_kernel, len(outer) - 2),
        [full, half, jax.ShapeDtypeStruct((patches // BS * R, ens), BF16), edge, edge],
        shift, scale, slip, basis_out, basis_in, near, *outer,
    )
    coeffs = row_coeffs(coeff)
    outer = second_step(*first_step(coeffs, pair, cross, False), False)
    shift, slip_rest, rest = call(
        prepare_second_kernel, [full] * 3,
        slip, state, speed, rest, scale_mid, numbers, near, rounded,
    )
    slip_out, state_out = call(
        functools.partial(finish_second_kernel, len(outer) - 2),
        [full] * 2,
        shift, scale_mid, rest, slip_rest, numbers, basis_out, near, *outer,
        out_specs=[HBM] * 2,
        scratch_shapes=[
            pltpu.VMEM((patches, ens), F32),
            pltpu.VMEM((patches, ens), F32),
            pltpu.SemaphoreType.DMA((2, patches // BS)),
        ],
    )
    return (slip_out, state_out)


def solution(mesh):
    in_specs = (
        P(("row", "col"), None),
        P(("row", "col"), None),
        P(("row", "col")),
        P(("row", "col")),
        P(("row", "col")),
        P(("row", "col")),
        P(("row", "col")),
        P(("row", "col")),
        P(None, ("row", "col"), None),
        P(None, ("row", "col")),
        P(None, ("row", "col")),
        P("row", None, "col"),
        P("row", None, "col"),
        P(None, ("row", "col")),
        P(("row", "col")),
        P(None, ("row", "col")),
        P("col", None),
        P("col", None),
    )
    out_specs = (P(("row", "col"), None), P(("row", "col"), None))
    return jax.shard_map(
        per_device, mesh=mesh, in_specs=in_specs, out_specs=out_specs, check_vma=False
    )
```

```python
import functools

import jax
import jax.numpy as jnp
from jax import lax
from jax.experimental import pallas as pl
from jax.experimental.pallas import tpu as pltpu
from jax.sharding import PartitionSpec as P

BS = 256
R = 32

STEP_SIZE = 0.5
REF_FRICTION = 0.6
LIMIT = 16 * 1024 * 1024
F32 = jnp.float32
BF16 = jnp.bfloat16


def dot(a, b):
    return jnp.dot(a, b, preferred_element_type=F32)


def dot_t(a, b):
    return lax.dot_general(a, b, (((0,), (0,)), ((), ())), preferred_element_type=F32)


VMEM = pl.BlockSpec(memory_space=pltpu.VMEM)


def call(kernel, outs, *operands, specs=None, **grid):
    return pl.pallas_call(
        kernel,
        in_specs=specs or [VMEM] * len(operands),
        out_shape=outs,
        compiler_params=pltpu.CompilerParams(vmem_limit_bytes=LIMIT),
        **grid,
    )(*operands)


def rows_at(n, size):
    return pl.ds(pl.multiple_of(n * size, size), size)


HBM = pl.BlockSpec(memory_space=pl.ANY)


def in_hbm(*arrays):
    return [pltpu.with_memory_space_constraint(array, pltpu.HBM) for array in arrays]


def start_copies(pairs, sems, first=0):
    copies = [pltpu.make_async_copy(a, b, sems.at[first + k]) for k, (a, b) in enumerate(pairs)]
    for copy in copies:
        copy.start()
    return copies


def fill_edges(first, last, pair_ref, cross_ref):
    even = lax.rem(lax.axis_index("col"), 2) == 0
    pair_ref[...] = jnp.where(even, last, first)
    cross_ref[...] = jnp.where(even, first, last)


def project_kernel(slip_ref, basis_ref, coeff_ref, rounded_ref, pair_ref, cross_ref):
    for n in range(slip_ref.shape[0] // BS):
        at = pl.ds(n * BS, BS)
        rounded = slip_ref[at, :].astype(BF16)
        rounded_ref[at, :] = rounded
        coeff_ref[n * R : (n + 1) * R, :] = dot(basis_ref[:, at], rounded).astype(BF16)
    fill_edges(rounded_ref[:BS], rounded_ref[-BS:], pair_ref, cross_ref)


def project(slip, basis_in):
    patches, ens = slip.shape
    edge = jax.ShapeDtypeStruct((BS, ens), BF16)
    return call(
        project_kernel,
        [
            jax.ShapeDtypeStruct((patches // BS * R, ens), BF16),
            jax.ShapeDtypeStruct((patches, ens), BF16),
            edge,
            edge,
        ],
        slip,
        basis_in,
    )


def ranks_kernel(
    col_count, rank_hbm, now_hbm, rate_hbm, wide_ref, joined_ref, rank_ref, sems
):
    sources, share, blocks = rank_ref.shape
    ens = now_hbm.shape[1]
    copies = start_copies(
        [
            (rank_hbm, rank_ref),
            (now_hbm, joined_ref.at[:, pl.ds(0, ens)]),
            (rate_hbm, joined_ref.at[:, pl.ds(ens, ens)]),
        ],
        sems,
    )
    width = share * R
    column = lax.broadcasted_iota(jnp.int32, (share, width), 1)
    spread = (lax.div(column, R) == lax.broadcasted_iota(jnp.int32, (share, width), 0)).astype(F32).astype(BF16)
    level = lax.rem(lax.broadcasted_iota(jnp.int32, (blocks, width), 1), R).astype(F32)
    receiver = lax.axis_index("row") * blocks + lax.broadcasted_iota(jnp.int32, (share, blocks), 1)
    copies[0].wait()
    for source in range(sources):
        own = (source * col_count + lax.axis_index("col")) * share + lax.broadcasted_iota(jnp.int32, (share, blocks), 0)
        rank = jnp.where(jnp.abs(receiver - own) > 1, rank_ref[source], 0).astype(F32)
        wide = dot_t(rank.astype(BF16), spread)
        wide_ref[source] = jnp.where(level < wide, wide, 0.0)
    copies[1].wait()
    copies[2].wait()


def side_by_side_kernel(*refs):
    pieces, out_ref = refs[:-1], refs[-1]
    size = pieces[0].shape[0]
    for k, piece in enumerate(pieces):
        out_ref[k * size : (k + 1) * size, :] = piece[...]


def weights_kernel(heights, size, start, *refs):
    begun = start > 0
    sources, rest = refs[:9], refs[9:]
    near_hbm, state_hbm, begun_ref = rest[:3] if begun else (None, None, None)
    rest = rest[4:] if begun else rest[1:]
    numbers_ref, matrix_ref = rest[:2]
    near_ref, state_ref = rest[2:4] if begun else (None, None)
    vectors, lists, sems = rest[-5], rest[-4:-1], rest[-1]
    targets = [vectors.at[k] for k in range(6)] + list(lists)
    copies = start_copies(list(zip(sources, targets)), sems)
    large = [(near_hbm, near_ref), (state_hbm, state_ref)] if begun else []
    large = start_copies(large, sems, len(targets))
    if begun:
        numbers_ref[:start, :] = begun_ref[...]
    count_ref, bricks_ref, weight_ref = lists
    slots = bricks_ref.shape[0]
    col = lax.axis_index("col")
    height, core = lax.div(col, 2).astype(F32), lax.rem(col, 2).astype(F32)
    group, lanes, unrolled = 16, 128, 8
    for copy in copies:
        copy.wait()

    @pl.loop(0, matrix_ref.shape[1] // lanes)
    def _(n):
        own_at = rows_at(n, lanes)
        at = pl.ds(pl.multiple_of(start + n * lanes, lanes), lanes)
        load, normal, direct, evolution, distance, stiffness = (vectors[k, :, at] for k in range(6))
        rows = [load, normal, 1.0 / direct, 1.0 / evolution, evolution / distance, stiffness, load, normal]
        numbers_ref[at if begun else own_at, :] = jnp.concatenate(rows, axis=0).T
        bricks = bricks_ref[:, at].astype(F32)
        live = lax.broadcasted_iota(jnp.int32, (slots, lanes), 0) < count_ref[:, at]
        weights = jnp.where(live, weight_ref[:, at], 0.0)
        merged = jnp.zeros((slots, lanes), F32)
        for k in range(slots):
            merged = merged + jnp.where(bricks == bricks[k : k + 1], weights[k : k + 1], 0.0)
        shares = merged / jnp.sum(weights, axis=0, keepdims=True)
        owner = jnp.floor((bricks + 0.5) * (1.0 / size))
        chip = jnp.floor(owner * 0.5 + 0.25)
        away = height - chip
        away = jnp.where(away < 0, away + heights, away)
        other = jnp.where(owner - 2.0 * chip == core, 0.0, float(heights))
        place = jnp.where(live, (other + away - owner) * size + bricks, -1.0)
        high = jnp.floor((place + 0.5) * (1.0 / group))
        low = place - high * group
        spread = lambda rows, k: jnp.broadcast_to(rows[k : k + 1], (group, lanes)).astype(BF16)
        line = lax.broadcasted_iota(jnp.int32, (group, lanes), 0).astype(F32).astype(BF16)
        none = jnp.full((group, lanes), -1.0, BF16)
        highs = [jnp.where(spread(low, k) == line, spread(high, k), none) for k in range(slots)]
        values = [spread(shares, k) for k in range(slots)]

        @pl.loop(0, matrix_ref.shape[0] // (group * unrolled))
        def _(m):
            first = jnp.full((group, lanes), (m * unrolled).astype(F32)).astype(BF16)
            for step in range(unrolled):
                here = first + jnp.asarray(step, BF16)
                tile = jnp.zeros((group, lanes), BF16)
                for k in range(slots):
                    tile = jnp.where(highs[k] == here, values[k], tile)
                to = pl.ds(pl.multiple_of((m * unrolled + step) * group, group), group)
                matrix_ref[to, own_at] = tile

    for copy in large:
        copy.wait()


def couple_kernel(sources, heights, flip, matrix_ref, *refs):
    coeffs, edges, out_ref = refs[:sources], refs[sources:-1], refs[-1]
    share = coeffs[0].shape[0]
    row, col = lax.axis_index("row"), lax.axis_index("col")
    height, core = lax.div(col, 2), lax.rem(col + flip, 2)

    @pl.loop(0, heights, unroll=True)
    def _(d):
        partner = lax.rem(d, 2) * (1 - 2 * lax.rem(height, 2))
        at = rows_at(2 * lax.rem(height + partner + d - lax.rem(d, 2) + heights, heights) + core, share)
        total = None
        for step in range(sources):
            term = dot(matrix_ref[lax.rem(row + (sources - step), sources), at, :], coeffs[step][...])
            total = term if total is None else total + term
        out_ref[rows_at(d, share), :] = total.astype(out_ref.dtype)

    for edge in edges:
        out_ref[heights * share :, :] = edge[...]


def couple(flip, matrix, coeffs, heights, kind, *edges):
    share, ens = coeffs[0].shape
    return call(
        functools.partial(couple_kernel, len(coeffs), heights, flip),
        jax.ShapeDtypeStruct((heights * share + len(edges) * BS, ens), kind),
        matrix,
        *coeffs,
        *edges,
    )


def chip_sum_kernel(kept_ref, sent_ref, own_ref, direct_ref, pass_ref, keep_ref):
    share = own_ref.shape[0]
    group = 32
    for place in range(2 + 2 * (keep_ref.shape[0] // share)):
        far = place // 2 - 1
        out_ref = (own_ref, direct_ref)[place % 2] if far < 0 else (keep_ref, pass_ref)[place % 2]

        @pl.loop(0, share // group)
        def _(n):
            at = pl.ds(pl.multiple_of(place * share + n * group, group), group)
            to = pl.ds(pl.multiple_of(max(far, 0) * share + n * group, group), group)
            out_ref[to, :] = (kept_ref[at, :] + sent_ref[at, :].astype(F32)).astype(out_ref.dtype)


def chip_sum(kept, sent, heights):
    rows, ens = kept.shape
    share = rows // heights
    far = (heights // 2 - 1) * share
    shapes = [(share, BF16), (share, BF16), (far, BF16), (far, F32)]
    return call(chip_sum_kernel, [jax.ShapeDtypeStruct((n, ens), kind) for n, kind in shapes], kept, sent)


def pair_sum_kernel(keep_ref, came_ref, *outs):
    share = outs[0].shape[0]
    group = 32
    for far, out_ref in enumerate(outs):

        @pl.loop(0, share // group)
        def _(n):
            at = pl.ds(pl.multiple_of(far * share + n * group, group), group)
            out_ref[rows_at(n, group), :] = (keep_ref[at, :] + came_ref[at, :].astype(F32)).astype(BF16)


def near_tau(n, slip, numbers, near_ref, rounded_ref):
    count = rounded_ref.shape[0] // BS
    at = rows_at(n, BS)
    none = jnp.zeros((BS, rounded_ref.shape[1]), BF16)
    before = jnp.where(n == 0, none, rounded_ref[rows_at(jnp.maximum(n - 1, 0), BS), :])
    after = jnp.where(n == count - 1, none, rounded_ref[rows_at(jnp.minimum(n + 1, count - 1), BS), :])
    near = dot(near_ref[0, at, :], before) + dot(near_ref[1, at, :], rounded_ref[at, :]) + dot(near_ref[2, at, :], after)
    return numbers[:, 0:1] - numbers[:, 5:6] * slip - near


def prepare_first_kernel(
    low_ref, high_ref, own_ref, other_ref, slip_ref, state_ref, numbers_ref, near_ref, rounded_ref,
    shift_ref, scale_ref, rest_ref, scale_mid_ref,
):
    half = own_ref.shape[0]
    ens = slip_ref.shape[1]
    blocks = low_ref.shape[1] // BS

    def block(matrix_ref, m, n):
        at, own_at = rows_at(n, BS), rows_at(m, BS)
        total = dot_t(matrix_ref[:half, own_at], own_ref[...]) + dot_t(matrix_ref[half:, own_at], other_ref[...])
        numbers = numbers_ref[at, :]
        normal, inv_direct, inv_evolution, ratio = (numbers[:, k : k + 1] for k in range(1, 5))
        base = total[:, :ens]
        scale = inv_direct / (normal - base)
        scale_ref[at, :] = scale
        scale_mid_ref[at, :] = inv_direct / (normal - (base + STEP_SIZE * total[:, ens:]))
        state = state_ref[at, :]
        tau = near_tau(n, slip_ref[at, :], numbers, near_ref, rounded_ref)
        shift_ref[at, :] = tau * scale - state * inv_direct
        rest_ref[at, :] = state + (STEP_SIZE * ratio) * jnp.exp((REF_FRICTION - state) * inv_evolution)

    @pl.loop(0, blocks, unroll=2)
    def _(m):
        block(low_ref, m, m)

    @pl.loop(0, blocks, unroll=2)
    def _(m):
        block(high_ref, m, blocks + m)


def over_blocks(block, basis_ref, near_ref, parts, pair_ref, cross_ref):
    count = near_ref.shape[1] // BS

    def far(n):
        levels = rows_at(n, R)
        total = parts[0][levels, :].astype(F32)
        for part in parts[1:]:
            total = total + part[levels, :].astype(F32)
        return dot_t(basis_ref[:, rows_at(n, BS)], total.astype(BF16))

    even = lax.rem(lax.axis_index("col"), 2) == 0
    pair, cross = pair_ref[-BS:], cross_ref[...]
    block(0, far(0) + dot(near_ref[0, :BS, :], jnp.where(even, cross, pair)))

    @pl.loop(1, count - 1, unroll=True)
    def _(n):
        block(n, far(n))

    block(count - 1, far(count - 1) + dot(near_ref[2, -BS:, :], jnp.where(even, pair, cross)))


def finish_first_kernel(
    count, shift_ref, scale_ref, slip_ref, basis_out_ref, basis_in_ref, near_ref, *refs
):
    parts, pair_ref, cross_ref = refs[:count], refs[count], refs[count + 1]
    speed_ref, rounded_ref, coeff_ref, pair_out, cross_out = refs[count + 2 :]

    def block(n, outer):
        at = rows_at(n, BS)
        speed = jnp.exp(shift_ref[at, :] - scale_ref[at, :] * outer)
        speed_ref[at, :] = speed
        rounded = (slip_ref[at, :] + STEP_SIZE * speed).astype(BF16)
        rounded_ref[at, :] = rounded
        coeff_ref[rows_at(n, R), :] = dot(basis_in_ref[:, at], rounded).astype(BF16)

    over_blocks(block, basis_out_ref, near_ref, parts, pair_ref, cross_ref)
    fill_edges(rounded_ref[:BS], rounded_ref[-BS:], pair_out, cross_out)


def prepare_second_kernel(
    slip_ref, state_ref, speed_ref, part_ref, scale_ref, numbers_ref, near_ref, rounded_ref,
    shift_ref, slip_rest_ref, rest_ref,
):
    @pl.loop(0, slip_ref.shape[0] // BS, unroll=2)
    def _(n):
        at = rows_at(n, BS)
        numbers = numbers_ref[at, :]
        inv_direct, inv_evolution, ratio = (numbers[:, k : k + 1] for k in range(2, 5))
        speed = speed_ref[at, :]
        slip = slip_ref[at, :] + STEP_SIZE * speed
        state = part_ref[at, :] - (STEP_SIZE * ratio) * speed
        tau = near_tau(n, slip, numbers, near_ref, rounded_ref)
        shift_ref[at, :] = tau * scale_ref[at, :] - state * inv_direct
        slip_rest_ref[at, :] = 0.5 * (slip_ref[at, :] + slip)
        friction = jnp.exp((REF_FRICTION - state) * inv_evolution)
        rest_ref[at, :] = 0.5 * (state_ref[at, :] + state) + (0.5 * STEP_SIZE * ratio) * friction


def finish_second_kernel(
    count, shift_ref, scale_ref, rest_ref, slip_rest_ref, numbers_ref, basis_out_ref, near_ref, *refs
):
    parts, pair_ref, cross_ref = refs[:count], refs[count], refs[count + 1]
    slip_hbm, state_hbm, slip_ref, state_ref, sems = refs[count + 2 :]

    def copies(n):
        at = rows_at(n, BS)
        return [
            pltpu.make_async_copy(slip_ref.at[at, :], slip_hbm.at[at, :], sems.at[0, n]),
            pltpu.make_async_copy(state_ref.at[at, :], state_hbm.at[at, :], sems.at[1, n]),
        ]

    def block(n, outer):
        at = rows_at(n, BS)
        speed = jnp.exp(shift_ref[at, :] - scale_ref[at, :] * outer)
        slip_ref[at, :] = slip_rest_ref[at, :] + (0.5 * STEP_SIZE) * speed
        state_ref[at, :] = rest_ref[at, :] - (0.5 * STEP_SIZE * numbers_ref[at, 4:5]) * speed
        for copy in copies(n):
            copy.start()

    over_blocks(block, basis_out_ref, near_ref, parts, pair_ref, cross_ref)

    @pl.loop(0, slip_ref.shape[0] // BS)
    def _(n):
        for copy in copies(n):
            copy.wait()


def masked_coupling(coupling, wide):
    rows, sources, width = coupling.shape
    blocks = rows // R
    keep = jnp.arange(R, dtype=jnp.int32).astype(F32)[None, None, :, None] < wide[:, :, None, :]
    matrix = jnp.transpose(coupling, (1, 0, 2)).reshape(sources, blocks, R, width)
    masked = jnp.where(keep, matrix, jnp.zeros((), BF16)).reshape(sources, rows, width)
    return pltpu.with_memory_space_constraint(masked, pltpu.VMEM)


def per_device(
    slip,
    state,
    tau_load,
    normal_stress,
    direct_effect,
    evolution_effect,
    slip_distance,
    self_stiffness,
    near_blocks,
    basis_in,
    basis_out,
    coupling,
    block_rank,
    adj_bricks,
    adj_count,
    adj_weight,
    pressure_now,
    pressure_rate,
):
    row_count = lax.axis_size("row")
    col_count = lax.axis_size("col")
    row_index = lax.axis_index("row")
    col_index = lax.axis_index("col")
    heights = col_count // 2
    height, core = col_index // 2, col_index % 2
    both = ("row", "col")
    devices = row_count * col_count

    def to_row(array, d):
        return lax.ppermute(array, "row", [(i, (i + d) % row_count) for i in range(row_count)])

    def to_height(array, d):
        pairs = [(2 * z + k, 2 * ((z + d) % heights) + k) for z in range(heights) for k in range(2)]
        return lax.ppermute(array, "col", pairs)

    def to_core(array):
        return lax.ppermute(array, "col", [(2 * z + k, 2 * z + 1 - k) for z in range(heights) for k in range(2)])

    def to_chip(array):
        ends = [(i, i + 1) for i in range(1, devices - 1, 2)]
        return lax.ppermute(array, both, ends + [(j, i) for i, j in ends])

    patches, ens = slip.shape
    slots = adj_bricks.shape[0]
    size = pressure_now.shape[0]
    share = coupling.shape[2]
    def to_partner(array):
        pairs = [(2 * z + k, 2 * (z + 1 - 2 * (z % 2)) + k) for z in range(heights) for k in range(2)]
        return lax.ppermute(array, "col", pairs)

    def first_step(coeffs, pair, cross, later):
        sent = to_core(couple(1, masked, coeffs, heights, BF16, pair))
        kept = couple(0, masked, coeffs, heights, F32)
        own, direct, passed, keep = chip_sum(kept, sent, heights)
        if not later:
            own, cross = lax.optimization_barrier((own, cross))
        return own, to_partner(passed), to_partner(direct), keep, sent, cross if later else to_chip(cross)

    def second_step(own, came, direct, keep, sent, cross, later):
        sums = call(pair_sum_kernel, [jax.ShapeDtypeStruct((share, ens), BF16)] * (heights // 2 - 1), keep, came)
        if later:
            sums, cross = lax.optimization_barrier((sums, cross))
            cross = to_chip(cross)
        return [to_height(part, 2 * (d + 1)) for d, part in enumerate(sums)] + [own, direct, sent, cross]

    def row_coeffs(coeff):
        return [coeff] + [to_row(coeff, d) for d in range(1, row_count)]

    full = jax.ShapeDtypeStruct((patches, ens), F32)
    half = jax.ShapeDtypeStruct((patches, ens), BF16)
    edge = jax.ShapeDtypeStruct((BS, ens), BF16)
    per_patch = [tau_load, normal_stress, direct_effect, evolution_effect, slip_distance, self_stiffness]

    ranks = jnp.transpose(block_rank, (1, 2, 0))
    wide, joined = call(
        functools.partial(ranks_kernel, col_count),
        [
            jax.ShapeDtypeStruct((ranks.shape[0], ranks.shape[2], share), F32),
            jax.ShapeDtypeStruct((size, 2 * ens), BF16),
        ],
        *in_hbm(ranks, pressure_now, pressure_rate),
        specs=[HBM] * 3,
        scratch_shapes=[pltpu.VMEM(ranks.shape, jnp.int32), pltpu.SemaphoreType.DMA((3,))],
    )
    fields = [joined] + [to_height(joined, d) for d in range(1, heights)]
    masked = masked_coupling(coupling, wide)
    masked, slip = lax.optimization_barrier((masked, slip))
    coeff, rounded, pair, cross = project(slip, basis_in)
    coeffs = row_coeffs(coeff)
    brick_lists = [adj_count[None], adj_bricks, adj_weight]
    columns = [array[None] for array in per_patch] + brick_lists
    start = patches // 2
    part = jax.ShapeDtypeStruct((2 * heights * size, start), BF16)
    scratch = [
        pltpu.VMEM((6, 1, patches), F32),
        pltpu.VMEM((1, patches), jnp.int32),
        pltpu.VMEM(adj_bricks.shape, jnp.int32),
        pltpu.VMEM(adj_weight.shape, F32),
        pltpu.SemaphoreType.DMA((11,)),
    ]
    numbers, low = call(
        functools.partial(weights_kernel, heights, size, 0),
        [jax.ShapeDtypeStruct((start, 8), F32), part],
        *in_hbm(*columns),
        coeff,
        specs=[HBM] * 9 + [VMEM],
        scratch_shapes=scratch,
    )
    fields, coeffs, low = lax.optimization_barrier((fields, coeffs, low))
    own = call(
        side_by_side_kernel, jax.ShapeDtypeStruct((heights * size, 2 * ens), BF16), *fields
    )
    other = to_core(own)
    own_part, came, direct, keep, sent, cross = first_step(coeffs, pair, cross, True)
    numbers, high, near, state = call(
        functools.partial(weights_kernel, heights, size, start),
        [jax.ShapeDtypeStruct((patches, 8), F32), part, jax.ShapeDtypeStruct(near_blocks.shape, BF16), full],
        *in_hbm(*columns, near_blocks, state),
        numbers,
        own_part,
        specs=[HBM] * 11 + [VMEM] * 2,
        scratch_shapes=scratch,
    )
    came, high = lax.optimization_barrier((came, high))
    outer = second_step(own_part, came, direct, keep, sent, cross, True)
    shift, scale, rest, scale_mid = call(
        prepare_first_kernel, [full] * 4, low, high, own, other, slip, state, numbers, near, rounded
    )
    speed, rounded, coeff, pair, cross = call(
        functools.partial(finish_first_kernel, len(outer) - 2),
        [full, half, jax.ShapeDtypeStruct((patches // BS * R, ens), BF16), edge, edge],
        shift, scale, slip, basis_out, basis_in, near, *outer,
    )
    coeffs = row_coeffs(coeff)
    outer = second_step(*first_step(coeffs, pair, cross, False), False)
    shift, slip_rest, rest = call(
        prepare_second_kernel, [full] * 3,
        slip, state, speed, rest, scale_mid, numbers, near, rounded,
    )
    slip_out, state_out = call(
        functools.partial(finish_second_kernel, len(outer) - 2),
        [full] * 2,
        shift, scale_mid, rest, slip_rest, numbers, basis_out, near, *outer,
        out_specs=[HBM] * 2,
        scratch_shapes=[
            pltpu.VMEM((patches, ens), F32),
            pltpu.VMEM((patches, ens), F32),
            pltpu.SemaphoreType.DMA((2, patches // BS)),
        ],
    )
    return (slip_out, state_out)


def solution(mesh):
    in_specs = (
        P(("row", "col"), None),
        P(("row", "col"), None),
        P(("row", "col")),
        P(("row", "col")),
        P(("row", "col")),
        P(("row", "col")),
        P(("row", "col")),
        P(("row", "col")),
        P(None, ("row", "col"), None),
        P(None, ("row", "col")),
        P(None, ("row", "col")),
        P("row", None, "col"),
        P("row", None, "col"),
        P(None, ("row", "col")),
        P(("row", "col")),
        P(None, ("row", "col")),
        P("col", None),
        P("col", None),
    )
    out_specs = (P(("row", "col"), None), P(("row", "col"), None))
    return jax.shard_map(
        per_device, mesh=mesh, in_specs=in_specs, out_specs=out_specs, check_vma=False
    )
```

```python
import functools

import jax
import jax.numpy as jnp
from jax import lax
from jax.experimental import pallas as pl
from jax.experimental.pallas import tpu as pltpu
from jax.sharding import PartitionSpec as P

BS = 256
R = 32

STEP_SIZE = 0.5
REF_FRICTION = 0.6
LIMIT = 16 * 1024 * 1024
F32 = jnp.float32
BF16 = jnp.bfloat16


def dot(a, b):
    return jnp.dot(a, b, preferred_element_type=F32)


def dot_t(a, b):
    return lax.dot_general(a, b, (((0,), (0,)), ((), ())), preferred_element_type=F32)


VMEM = pl.BlockSpec(memory_space=pltpu.VMEM)


def call(kernel, outs, *operands, specs=None, **grid):
    return pl.pallas_call(
        kernel,
        in_specs=specs or [VMEM] * len(operands),
        out_shape=outs,
        compiler_params=pltpu.CompilerParams(vmem_limit_bytes=LIMIT),
        **grid,
    )(*operands)


def rows_at(n, size):
    return pl.ds(pl.multiple_of(n * size, size), size)


HBM = pl.BlockSpec(memory_space=pl.ANY)


def in_hbm(*arrays):
    return [pltpu.with_memory_space_constraint(array, pltpu.HBM) for array in arrays]


def start_copies(pairs, sems, first=0):
    copies = [pltpu.make_async_copy(a, b, sems.at[first + k]) for k, (a, b) in enumerate(pairs)]
    for copy in copies:
        copy.start()
    return copies


def fill_edges(first, last, pair_ref, cross_ref):
    even = lax.rem(lax.axis_index("col"), 2) == 0
    pair_ref[...] = jnp.where(even, last, first)
    cross_ref[...] = jnp.where(even, first, last)


def project_kernel(slip_ref, basis_ref, coeff_ref, rounded_ref, pair_ref, cross_ref):
    for n in range(slip_ref.shape[0] // BS):
        at = pl.ds(n * BS, BS)
        rounded = slip_ref[at, :].astype(BF16)
        rounded_ref[at, :] = rounded
        coeff_ref[n * R : (n + 1) * R, :] = dot(basis_ref[:, at], rounded).astype(BF16)
    fill_edges(rounded_ref[:BS], rounded_ref[-BS:], pair_ref, cross_ref)


def project(slip, basis_in):
    patches, ens = slip.shape
    edge = jax.ShapeDtypeStruct((BS, ens), BF16)
    return call(
        project_kernel,
        [
            jax.ShapeDtypeStruct((patches // BS * R, ens), BF16),
            jax.ShapeDtypeStruct((patches, ens), BF16),
            edge,
            edge,
        ],
        slip,
        basis_in,
    )


def ranks_kernel(
    col_count, rank_hbm, now_hbm, rate_hbm, wide_ref, joined_ref, rank_ref, sems
):
    sources, share, blocks = rank_ref.shape
    ens = now_hbm.shape[1]
    copies = start_copies(
        [
            (rank_hbm, rank_ref),
            (now_hbm, joined_ref.at[:, pl.ds(0, ens)]),
            (rate_hbm, joined_ref.at[:, pl.ds(ens, ens)]),
        ],
        sems,
    )
    width = share * R
    column = lax.broadcasted_iota(jnp.int32, (share, width), 1)
    spread = (lax.div(column, R) == lax.broadcasted_iota(jnp.int32, (share, width), 0)).astype(F32).astype(BF16)
    level = lax.rem(lax.broadcasted_iota(jnp.int32, (blocks, width), 1), R).astype(F32)
    receiver = lax.axis_index("row") * blocks + lax.broadcasted_iota(jnp.int32, (share, blocks), 1)
    copies[0].wait()
    for source in range(sources):
        own = (source * col_count + lax.axis_index("col")) * share + lax.broadcasted_iota(jnp.int32, (share, blocks), 0)
        rank = jnp.where(jnp.abs(receiver - own) > 1, rank_ref[source], 0).astype(F32)
        wide = dot_t(rank.astype(BF16), spread)
        wide_ref[source] = jnp.where(level < wide, wide, 0.0)
    copies[1].wait()
    copies[2].wait()


def side_by_side_kernel(*refs):
    pieces, out_ref = refs[:-1], refs[-1]
    size = pieces[0].shape[0]
    for k, piece in enumerate(pieces):
        out_ref[k * size : (k + 1) * size, :] = piece[...]


def weights_kernel(heights, size, start, *refs):
    begun = start > 0
    sources, rest = refs[:9], refs[9:]
    near_hbm, state_hbm, begun_ref = rest[:3] if begun else (None, None, None)
    rest = rest[4:] if begun else rest[1:]
    numbers_ref, matrix_ref = rest[:2]
    near_ref, state_ref = rest[2:4] if begun else (None, None)
    vectors, lists, sems = rest[-5], rest[-4:-1], rest[-1]
    targets = [vectors.at[k] for k in range(6)] + list(lists)
    copies = start_copies(list(zip(sources, targets)), sems)
    large = [(near_hbm, near_ref), (state_hbm, state_ref)] if begun else []
    large = start_copies(large, sems, len(targets))
    if begun:
        numbers_ref[:start, :] = begun_ref[...]
    count_ref, bricks_ref, weight_ref = lists
    slots = bricks_ref.shape[0]
    col = lax.axis_index("col")
    height, core = lax.div(col, 2).astype(F32), lax.rem(col, 2).astype(F32)
    group, lanes, unrolled = 16, 128, 8
    for copy in copies:
        copy.wait()

    @pl.loop(0, matrix_ref.shape[1] // lanes)
    def _(n):
        own_at = rows_at(n, lanes)
        at = pl.ds(pl.multiple_of(start + n * lanes, lanes), lanes)
        load, normal, direct, evolution, distance, stiffness = (vectors[k, :, at] for k in range(6))
        rows = [load, normal, 1.0 / direct, 1.0 / evolution, evolution / distance, stiffness, load, normal]
        numbers_ref[at if begun else own_at, :] = jnp.concatenate(rows, axis=0).T
        bricks = bricks_ref[:, at].astype(F32)
        live = lax.broadcasted_iota(jnp.int32, (slots, lanes), 0) < count_ref[:, at]
        weights = jnp.where(live, weight_ref[:, at], 0.0)
        merged = jnp.zeros((slots, lanes), F32)
        for k in range(slots):
            merged = merged + jnp.where(bricks == bricks[k : k + 1], weights[k : k + 1], 0.0)
        shares = merged / jnp.sum(weights, axis=0, keepdims=True)
        owner = jnp.floor((bricks + 0.5) * (1.0 / size))
        chip = jnp.floor(owner * 0.5 + 0.25)
        away = height - chip
        away = jnp.where(away < 0, away + heights, away)
        other = jnp.where(owner - 2.0 * chip == core, 0.0, float(heights))
        place = jnp.where(live, (other + away - owner) * size + bricks, -1.0)
        high = jnp.floor((place + 0.5) * (1.0 / group))
        low = place - high * group
        spread = lambda rows, k: jnp.broadcast_to(rows[k : k + 1], (group, lanes)).astype(BF16)
        line = lax.broadcasted_iota(jnp.int32, (group, lanes), 0).astype(F32).astype(BF16)
        none = jnp.full((group, lanes), -1.0, BF16)
        highs = [jnp.where(spread(low, k) == line, spread(high, k), none) for k in range(slots)]
        values = [spread(shares, k) for k in range(slots)]

        @pl.loop(0, matrix_ref.shape[0] // (group * unrolled))
        def _(m):
            first = jnp.full((group, lanes), (m * unrolled).astype(F32)).astype(BF16)
            for step in range(unrolled):
                here = first + jnp.asarray(step, BF16)
                tile = jnp.zeros((group, lanes), BF16)
                for k in range(slots):
                    tile = jnp.where(highs[k] == here, values[k], tile)
                to = pl.ds(pl.multiple_of((m * unrolled + step) * group, group), group)
                matrix_ref[to, own_at] = tile

    for copy in large:
        copy.wait()


def couple_kernel(sources, heights, flip, matrix_ref, *refs):
    coeffs, edges, out_ref = refs[:sources], refs[sources:-1], refs[-1]
    share = coeffs[0].shape[0]
    row, col = lax.axis_index("row"), lax.axis_index("col")
    height, core = lax.div(col, 2), lax.rem(col + flip, 2)

    @pl.loop(0, heights, unroll=True)
    def _(d):
        partner = lax.rem(d, 2) * (1 - 2 * lax.rem(height, 2))
        at = rows_at(2 * lax.rem(height + partner + d - lax.rem(d, 2) + heights, heights) + core, share)
        total = None
        for step in range(sources):
            term = dot(matrix_ref[lax.rem(row + (sources - step), sources), at, :], coeffs[step][...])
            total = term if total is None else total + term
        out_ref[rows_at(d, share), :] = total.astype(out_ref.dtype)

    for edge in edges:
        out_ref[heights * share :, :] = edge[...]


def couple(flip, matrix, coeffs, heights, kind, *edges):
    share, ens = coeffs[0].shape
    return call(
        functools.partial(couple_kernel, len(coeffs), heights, flip),
        jax.ShapeDtypeStruct((heights * share + len(edges) * BS, ens), kind),
        matrix,
        *coeffs,
        *edges,
    )


def chip_sum_kernel(kept_ref, sent_ref, own_ref, direct_ref, pass_ref, keep_ref):
    share = own_ref.shape[0]
    group = 32
    for place in range(2 + 2 * (keep_ref.shape[0] // share)):
        far = place // 2 - 1
        out_ref = (own_ref, direct_ref)[place % 2] if far < 0 else (keep_ref, pass_ref)[place % 2]

        @pl.loop(0, share // group)
        def _(n):
            at = pl.ds(pl.multiple_of(place * share + n * group, group), group)
            to = pl.ds(pl.multiple_of(max(far, 0) * share + n * group, group), group)
            out_ref[to, :] = (kept_ref[at, :] + sent_ref[at, :].astype(F32)).astype(out_ref.dtype)


def chip_sum(kept, sent, heights):
    rows, ens = kept.shape
    share = rows // heights
    far = (heights // 2 - 1) * share
    shapes = [(share, BF16), (share, BF16), (far, BF16), (far, F32)]
    return call(chip_sum_kernel, [jax.ShapeDtypeStruct((n, ens), kind) for n, kind in shapes], kept, sent)


def pair_sum_kernel(keep_ref, came_ref, *outs):
    share = outs[0].shape[0]
    group = 32
    for far, out_ref in enumerate(outs):

        @pl.loop(0, share // group)
        def _(n):
            at = pl.ds(pl.multiple_of(far * share + n * group, group), group)
            out_ref[rows_at(n, group), :] = (keep_ref[at, :] + came_ref[at, :].astype(F32)).astype(BF16)


def near_tau(n, slip, numbers, near_ref, rounded_ref):
    count = rounded_ref.shape[0] // BS
    at = rows_at(n, BS)
    none = jnp.zeros((BS, rounded_ref.shape[1]), BF16)
    before = jnp.where(n == 0, none, rounded_ref[rows_at(jnp.maximum(n - 1, 0), BS), :])
    after = jnp.where(n == count - 1, none, rounded_ref[rows_at(jnp.minimum(n + 1, count - 1), BS), :])
    near = dot(near_ref[0, at, :], before) + dot(near_ref[1, at, :], rounded_ref[at, :]) + dot(near_ref[2, at, :], after)
    return numbers[:, 0:1] - numbers[:, 5:6] * slip - near


def prepare_first_kernel(
    low_ref, high_ref, own_ref, other_ref, slip_ref, state_ref, numbers_ref, near_ref, rounded_ref,
    shift_ref, scale_ref, rest_ref, scale_mid_ref,
):
    half = own_ref.shape[0]
    ens = slip_ref.shape[1]
    blocks = low_ref.shape[1] // BS

    def block(matrix_ref, m, n):
        at, own_at = rows_at(n, BS), rows_at(m, BS)
        total = dot_t(matrix_ref[:half, own_at], own_ref[...]) + dot_t(matrix_ref[half:, own_at], other_ref[...])
        numbers = numbers_ref[at, :]
        normal, inv_direct, inv_evolution, ratio = (numbers[:, k : k + 1] for k in range(1, 5))
        base = total[:, :ens]
        scale = inv_direct / (normal - base)
        scale_ref[at, :] = scale
        scale_mid_ref[at, :] = inv_direct / (normal - (base + STEP_SIZE * total[:, ens:]))
        state = state_ref[at, :]
        tau = near_tau(n, slip_ref[at, :], numbers, near_ref, rounded_ref)
        shift_ref[at, :] = tau * scale - state * inv_direct
        rest_ref[at, :] = state + (STEP_SIZE * ratio) * jnp.exp((REF_FRICTION - state) * inv_evolution)

    @pl.loop(0, blocks, unroll=2)
    def _(m):
        block(low_ref, m, m)

    @pl.loop(0, high_ref.shape[1] // BS, unroll=2)
    def _(m):
        block(high_ref, m, blocks + m)


def over_blocks(block, basis_ref, near_ref, parts, pair_ref, cross_ref):
    count = near_ref.shape[1] // BS

    def far(n):
        levels = rows_at(n, R)
        total = parts[0][levels, :].astype(F32)
        for part in parts[1:]:
            total = total + part[levels, :].astype(F32)
        return dot_t(basis_ref[:, rows_at(n, BS)], total.astype(BF16))

    even = lax.rem(lax.axis_index("col"), 2) == 0
    pair, cross = pair_ref[-BS:], cross_ref[...]
    block(0, far(0) + dot(near_ref[0, :BS, :], jnp.where(even, cross, pair)))

    @pl.loop(1, count - 1, unroll=True)
    def _(n):
        block(n, far(n))

    block(count - 1, far(count - 1) + dot(near_ref[2, -BS:, :], jnp.where(even, pair, cross)))


def finish_first_kernel(
    count, shift_ref, scale_ref, slip_ref, basis_out_ref, basis_in_ref, near_ref, *refs
):
    parts, pair_ref, cross_ref = refs[:count], refs[count], refs[count + 1]
    speed_ref, rounded_ref, coeff_ref, pair_out, cross_out = refs[count + 2 :]

    def block(n, outer):
        at = rows_at(n, BS)
        speed = jnp.exp(shift_ref[at, :] - scale_ref[at, :] * outer)
        speed_ref[at, :] = speed
        rounded = (slip_ref[at, :] + STEP_SIZE * speed).astype(BF16)
        rounded_ref[at, :] = rounded
        coeff_ref[rows_at(n, R), :] = dot(basis_in_ref[:, at], rounded).astype(BF16)

    over_blocks(block, basis_out_ref, near_ref, parts, pair_ref, cross_ref)
    fill_edges(rounded_ref[:BS], rounded_ref[-BS:], pair_out, cross_out)


def prepare_second_kernel(
    slip_ref, state_ref, speed_ref, part_ref, scale_ref, numbers_ref, near_ref, rounded_ref,
    shift_ref, slip_rest_ref, rest_ref,
):
    @pl.loop(0, slip_ref.shape[0] // BS, unroll=2)
    def _(n):
        at = rows_at(n, BS)
        numbers = numbers_ref[at, :]
        inv_direct, inv_evolution, ratio = (numbers[:, k : k + 1] for k in range(2, 5))
        speed = speed_ref[at, :]
        slip = slip_ref[at, :] + STEP_SIZE * speed
        state = part_ref[at, :] - (STEP_SIZE * ratio) * speed
        tau = near_tau(n, slip, numbers, near_ref, rounded_ref)
        shift_ref[at, :] = tau * scale_ref[at, :] - state * inv_direct
        slip_rest_ref[at, :] = 0.5 * (slip_ref[at, :] + slip)
        friction = jnp.exp((REF_FRICTION - state) * inv_evolution)
        rest_ref[at, :] = 0.5 * (state_ref[at, :] + state) + (0.5 * STEP_SIZE * ratio) * friction


def finish_second_kernel(
    count, shift_ref, scale_ref, rest_ref, slip_rest_ref, numbers_ref, basis_out_ref, near_ref, *refs
):
    parts, pair_ref, cross_ref = refs[:count], refs[count], refs[count + 1]
    slip_hbm, state_hbm, slip_ref, state_ref, sems = refs[count + 2 :]

    def copies(n):
        at = rows_at(n, BS)
        return [
            pltpu.make_async_copy(slip_ref.at[at, :], slip_hbm.at[at, :], sems.at[0, n]),
            pltpu.make_async_copy(state_ref.at[at, :], state_hbm.at[at, :], sems.at[1, n]),
        ]

    def block(n, outer):
        at = rows_at(n, BS)
        speed = jnp.exp(shift_ref[at, :] - scale_ref[at, :] * outer)
        slip_ref[at, :] = slip_rest_ref[at, :] + (0.5 * STEP_SIZE) * speed
        state_ref[at, :] = rest_ref[at, :] - (0.5 * STEP_SIZE * numbers_ref[at, 4:5]) * speed
        for copy in copies(n):
            copy.start()

    over_blocks(block, basis_out_ref, near_ref, parts, pair_ref, cross_ref)

    @pl.loop(0, slip_ref.shape[0] // BS)
    def _(n):
        for copy in copies(n):
            copy.wait()


def masked_coupling(coupling, wide):
    rows, sources, width = coupling.shape
    blocks = rows // R
    keep = jnp.arange(R, dtype=jnp.int32).astype(F32)[None, None, :, None] < wide[:, :, None, :]
    matrix = jnp.transpose(coupling, (1, 0, 2)).reshape(sources, blocks, R, width)
    masked = jnp.where(keep, matrix, jnp.zeros((), BF16)).reshape(sources, rows, width)
    return pltpu.with_memory_space_constraint(masked, pltpu.VMEM)


def per_device(
    slip,
    state,
    tau_load,
    normal_stress,
    direct_effect,
    evolution_effect,
    slip_distance,
    self_stiffness,
    near_blocks,
    basis_in,
    basis_out,
    coupling,
    block_rank,
    adj_bricks,
    adj_count,
    adj_weight,
    pressure_now,
    pressure_rate,
):
    row_count = lax.axis_size("row")
    col_count = lax.axis_size("col")
    row_index = lax.axis_index("row")
    col_index = lax.axis_index("col")
    heights = col_count // 2
    height, core = col_index // 2, col_index % 2
    both = ("row", "col")
    devices = row_count * col_count

    def to_row(array, d):
        return lax.ppermute(array, "row", [(i, (i + d) % row_count) for i in range(row_count)])

    def to_height(array, d):
        pairs = [(2 * z + k, 2 * ((z + d) % heights) + k) for z in range(heights) for k in range(2)]
        return lax.ppermute(array, "col", pairs)

    def to_core(array):
        return lax.ppermute(array, "col", [(2 * z + k, 2 * z + 1 - k) for z in range(heights) for k in range(2)])

    def to_chip(array):
        ends = [(i, i + 1) for i in range(1, devices - 1, 2)]
        return lax.ppermute(array, both, ends + [(j, i) for i, j in ends])

    patches, ens = slip.shape
    slots = adj_bricks.shape[0]
    size = pressure_now.shape[0]
    share = coupling.shape[2]
    def to_partner(array):
        pairs = [(2 * z + k, 2 * (z + 1 - 2 * (z % 2)) + k) for z in range(heights) for k in range(2)]
        return lax.ppermute(array, "col", pairs)

    def first_step(coeffs, pair, cross, later):
        sent = to_core(couple(1, masked, coeffs, heights, BF16, pair))
        kept = couple(0, masked, coeffs, heights, F32)
        own, direct, passed, keep = chip_sum(kept, sent, heights)
        if not later:
            own, cross = lax.optimization_barrier((own, cross))
        return own, to_partner(passed), to_partner(direct), keep, sent, cross if later else to_chip(cross)

    def second_step(own, came, direct, keep, sent, cross, later):
        sums = call(pair_sum_kernel, [jax.ShapeDtypeStruct((share, ens), BF16)] * (heights // 2 - 1), keep, came)
        if later:
            sums, cross = lax.optimization_barrier((sums, cross))
            cross = to_chip(cross)
        return [to_height(part, 2 * (d + 1)) for d, part in enumerate(sums)] + [own, direct, sent, cross]

    def row_coeffs(coeff):
        return [coeff] + [to_row(coeff, d) for d in range(1, row_count)]

    full = jax.ShapeDtypeStruct((patches, ens), F32)
    half = jax.ShapeDtypeStruct((patches, ens), BF16)
    edge = jax.ShapeDtypeStruct((BS, ens), BF16)
    per_patch = [tau_load, normal_stress, direct_effect, evolution_effect, slip_distance, self_stiffness]

    ranks = jnp.transpose(block_rank, (1, 2, 0))
    wide, joined = call(
        functools.partial(ranks_kernel, col_count),
        [
            jax.ShapeDtypeStruct((ranks.shape[0], ranks.shape[2], share), F32),
            jax.ShapeDtypeStruct((size, 2 * ens), BF16),
        ],
        *in_hbm(ranks, pressure_now, pressure_rate),
        specs=[HBM] * 3,
        scratch_shapes=[pltpu.VMEM(ranks.shape, jnp.int32), pltpu.SemaphoreType.DMA((3,))],
    )
    fields = [joined] + [to_height(joined, d) for d in range(1, heights)]
    masked = masked_coupling(coupling, wide)
    masked, slip = lax.optimization_barrier((masked, slip))
    coeff, rounded, pair, cross = project(slip, basis_in)
    coeffs = row_coeffs(coeff)
    brick_lists = [adj_count[None], adj_bricks, adj_weight]
    columns = [array[None] for array in per_patch] + brick_lists
    start = (5 * (patches // BS) // 8) * BS
    part, last_part = (
        jax.ShapeDtypeStruct((2 * heights * size, n), BF16) for n in (start, patches - start)
    )
    scratch = [
        pltpu.VMEM((6, 1, patches), F32),
        pltpu.VMEM((1, patches), jnp.int32),
        pltpu.VMEM(adj_bricks.shape, jnp.int32),
        pltpu.VMEM(adj_weight.shape, F32),
        pltpu.SemaphoreType.DMA((11,)),
    ]
    numbers, low = call(
        functools.partial(weights_kernel, heights, size, 0),
        [jax.ShapeDtypeStruct((start, 8), F32), part],
        *in_hbm(*columns),
        coeff,
        specs=[HBM] * 9 + [VMEM],
        scratch_shapes=scratch,
    )
    fields, coeffs, low = lax.optimization_barrier((fields, coeffs, low))
    own = call(
        side_by_side_kernel, jax.ShapeDtypeStruct((heights * size, 2 * ens), BF16), *fields
    )
    other = to_core(own)
    own_part, came, direct, keep, sent, cross = first_step(coeffs, pair, cross, True)
    numbers, high, near, state = call(
        functools.partial(weights_kernel, heights, size, start),
        [jax.ShapeDtypeStruct((patches, 8), F32), last_part, jax.ShapeDtypeStruct(near_blocks.shape, BF16), full],
        *in_hbm(*columns, near_blocks, state),
        numbers,
        own_part,
        specs=[HBM] * 11 + [VMEM] * 2,
        scratch_shapes=scratch,
    )
    came, high = lax.optimization_barrier((came, high))
    outer = second_step(own_part, came, direct, keep, sent, cross, True)
    shift, scale, rest, scale_mid = call(
        prepare_first_kernel, [full] * 4, low, high, own, other, slip, state, numbers, near, rounded
    )
    speed, rounded, coeff, pair, cross = call(
        functools.partial(finish_first_kernel, len(outer) - 2),
        [full, half, jax.ShapeDtypeStruct((patches // BS * R, ens), BF16), edge, edge],
        shift, scale, slip, basis_out, basis_in, near, *outer,
    )
    coeffs = row_coeffs(coeff)
    outer = second_step(*first_step(coeffs, pair, cross, False), False)
    shift, slip_rest, rest = call(
        prepare_second_kernel, [full] * 3,
        slip, state, speed, rest, scale_mid, numbers, near, rounded,
    )
    slip_out, state_out = call(
        functools.partial(finish_second_kernel, len(outer) - 2),
        [full] * 2,
        shift, scale_mid, rest, slip_rest, numbers, basis_out, near, *outer,
        out_specs=[HBM] * 2,
        scratch_shapes=[
            pltpu.VMEM((patches, ens), F32),
            pltpu.VMEM((patches, ens), F32),
            pltpu.SemaphoreType.DMA((2, patches // BS)),
        ],
    )
    return (slip_out, state_out)


def solution(mesh):
    in_specs = (
        P(("row", "col"), None),
        P(("row", "col"), None),
        P(("row", "col")),
        P(("row", "col")),
        P(("row", "col")),
        P(("row", "col")),
        P(("row", "col")),
        P(("row", "col")),
        P(None, ("row", "col"), None),
        P(None, ("row", "col")),
        P(None, ("row", "col")),
        P("row", None, "col"),
        P("row", None, "col"),
        P(None, ("row", "col")),
        P(("row", "col")),
        P(None, ("row", "col")),
        P("col", None),
        P("col", None),
    )
    out_specs = (P(("row", "col"), None), P(("row", "col"), None))
    return jax.shard_map(
        per_device, mesh=mesh, in_specs=in_specs, out_specs=out_specs, check_vma=False
    )
```

```python
import functools

import jax
import jax.numpy as jnp
from jax import lax
from jax.experimental import pallas as pl
from jax.experimental.pallas import tpu as pltpu
from jax.sharding import PartitionSpec as P

BS = 256
R = 32

STEP_SIZE = 0.5
REF_FRICTION = 0.6
LIMIT = 16 * 1024 * 1024
F32 = jnp.float32
BF16 = jnp.bfloat16


def dot(a, b):
    return jnp.dot(a, b, preferred_element_type=F32)


def dot_t(a, b):
    return lax.dot_general(a, b, (((0,), (0,)), ((), ())), preferred_element_type=F32)


VMEM = pl.BlockSpec(memory_space=pltpu.VMEM)


def call(kernel, outs, *operands, specs=None, **grid):
    return pl.pallas_call(
        kernel,
        in_specs=specs or [VMEM] * len(operands),
        out_shape=outs,
        compiler_params=pltpu.CompilerParams(vmem_limit_bytes=LIMIT),
        **grid,
    )(*operands)


def rows_at(n, size):
    return pl.ds(pl.multiple_of(n * size, size), size)


HBM = pl.BlockSpec(memory_space=pl.ANY)


def in_hbm(*arrays):
    return [pltpu.with_memory_space_constraint(array, pltpu.HBM) for array in arrays]


def start_copies(pairs, sems, first=0):
    copies = [pltpu.make_async_copy(a, b, sems.at[first + k]) for k, (a, b) in enumerate(pairs)]
    for copy in copies:
        copy.start()
    return copies


def fill_edges(first, last, pair_ref, cross_ref):
    even = lax.rem(lax.axis_index("col"), 2) == 0
    pair_ref[...] = jnp.where(even, last, first)
    cross_ref[...] = jnp.where(even, first, last)


def project_kernel(slip_ref, basis_ref, coeff_ref, rounded_ref, pair_ref, cross_ref):
    for n in range(slip_ref.shape[0] // BS):
        at = pl.ds(n * BS, BS)
        rounded = slip_ref[at, :].astype(BF16)
        rounded_ref[at, :] = rounded
        coeff_ref[n * R : (n + 1) * R, :] = dot(basis_ref[:, at], rounded).astype(BF16)
    fill_edges(rounded_ref[:BS], rounded_ref[-BS:], pair_ref, cross_ref)


def project(slip, basis_in):
    patches, ens = slip.shape
    edge = jax.ShapeDtypeStruct((BS, ens), BF16)
    return call(
        project_kernel,
        [
            jax.ShapeDtypeStruct((patches // BS * R, ens), BF16),
            jax.ShapeDtypeStruct((patches, ens), BF16),
            edge,
            edge,
        ],
        slip,
        basis_in,
    )


def ranks_kernel(
    col_count, rank_hbm, now_hbm, rate_hbm, wide_ref, joined_ref, rank_ref, sems
):
    sources, share, blocks = rank_ref.shape
    ens = now_hbm.shape[1]
    copies = start_copies(
        [
            (rank_hbm, rank_ref),
            (now_hbm, joined_ref.at[:, pl.ds(0, ens)]),
            (rate_hbm, joined_ref.at[:, pl.ds(ens, ens)]),
        ],
        sems,
    )
    width = share * R
    column = lax.broadcasted_iota(jnp.int32, (share, width), 1)
    spread = (lax.div(column, R) == lax.broadcasted_iota(jnp.int32, (share, width), 0)).astype(F32).astype(BF16)
    level = lax.rem(lax.broadcasted_iota(jnp.int32, (blocks, width), 1), R).astype(F32)
    receiver = lax.axis_index("row") * blocks + lax.broadcasted_iota(jnp.int32, (share, blocks), 1)
    copies[0].wait()
    for source in range(sources):
        own = (source * col_count + lax.axis_index("col")) * share + lax.broadcasted_iota(jnp.int32, (share, blocks), 0)
        rank = jnp.where(jnp.abs(receiver - own) > 1, rank_ref[source], 0).astype(F32)
        wide = dot_t(rank.astype(BF16), spread)
        wide_ref[source] = jnp.where(level < wide, wide, 0.0)
    copies[1].wait()
    copies[2].wait()


def side_by_side_kernel(*refs):
    pieces, out_ref = refs[:-1], refs[-1]
    size = pieces[0].shape[0]
    for k, piece in enumerate(pieces):
        out_ref[k * size : (k + 1) * size, :] = piece[...]


def weights_kernel(heights, size, start, *refs):
    begun = start > 0
    sources, rest = refs[:9], refs[9:]
    near_hbm, state_hbm, begun_ref = rest[:3] if begun else (None, None, None)
    rest = rest[4:] if begun else rest[1:]
    numbers_ref, matrix_ref = rest[:2]
    near_ref, state_ref = rest[2:4] if begun else (None, None)
    vectors, lists, sems = rest[-5], rest[-4:-1], rest[-1]
    targets = [vectors.at[k] for k in range(6)] + list(lists)
    copies = start_copies(list(zip(sources, targets)), sems)
    large = [(near_hbm, near_ref), (state_hbm, state_ref)] if begun else []
    large = start_copies(large, sems, len(targets))
    if begun:
        numbers_ref[:start, :] = begun_ref[...]
    count_ref, bricks_ref, weight_ref = lists
    slots = bricks_ref.shape[0]
    col = lax.axis_index("col")
    height, core = lax.div(col, 2).astype(F32), lax.rem(col, 2).astype(F32)
    group, lanes, unrolled = 16, 128, 16
    for copy in copies:
        copy.wait()

    @pl.loop(0, matrix_ref.shape[1] // lanes)
    def _(n):
        own_at = rows_at(n, lanes)
        at = pl.ds(pl.multiple_of(start + n * lanes, lanes), lanes)
        load, normal, direct, evolution, distance, stiffness = (vectors[k, :, at] for k in range(6))
        rows = [load, normal, 1.0 / direct, 1.0 / evolution, evolution / distance, stiffness, load, normal]
        numbers_ref[at if begun else own_at, :] = jnp.concatenate(rows, axis=0).T
        bricks = bricks_ref[:, at].astype(F32)
        live = lax.broadcasted_iota(jnp.int32, (slots, lanes), 0) < count_ref[:, at]
        weights = jnp.where(live, weight_ref[:, at], 0.0)
        merged = jnp.zeros((slots, lanes), F32)
        for k in range(slots):
            merged = merged + jnp.where(bricks == bricks[k : k + 1], weights[k : k + 1], 0.0)
        shares = merged / jnp.sum(weights, axis=0, keepdims=True)
        owner = jnp.floor((bricks + 0.5) * (1.0 / size))
        chip = jnp.floor(owner * 0.5 + 0.25)
        away = height - chip
        away = jnp.where(away < 0, away + heights, away)
        other = jnp.where(owner - 2.0 * chip == core, 0.0, float(heights))
        place = jnp.where(live, (other + away - owner) * size + bricks, -1.0)
        high = jnp.floor((place + 0.5) * (1.0 / group))
        low = place - high * group
        spread = lambda rows, k: jnp.broadcast_to(rows[k : k + 1], (group, lanes)).astype(BF16)
        line = lax.broadcasted_iota(jnp.int32, (group, lanes), 0).astype(F32).astype(BF16)
        none = jnp.full((group, lanes), -1.0, BF16)
        highs = [jnp.where(spread(low, k) == line, spread(high, k), none) for k in range(slots)]
        values = [spread(shares, k) for k in range(slots)]

        @pl.loop(0, matrix_ref.shape[0] // (group * unrolled))
        def _(m):
            first = jnp.full((group, lanes), (m * unrolled).astype(F32)).astype(BF16)
            for step in range(unrolled):
                here = first + jnp.asarray(step, BF16)
                tile = jnp.zeros((group, lanes), BF16)
                for k in range(slots):
                    tile = jnp.where(highs[k] == here, values[k], tile)
                to = pl.ds(pl.multiple_of((m * unrolled + step) * group, group), group)
                matrix_ref[to, own_at] = tile

    for copy in large:
        copy.wait()


def couple_kernel(sources, heights, flip, matrix_ref, *refs):
    coeffs, edges, out_ref = refs[:sources], refs[sources:-1], refs[-1]
    share = coeffs[0].shape[0]
    row, col = lax.axis_index("row"), lax.axis_index("col")
    height, core = lax.div(col, 2), lax.rem(col + flip, 2)

    @pl.loop(0, heights, unroll=True)
    def _(d):
        partner = lax.rem(d, 2) * (1 - 2 * lax.rem(height, 2))
        at = rows_at(2 * lax.rem(height + partner + d - lax.rem(d, 2) + heights, heights) + core, share)
        total = None
        for step in range(sources):
            term = dot(matrix_ref[lax.rem(row + (sources - step), sources), at, :], coeffs[step][...])
            total = term if total is None else total + term
        out_ref[rows_at(d, share), :] = total.astype(out_ref.dtype)

    for edge in edges:
        out_ref[heights * share :, :] = edge[...]


def couple(flip, matrix, coeffs, heights, kind, *edges):
    share, ens = coeffs[0].shape
    return call(
        functools.partial(couple_kernel, len(coeffs), heights, flip),
        jax.ShapeDtypeStruct((heights * share + len(edges) * BS, ens), kind),
        matrix,
        *coeffs,
        *edges,
    )


def chip_sum_kernel(kept_ref, sent_ref, own_ref, direct_ref, pass_ref, keep_ref):
    share = own_ref.shape[0]
    group = 32
    for place in range(2 + 2 * (keep_ref.shape[0] // share)):
        far = place // 2 - 1
        out_ref = (own_ref, direct_ref)[place % 2] if far < 0 else (keep_ref, pass_ref)[place % 2]

        @pl.loop(0, share // group)
        def _(n):
            at = pl.ds(pl.multiple_of(place * share + n * group, group), group)
            to = pl.ds(pl.multiple_of(max(far, 0) * share + n * group, group), group)
            out_ref[to, :] = (kept_ref[at, :] + sent_ref[at, :].astype(F32)).astype(out_ref.dtype)


def chip_sum(kept, sent, heights):
    rows, ens = kept.shape
    share = rows // heights
    far = (heights // 2 - 1) * share
    shapes = [(share, BF16), (share, BF16), (far, BF16), (far, F32)]
    return call(chip_sum_kernel, [jax.ShapeDtypeStruct((n, ens), kind) for n, kind in shapes], kept, sent)


def pair_sum_kernel(keep_ref, came_ref, *outs):
    share = outs[0].shape[0]
    group = 32
    for far, out_ref in enumerate(outs):

        @pl.loop(0, share // group)
        def _(n):
            at = pl.ds(pl.multiple_of(far * share + n * group, group), group)
            out_ref[rows_at(n, group), :] = (keep_ref[at, :] + came_ref[at, :].astype(F32)).astype(BF16)


def near_tau(n, slip, numbers, near_ref, rounded_ref):
    count = rounded_ref.shape[0] // BS
    at = rows_at(n, BS)
    none = jnp.zeros((BS, rounded_ref.shape[1]), BF16)
    before = jnp.where(n == 0, none, rounded_ref[rows_at(jnp.maximum(n - 1, 0), BS), :])
    after = jnp.where(n == count - 1, none, rounded_ref[rows_at(jnp.minimum(n + 1, count - 1), BS), :])
    near = dot(near_ref[0, at, :], before) + dot(near_ref[1, at, :], rounded_ref[at, :]) + dot(near_ref[2, at, :], after)
    return numbers[:, 0:1] - numbers[:, 5:6] * slip - near


def prepare_first_kernel(
    low_ref, high_ref, own_ref, other_ref, slip_ref, state_ref, numbers_ref, near_ref, rounded_ref,
    shift_ref, scale_ref, rest_ref, scale_mid_ref,
):
    half = own_ref.shape[0]
    ens = slip_ref.shape[1]
    blocks = low_ref.shape[1] // BS

    def block(matrix_ref, m, n):
        at, own_at = rows_at(n, BS), rows_at(m, BS)
        total = dot_t(matrix_ref[:half, own_at], own_ref[...]) + dot_t(matrix_ref[half:, own_at], other_ref[...])
        numbers = numbers_ref[at, :]
        normal, inv_direct, inv_evolution, ratio = (numbers[:, k : k + 1] for k in range(1, 5))
        base = total[:, :ens]
        scale = inv_direct / (normal - base)
        scale_ref[at, :] = scale
        scale_mid_ref[at, :] = inv_direct / (normal - (base + STEP_SIZE * total[:, ens:]))
        state = state_ref[at, :]
        tau = near_tau(n, slip_ref[at, :], numbers, near_ref, rounded_ref)
        shift_ref[at, :] = tau * scale - state * inv_direct
        rest_ref[at, :] = state + (STEP_SIZE * ratio) * jnp.exp((REF_FRICTION - state) * inv_evolution)

    @pl.loop(0, blocks, unroll=2)
    def _(m):
        block(low_ref, m, m)

    @pl.loop(0, blocks, unroll=2)
    def _(m):
        block(high_ref, m, blocks + m)


def over_blocks(block, basis_ref, near_ref, parts, pair_ref, cross_ref):
    count = near_ref.shape[1] // BS

    def far(n):
        levels = rows_at(n, R)
        total = parts[0][levels, :].astype(F32)
        for part in parts[1:]:
            total = total + part[levels, :].astype(F32)
        return dot_t(basis_ref[:, rows_at(n, BS)], total.astype(BF16))

    even = lax.rem(lax.axis_index("col"), 2) == 0
    pair, cross = pair_ref[-BS:], cross_ref[...]
    block(0, far(0) + dot(near_ref[0, :BS, :], jnp.where(even, cross, pair)))

    @pl.loop(1, count - 1, unroll=True)
    def _(n):
        block(n, far(n))

    block(count - 1, far(count - 1) + dot(near_ref[2, -BS:, :], jnp.where(even, pair, cross)))


def finish_first_kernel(
    count, shift_ref, scale_ref, slip_ref, basis_out_ref, basis_in_ref, near_ref, *refs
):
    parts, pair_ref, cross_ref = refs[:count], refs[count], refs[count + 1]
    speed_ref, rounded_ref, coeff_ref, pair_out, cross_out = refs[count + 2 :]

    def block(n, outer):
        at = rows_at(n, BS)
        speed = jnp.exp(shift_ref[at, :] - scale_ref[at, :] * outer)
        speed_ref[at, :] = speed
        rounded = (slip_ref[at, :] + STEP_SIZE * speed).astype(BF16)
        rounded_ref[at, :] = rounded
        coeff_ref[rows_at(n, R), :] = dot(basis_in_ref[:, at], rounded).astype(BF16)

    over_blocks(block, basis_out_ref, near_ref, parts, pair_ref, cross_ref)
    fill_edges(rounded_ref[:BS], rounded_ref[-BS:], pair_out, cross_out)


def prepare_second_kernel(
    slip_ref, state_ref, speed_ref, part_ref, scale_ref, numbers_ref, near_ref, rounded_ref,
    shift_ref, slip_rest_ref, rest_ref,
):
    @pl.loop(0, slip_ref.shape[0] // BS, unroll=2)
    def _(n):
        at = rows_at(n, BS)
        numbers = numbers_ref[at, :]
        inv_direct, inv_evolution, ratio = (numbers[:, k : k + 1] for k in range(2, 5))
        speed = speed_ref[at, :]
        slip = slip_ref[at, :] + STEP_SIZE * speed
        state = part_ref[at, :] - (STEP_SIZE * ratio) * speed
        tau = near_tau(n, slip, numbers, near_ref, rounded_ref)
        shift_ref[at, :] = tau * scale_ref[at, :] - state * inv_direct
        slip_rest_ref[at, :] = 0.5 * (slip_ref[at, :] + slip)
        friction = jnp.exp((REF_FRICTION - state) * inv_evolution)
        rest_ref[at, :] = 0.5 * (state_ref[at, :] + state) + (0.5 * STEP_SIZE * ratio) * friction


def finish_second_kernel(
    count, shift_ref, scale_ref, rest_ref, slip_rest_ref, numbers_ref, basis_out_ref, near_ref, *refs
):
    parts, pair_ref, cross_ref = refs[:count], refs[count], refs[count + 1]
    slip_hbm, state_hbm, slip_ref, state_ref, sems = refs[count + 2 :]

    def copies(n):
        at = rows_at(n, BS)
        return [
            pltpu.make_async_copy(slip_ref.at[at, :], slip_hbm.at[at, :], sems.at[0, n]),
            pltpu.make_async_copy(state_ref.at[at, :], state_hbm.at[at, :], sems.at[1, n]),
        ]

    def block(n, outer):
        at = rows_at(n, BS)
        speed = jnp.exp(shift_ref[at, :] - scale_ref[at, :] * outer)
        slip_ref[at, :] = slip_rest_ref[at, :] + (0.5 * STEP_SIZE) * speed
        state_ref[at, :] = rest_ref[at, :] - (0.5 * STEP_SIZE * numbers_ref[at, 4:5]) * speed
        for copy in copies(n):
            copy.start()

    over_blocks(block, basis_out_ref, near_ref, parts, pair_ref, cross_ref)

    @pl.loop(0, slip_ref.shape[0] // BS)
    def _(n):
        for copy in copies(n):
            copy.wait()


def masked_coupling(coupling, wide):
    rows, sources, width = coupling.shape
    blocks = rows // R
    keep = jnp.arange(R, dtype=jnp.int32).astype(F32)[None, None, :, None] < wide[:, :, None, :]
    matrix = jnp.transpose(coupling, (1, 0, 2)).reshape(sources, blocks, R, width)
    masked = jnp.where(keep, matrix, jnp.zeros((), BF16)).reshape(sources, rows, width)
    return pltpu.with_memory_space_constraint(masked, pltpu.VMEM)


def per_device(
    slip,
    state,
    tau_load,
    normal_stress,
    direct_effect,
    evolution_effect,
    slip_distance,
    self_stiffness,
    near_blocks,
    basis_in,
    basis_out,
    coupling,
    block_rank,
    adj_bricks,
    adj_count,
    adj_weight,
    pressure_now,
    pressure_rate,
):
    row_count = lax.axis_size("row")
    col_count = lax.axis_size("col")
    row_index = lax.axis_index("row")
    col_index = lax.axis_index("col")
    heights = col_count // 2
    height, core = col_index // 2, col_index % 2
    both = ("row", "col")
    devices = row_count * col_count

    def to_row(array, d):
        return lax.ppermute(array, "row", [(i, (i + d) % row_count) for i in range(row_count)])

    def to_height(array, d):
        pairs = [(2 * z + k, 2 * ((z + d) % heights) + k) for z in range(heights) for k in range(2)]
        return lax.ppermute(array, "col", pairs)

    def to_core(array):
        return lax.ppermute(array, "col", [(2 * z + k, 2 * z + 1 - k) for z in range(heights) for k in range(2)])

    def to_chip(array):
        ends = [(i, i + 1) for i in range(1, devices - 1, 2)]
        return lax.ppermute(array, both, ends + [(j, i) for i, j in ends])

    patches, ens = slip.shape
    slots = adj_bricks.shape[0]
    size = pressure_now.shape[0]
    share = coupling.shape[2]
    def to_partner(array):
        pairs = [(2 * z + k, 2 * (z + 1 - 2 * (z % 2)) + k) for z in range(heights) for k in range(2)]
        return lax.ppermute(array, "col", pairs)

    def first_step(coeffs, pair, cross, later):
        sent = to_core(couple(1, masked, coeffs, heights, BF16, pair))
        kept = couple(0, masked, coeffs, heights, F32)
        own, direct, passed, keep = chip_sum(kept, sent, heights)
        if not later:
            own, cross = lax.optimization_barrier((own, cross))
        return own, to_partner(passed), to_partner(direct), keep, sent, cross if later else to_chip(cross)

    def second_step(own, came, direct, keep, sent, cross, later):
        sums = call(pair_sum_kernel, [jax.ShapeDtypeStruct((share, ens), BF16)] * (heights // 2 - 1), keep, came)
        if later:
            sums, cross = lax.optimization_barrier((sums, cross))
            cross = to_chip(cross)
        return [to_height(part, 2 * (d + 1)) for d, part in enumerate(sums)] + [own, direct, sent, cross]

    def row_coeffs(coeff):
        return [coeff] + [to_row(coeff, d) for d in range(1, row_count)]

    full = jax.ShapeDtypeStruct((patches, ens), F32)
    half = jax.ShapeDtypeStruct((patches, ens), BF16)
    edge = jax.ShapeDtypeStruct((BS, ens), BF16)
    per_patch = [tau_load, normal_stress, direct_effect, evolution_effect, slip_distance, self_stiffness]

    ranks = jnp.transpose(block_rank, (1, 2, 0))
    wide, joined = call(
        functools.partial(ranks_kernel, col_count),
        [
            jax.ShapeDtypeStruct((ranks.shape[0], ranks.shape[2], share), F32),
            jax.ShapeDtypeStruct((size, 2 * ens), BF16),
        ],
        *in_hbm(ranks, pressure_now, pressure_rate),
        specs=[HBM] * 3,
        scratch_shapes=[pltpu.VMEM(ranks.shape, jnp.int32), pltpu.SemaphoreType.DMA((3,))],
    )
    fields = [joined] + [to_height(joined, d) for d in range(1, heights)]
    masked = masked_coupling(coupling, wide)
    masked, slip = lax.optimization_barrier((masked, slip))
    coeff, rounded, pair, cross = project(slip, basis_in)
    coeffs = row_coeffs(coeff)
    brick_lists = [adj_count[None], adj_bricks, adj_weight]
    columns = [array[None] for array in per_patch] + brick_lists
    start = patches // 2
    part = jax.ShapeDtypeStruct((2 * heights * size, start), BF16)
    scratch = [
        pltpu.VMEM((6, 1, patches), F32),
        pltpu.VMEM((1, patches), jnp.int32),
        pltpu.VMEM(adj_bricks.shape, jnp.int32),
        pltpu.VMEM(adj_weight.shape, F32),
        pltpu.SemaphoreType.DMA((11,)),
    ]
    numbers, low = call(
        functools.partial(weights_kernel, heights, size, 0),
        [jax.ShapeDtypeStruct((start, 8), F32), part],
        *in_hbm(*columns),
        coeff,
        specs=[HBM] * 9 + [VMEM],
        scratch_shapes=scratch,
    )
    fields, coeffs, low = lax.optimization_barrier((fields, coeffs, low))
    own = call(
        side_by_side_kernel, jax.ShapeDtypeStruct((heights * size, 2 * ens), BF16), *fields
    )
    other = to_core(own)
    own_part, came, direct, keep, sent, cross = first_step(coeffs, pair, cross, True)
    numbers, high, near, state = call(
        functools.partial(weights_kernel, heights, size, start),
        [jax.ShapeDtypeStruct((patches, 8), F32), part, jax.ShapeDtypeStruct(near_blocks.shape, BF16), full],
        *in_hbm(*columns, near_blocks, state),
        numbers,
        own_part,
        specs=[HBM] * 11 + [VMEM] * 2,
        scratch_shapes=scratch,
    )
    came, high = lax.optimization_barrier((came, high))
    outer = second_step(own_part, came, direct, keep, sent, cross, True)
    shift, scale, rest, scale_mid = call(
        prepare_first_kernel, [full] * 4, low, high, own, other, slip, state, numbers, near, rounded
    )
    speed, rounded, coeff, pair, cross = call(
        functools.partial(finish_first_kernel, len(outer) - 2),
        [full, half, jax.ShapeDtypeStruct((patches // BS * R, ens), BF16), edge, edge],
        shift, scale, slip, basis_out, basis_in, near, *outer,
    )
    coeffs = row_coeffs(coeff)
    outer = second_step(*first_step(coeffs, pair, cross, False), False)
    shift, slip_rest, rest = call(
        prepare_second_kernel, [full] * 3,
        slip, state, speed, rest, scale_mid, numbers, near, rounded,
    )
    slip_out, state_out = call(
        functools.partial(finish_second_kernel, len(outer) - 2),
        [full] * 2,
        shift, scale_mid, rest, slip_rest, numbers, basis_out, near, *outer,
        out_specs=[HBM] * 2,
        scratch_shapes=[
            pltpu.VMEM((patches, ens), F32),
            pltpu.VMEM((patches, ens), F32),
            pltpu.SemaphoreType.DMA((2, patches // BS)),
        ],
    )
    return (slip_out, state_out)


def solution(mesh):
    in_specs = (
        P(("row", "col"), None),
        P(("row", "col"), None),
        P(("row", "col")),
        P(("row", "col")),
        P(("row", "col")),
        P(("row", "col")),
        P(("row", "col")),
        P(("row", "col")),
        P(None, ("row", "col"), None),
        P(None, ("row", "col")),
        P(None, ("row", "col")),
        P("row", None, "col"),
        P("row", None, "col"),
        P(None, ("row", "col")),
        P(("row", "col")),
        P(None, ("row", "col")),
        P("col", None),
        P("col", None),
    )
    out_specs = (P(("row", "col"), None), P(("row", "col"), None))
    return jax.shard_map(
        per_device, mesh=mesh, in_specs=in_specs, out_specs=out_specs, check_vma=False
    )
```
